32 devices in a mesh: row: 8 (over z, core), col: 4 (over y, x).
Axes of the slice: x: 2, y: 2, z: 4, core: 2. Of those that a mesh axis runs over, the one named last changes fastest.
Arguments:
- r_vals: bfloat16 [16384, 2048], P('row', 'col'), may hold values from -6 to 6
- s_vals: bfloat16 [2048, 1024], P('row', 'col'), may hold values from -0.125 to 0.125
- t_vals: bfloat16 [1024, 16384], P(None, ('row', 'col')), may hold values from -6 to 6
- r_pattern: int32 [128, 16], replicated, may hold values 0 or 1
- s_pattern: int32 [16, 8], replicated, may hold values 0 or 1
- t_pattern: int32 [8, 128], replicated, may hold values 0 or 1
Outputs:
- joined: bfloat16 [16384, 1024], P('row', 'col')
The draws below stay inside these ranges and needn't reach their ends.
All inputs are finite; a program needn't handle non-finite values.
Results may differ from the reference program's by a relative error of at most 0.001.
Values may be sent and summed in bfloat16 or wider, within the bound.
No kernel may reach another device: no remote copies, remote signals or barrier semaphores. Data moves between devices by JAX's collectives and lax.ppermute only.
A program may use at most 64 MiB of HBM per device.

```python
import jax
import jax.numpy as jnp
from jax import lax

BLK = 128
TI = 16
KT = 16
NA = 16384
NB = 2048
NC = 1024
TA = 128
TC = 8
N_ROW = 8


def touch_ends(entries, key, smallest, top_value):
    longest = entries.shape.index(max(entries.shape))
    spots = []
    for shift in (0, 1):
        where = [jax.random.randint(jax.random.fold_in(key, axis), (), 0, length) for axis, length in enumerate(entries.shape)]
        where[longest] = (where[longest] + shift) % entries.shape[longest]
        spots.append(tuple(where))
    return entries.at[spots[0]].set(smallest).at[spots[1]].set(top_value)


def block_levels(key, dims, cuts, least, high):
    def one(axis_at, blocks):
        draws = jax.random.uniform(jax.random.fold_in(jax.random.fold_in(key, 6), axis_at), (blocks,), jnp.float32, least / len(cuts), high / len(cuts))
        return jnp.repeat(jnp.exp(draws), dims[axis_at] // blocks).reshape((-1,) + (1,) * (len(dims) - axis_at - 1))

    gain = one(*cuts[0])
    for cut in cuts[1:]:
        gain = gain * one(*cut)
    return gain


def normal_values(key, extent, scale, bound, split=(), dtype=jnp.bfloat16):
    result = scale * jax.random.normal(key, extent, jnp.float32)
    if split:
        result = result * block_levels(key, extent, split, -0.22, 0.18)
    return jnp.clip(result, -bound, bound).astype(dtype)


def setup_inputs(seed: int = 0) -> dict:
    key_of = jax.random.split(jax.random.key(seed), 7)
    return {
        "r_vals": normal_values(key_of[0], (NA, NB), 1.0, 6.0, ((0, 8), (1, 4))),
        "s_vals": normal_values(key_of[1], (NB, NC), NB ** -0.5, 0.125, ((0, 8), (1, 4))),
        "t_vals": normal_values(key_of[2], (NC, NA), 1.0, 6.0, ((1, 32),)),
        "r_pattern": touch_ends((jax.random.randint(key_of[3], (TA, KT), 0, 3) < 2).astype(jnp.int32), jax.random.fold_in(key_of[3], 1), 0, 1),
        "s_pattern": touch_ends((jax.random.randint(key_of[4], (KT, TC), 0, 3) < 2).astype(jnp.int32), jax.random.fold_in(key_of[4], 1), 0, 1),
        "t_pattern": touch_ends((jax.random.randint(key_of[5], (TC, TA), 0, 3) < 2).astype(jnp.int32), jax.random.fold_in(key_of[5], 1), 0, 1),
    }


def tile_apply(values, pattern):
    tile_rows, tile_cols = pattern.shape
    blocks = values.astype(jnp.float32).reshape(tile_rows, BLK, tile_cols, BLK)
    blocks = blocks * pattern.astype(jnp.float32)[:, None, :, None]
    return blocks.reshape(values.shape).astype(jnp.bfloat16)


def reference(r_vals, s_vals, t_vals, r_pattern, s_pattern, t_pattern):
    r_eff = tile_apply(r_vals, r_pattern)
    s_eff = tile_apply(s_vals, s_pattern)
    t_eff = tile_apply(t_vals, t_pattern)
    row_blocks = r_eff.reshape(N_ROW, TI * BLK, NB)
    t_blocks = jnp.transpose(t_eff.reshape(NC, N_ROW, TI * BLK), (1, 2, 0))

    def one_block(pair):
        left, mirror = pair
        paths = jnp.dot(left, s_eff, preferred_element_type=jnp.float32)
        return (paths * mirror.astype(jnp.float32)).astype(jnp.bfloat16)

    joined = lax.map(one_block, (row_blocks, t_blocks))
    return joined.reshape(NA, NC)
```

```python
import functools
import math

import jax
import jax.numpy as jnp
from jax import lax
from jax.experimental import pallas as pl
from jax.experimental.pallas import tpu as pltpu
from jax.sharding import PartitionSpec as P

BLK = 128
STRIP = 16
LEVELS = 32767.0
FINE = 64.0
VMEM = 24 * 1024 * 1024


def masked(values, flag):
    return values * jnp.full((1, BLK), flag, jnp.float32).astype(jnp.bfloat16)


def masked_rows(r_ref, flags, tile_row, tile_col):
    rows, cols = r_ref.shape
    bands = []
    for t in range(rows // BLK):
        tiles = [
            masked(
                r_ref[t * BLK : (t + 1) * BLK, u * BLK : (u + 1) * BLK],
                flags[tile_row + t, tile_col + u].astype(jnp.float32),
            )
            for u in range(cols // BLK)
        ]
        bands.append(jnp.concatenate(tiles, axis=1) if len(tiles) > 1 else tiles[0])
    return jnp.concatenate(bands, axis=0) if len(bands) > 1 else bands[0]


def product(pieces, places, flags, r_refs, s_refs):
    total = None
    for e in range(pieces):
        rows, cols = r_refs[e].shape
        first = pl.program_id(0) * (rows // BLK)
        left = masked_rows(r_refs[e], flags, first, places[pieces + e] * (cols // BLK))
        term = jnp.dot(left, s_refs[e][0], preferred_element_type=jnp.float32)
        total = term if total is None else total + term
    return total


def own_kernel(pieces, places, flags, *refs):
    out = refs[-1]
    out[...] = product(pieces, places, flags, refs[:pieces], refs[pieces:-1])


def coded_kernel(pieces, places, flags, *refs):
    out = refs[-1]
    total = product(pieces, places, flags, refs[:pieces], refs[pieces:-1])
    rows, cols = total.shape
    group = rows // STRIP
    strip_row = lax.broadcasted_iota(jnp.int32, (STRIP, cols), 0)
    strip = jnp.zeros((STRIP, cols), jnp.float32)
    for g in range(STRIP):
        part = total[g * group : (g + 1) * group]
        top = jnp.max(jnp.max(jnp.abs(part), axis=0, keepdims=True), axis=1, keepdims=True)
        level = jnp.ceil(jnp.log2(jnp.maximum(top, 1e-30)) * FINE) + 1.0
        gain = jnp.exp2(level * (-1.0 / FINE)) * LEVELS
        code = jnp.clip(jnp.round(part * gain), -LEVELS, LEVELS)
        out[g * group : (g + 1) * group] = code.astype(jnp.int16)
        strip = jnp.where(strip_row == g, level, strip)
    out[rows:] = strip.astype(jnp.int16)


def join_kernel(parts, places, own, *refs):
    out, mirror = refs[-1], refs[-2]
    rows = own.shape[0]
    group = rows // STRIP
    for g in range(STRIP):
        at = slice(g * group, (g + 1) * group)
        total = own[at]
        for coded in refs[:parts]:
            level = coded[rows:].astype(jnp.float32)[g : g + 1]
            total += coded[at].astype(jnp.float32) * (
                jnp.exp2(level * (1.0 / FINE)) * (1.0 / LEVELS)
            )
        out[at] = (total * mirror[at].astype(jnp.float32)).astype(jnp.bfloat16)


def turn_kernel(pieces, width, places, flags, t_ref, *outs):
    a_width = t_ref.shape[1]
    for e in range(pieces):
        to = places[e]
        for t in range(width // BLK):
            start = pl.multiple_of(to * width + t * BLK, BLK)
            for u in range(a_width // BLK):
                tile = masked(
                    t_ref[pl.ds(start, BLK), u * BLK : (u + 1) * BLK],
                    flags[to * (width // BLK) + t, u].astype(jnp.float32),
                )
                outs[e][u * BLK : (u + 1) * BLK, t * BLK : (t + 1) * BLK] = tile.T


def params(**kwargs):
    return pltpu.CompilerParams(vmem_limit_bytes=VMEM, **kwargs)


def part_product(kernel, places, flags, r_pieces, s_stack, block, out_rows, dtype):
    pieces = len(r_pieces)
    a_rows, width = r_pieces[0].shape
    cols = s_stack.shape[2]
    steps = a_rows // block
    return pl.pallas_call(
        functools.partial(kernel, pieces),
        out_shape=jax.ShapeDtypeStruct((steps * out_rows, cols), dtype),
        grid_spec=pltpu.PrefetchScalarGridSpec(
            num_scalar_prefetch=2,
            grid=(steps,),
            in_specs=[pl.BlockSpec((block, width), lambda i, p, f: (i, 0)) for _ in range(pieces)]
            + [
                pl.BlockSpec((1, width, cols), functools.partial(lambda e, i, p, f: (p[e], 0, 0), e))
                for e in range(pieces)
            ],
            out_specs=pl.BlockSpec((out_rows, cols), lambda i, p, f: (i, 0)),
        ),
        compiler_params=params(),
        cost_estimate=pl.CostEstimate(
            flops=2 * a_rows * pieces * width * cols,
            bytes_accessed=2 * pieces * width * (a_rows + cols) + 4 * a_rows * cols,
            transcendentals=0,
        ),
    )(places, flags, *r_pieces, *([s_stack] * pieces))


def body(n_row, n_col, r_vals, s_vals, t_vals, r_pattern, s_pattern, t_pattern):
    side = math.isqrt(n_col)
    row = lax.axis_index("row")
    col = lax.axis_index("col")
    line, kind = row // 2, row % 2
    y, x = col // side, col % side
    a_rows, b_width = r_vals.shape
    b_rows, c_width = s_vals.shape
    a_part = t_vals.shape[1]
    a_tiles, ap_tiles = a_rows // BLK, a_part // BLK
    along = kind == 0
    gather_at = jnp.where(along, x, y)
    target_at = jnp.where(along, y, x)
    axes = ("row", "col")

    def place(k, h, yy, xx):
        return (k * 2 + h) * n_col + yy * side + xx

    def shifted(e, gather):
        pairs = []
        for k in range(n_row // 2):
            for h in range(2):
                for yy in range(side):
                    for xx in range(side):
                        if (h == 0) == gather:
                            to = (yy, (xx + e) % side)
                        else:
                            to = ((yy + e) % side, xx)
                        pairs.append((place(k, h, yy, xx), place(k, h, *to)))
        return pairs

    r_pieces = [r_vals] + [lax.ppermute(r_vals, axes, shifted(e, True)) for e in range(1, side)]

    s_tile_rows = max(1, b_rows // BLK)
    s_flags = lax.dynamic_slice(
        s_pattern, (row * b_rows // BLK, col * (c_width // BLK)), (s_tile_rows, c_width // BLK)
    ).astype(jnp.bfloat16)
    s_mask = jnp.repeat(jnp.repeat(s_flags, b_rows // s_tile_rows, axis=0), BLK, axis=1)
    s_eff = s_vals * s_mask
    same, other = [], []
    for a in range(side):
        for b in range(side):
            for c in range(side):
                for d in range(side):
                    k = a * side + b
                    to_even = (c * side + b, 0, a, d)
                    to_odd = (a * side + d, 1, c, b)
                    same.append((place(k, 0, c, d), place(*to_even)))
                    same.append((place(k, 1, c, d), place(*to_odd)))
                    other.append((place(k, 1, c, d), place(*to_even)))
                    other.append((place(k, 0, c, d), place(*to_odd)))
    s_same = lax.ppermute(s_eff, axes, same)
    s_other = lax.ppermute(s_eff, axes, other)
    s_held = jnp.concatenate(
        [jnp.where(along, s_same, s_other), jnp.where(along, s_other, s_same)], axis=0
    )
    s_pieces = [s_held]
    for d in range(1, n_col):
        pairs = [
            ((k * 2 + h), (((k + d) % n_col) * 2 + h)) for k in range(n_col) for h in range(2)
        ]
        s_pieces.append(lax.ppermute(s_held, "row", pairs))
    s_stack = jnp.stack(s_pieces)

    flat = n_col & (n_col - 1) == 0
    partner = [(col ^ e) if flat else (col + e) % n_col for e in range(n_col)]
    origin = [(col ^ e) if flat else (col - e) % n_col for e in range(n_col)]
    t_flags = lax.dynamic_slice_in_dim(t_pattern, (row * n_col + col) * ap_tiles, ap_tiles, 1)
    turned = pl.pallas_call(
        functools.partial(turn_kernel, n_col, c_width),
        out_shape=[jax.ShapeDtypeStruct((a_part, c_width), jnp.bfloat16)] * n_col,
        grid_spec=pltpu.PrefetchScalarGridSpec(
            num_scalar_prefetch=2,
            grid=(1,),
            in_specs=[pl.BlockSpec(t_vals.shape, lambda i, p, f: (0, 0))],
            out_specs=[pl.BlockSpec((a_part, c_width), lambda i, p, f: (0, 0))] * n_col,
        ),
        compiler_params=params(),
        cost_estimate=pl.CostEstimate(
            flops=0, bytes_accessed=4 * a_part * c_width * n_col, transcendentals=0
        ),
    )(jnp.stack(partner).astype(jnp.int32), t_flags, t_vals)
    held = lax.optimization_barrier(tuple(r_pieces[1:]) + tuple(turned))
    r_pieces = r_pieces[:1] + list(held[: side - 1])
    turned = held[side - 1 :]
    mirrors = [turned[0]]
    for e in range(1, n_col):
        pairs = [(j, (j ^ e) if flat else (j + e) % n_col) for j in range(n_col)]
        mirrors.append(lax.ppermute(turned[e], "col", pairs))
    mirror = jnp.concatenate(mirrors, axis=0)

    flags = lax.dynamic_slice_in_dim(r_pattern, row * a_tiles, a_tiles, 0)

    def places(target):
        spots, blocks = [], []
        for e in range(side):
            g = (gather_at - e) % side
            k = jnp.where(along, target * side + g, g * side + target)
            spots.append((line - k) % n_col)
            blocks.append(jnp.where(along, y * side + g, g * side + x))
        return jnp.stack(spots + blocks).astype(jnp.int32)

    block = a_part
    coded = []
    for e in range(1, side):
        codes = part_product(
            coded_kernel, places((target_at + e) % side), flags, r_pieces, s_stack,
            block, block + STRIP, jnp.int16,
        )
        coded.append(lax.ppermute(codes, axes, shifted(e, False)))
    own = part_product(
        own_kernel, places(target_at), flags, r_pieces, s_stack, block, block, jnp.float32
    )

    at = lambda i, p: (p[i], 0)
    return pl.pallas_call(
        functools.partial(join_kernel, side - 1),
        out_shape=jax.ShapeDtypeStruct((a_rows, c_width), jnp.bfloat16),
        grid_spec=pltpu.PrefetchScalarGridSpec(
            num_scalar_prefetch=1,
            grid=(n_col,),
            in_specs=[pl.BlockSpec((block, c_width), at)]
            + [pl.BlockSpec((block + STRIP, c_width), at)] * (side - 1)
            + [pl.BlockSpec((block, c_width), lambda i, p: (i, 0))],
            out_specs=pl.BlockSpec((block, c_width), at),
        ),
        compiler_params=params(),
        cost_estimate=pl.CostEstimate(
            flops=0, bytes_accessed=(8 + 2 * side) * a_rows * c_width, transcendentals=0
        ),
    )(jnp.stack(origin).astype(jnp.int32), own, *coded, mirror)


def solution(mesh):
    placed = (P("row", "col"), P("row", "col"), P(None, ("row", "col")), P(), P(), P())
    n_row, n_col = mesh.shape["row"], mesh.shape["col"]
    return jax.shard_map(
        functools.partial(body, n_row, n_col),
        mesh=mesh,
        in_specs=placed,
        out_specs=P("row", "col"),
        check_vma=False,
    )
```

```python
import functools
import math

import jax
import jax.numpy as jnp
from jax import lax
from jax.experimental import pallas as pl
from jax.experimental.pallas import tpu as pltpu
from jax.sharding import PartitionSpec as P

BLK = 128
STRIP = 16
LEVELS = 32767.0
FINE = 64.0
VMEM = 24 * 1024 * 1024


def masked(values, flag):
    return values * jnp.full((1, BLK), flag, jnp.float32).astype(jnp.bfloat16)


def masked_tiles(ref, flags, tile_row, tile_col):
    rows, cols = ref.shape
    bands = []
    for t in range(rows // BLK):
        tiles = [
            masked(
                ref[t * BLK : (t + 1) * BLK, u * BLK : (u + 1) * BLK],
                flags[tile_row + t, tile_col + u].astype(jnp.float32),
            )
            for u in range(cols // BLK)
        ]
        bands.append(jnp.concatenate(tiles, axis=1) if len(tiles) > 1 else tiles[0])
    return jnp.concatenate(bands, axis=0) if len(bands) > 1 else bands[0]


def product(pieces, places, r_flags, s_flags, r_refs, s_refs, held):
    rows, width = r_refs[0].shape
    cols = held.shape[2]
    b_tiles, c_tiles = width // BLK, cols // BLK

    @pl.when(pl.program_id(0) == 0)
    def _():
        for e in range(pieces):
            for d, s_ref in enumerate(s_refs):

                @pl.when(places[e] == d)
                def _(e=e, s_ref=s_ref):
                    held[e] = masked_tiles(
                        s_ref, s_flags, places[pieces + e] * b_tiles, places[2 * pieces] * c_tiles
                    )

    total = None
    for e in range(pieces):
        first = pl.program_id(0) * (rows // BLK)
        left = masked_tiles(r_refs[e], r_flags, first, places[pieces + e] * b_tiles)
        term = jnp.dot(left, held[e], preferred_element_type=jnp.float32)
        total = term if total is None else total + term
    return total


def own_kernel(pieces, places, r_flags, s_flags, *refs):
    *ins, out, held = refs
    out[...] = product(pieces, places, r_flags, s_flags, ins[:pieces], ins[pieces:], held)


def coded_kernel(pieces, places, r_flags, s_flags, *refs):
    *ins, out, held = refs
    total = product(pieces, places, r_flags, s_flags, ins[:pieces], ins[pieces:], held)
    rows, cols = total.shape
    group = rows // STRIP
    strip_row = lax.broadcasted_iota(jnp.int32, (STRIP, cols), 0)
    strip = jnp.zeros((STRIP, cols), jnp.float32)
    for g in range(STRIP):
        part = total[g * group : (g + 1) * group]
        top = jnp.max(jnp.max(jnp.abs(part), axis=0, keepdims=True), axis=1, keepdims=True)
        level = jnp.ceil(jnp.log2(jnp.maximum(top, 1e-30)) * FINE) + 1.0
        gain = jnp.exp2(level * (-1.0 / FINE)) * LEVELS
        code = jnp.clip(jnp.round(part * gain), -LEVELS, LEVELS)
        out[g * group : (g + 1) * group] = code.astype(jnp.int16)
        strip = jnp.where(strip_row == g, level, strip)
    out[rows:] = strip.astype(jnp.int16)


def join_kernel(parts, places, own, *refs):
    coded, mirrors, out = refs[:parts], refs[parts:-1], refs[-1]
    rows = own.shape[0]
    group = rows // STRIP
    for e, mirror in enumerate(mirrors):

        @pl.when(pl.program_id(0) == e)
        def _(mirror=mirror):
            for g in range(STRIP):
                at = slice(g * group, (g + 1) * group)
                total = own[at]
                for codes in coded:
                    level = codes[rows:].astype(jnp.float32)[g : g + 1]
                    total += codes[at].astype(jnp.float32) * (
                        jnp.exp2(level * (1.0 / FINE)) * (1.0 / LEVELS)
                    )
                out[at] = (total * mirror[at].astype(jnp.float32)).astype(jnp.bfloat16)


def turn_kernel(pieces, width, places, flags, t_ref, *outs):
    a_width = t_ref.shape[1]
    for e in range(pieces):
        to = places[e]
        for t in range(width // BLK):
            start = pl.multiple_of(to * width + t * BLK, BLK)
            for u in range(a_width // BLK):
                tile = masked(
                    t_ref[pl.ds(start, BLK), u * BLK : (u + 1) * BLK],
                    flags[to * (width // BLK) + t, u].astype(jnp.float32),
                )
                outs[e][u * BLK : (u + 1) * BLK, t * BLK : (t + 1) * BLK] = tile.T


def params(**kwargs):
    return pltpu.CompilerParams(vmem_limit_bytes=VMEM, **kwargs)


def part_product(kernel, places, flags, r_pieces, s_pieces, block, out_rows, dtype, cost):
    pieces = len(r_pieces)
    a_rows, width = r_pieces[0].shape
    cols = s_pieces[0].shape[1]
    steps = a_rows // block
    row_block = lambda i, *_: (i, 0)
    return pl.pallas_call(
        functools.partial(kernel, pieces),
        out_shape=jax.ShapeDtypeStruct((steps * out_rows, cols), dtype),
        grid_spec=pltpu.PrefetchScalarGridSpec(
            num_scalar_prefetch=3,
            grid=(steps,),
            in_specs=[pl.BlockSpec((block, width), row_block)] * pieces
            + [pl.BlockSpec((width, cols), lambda i, *_: (0, 0))] * len(s_pieces),
            out_specs=pl.BlockSpec((out_rows, cols), row_block),
            scratch_shapes=[pltpu.VMEM((pieces, width, cols), jnp.bfloat16)],
        ),
        compiler_params=params(),
        cost_estimate=pl.CostEstimate(flops=cost, bytes_accessed=0, transcendentals=0),
    )(places, *flags, *r_pieces, *s_pieces)


def body(n_row, n_col, r_vals, s_vals, t_vals, r_pattern, s_pattern, t_pattern):
    side = math.isqrt(n_col)
    row = lax.axis_index("row")
    col = lax.axis_index("col")
    line, kind = row // 2, row % 2
    y, x = col // side, col % side
    a_rows, b_width = r_vals.shape
    b_rows, c_width = s_vals.shape
    a_part = t_vals.shape[1]
    a_tiles, ap_tiles = a_rows // BLK, a_part // BLK
    along = kind == 0
    gather_at = jnp.where(along, x, y)
    target_at = jnp.where(along, y, x)
    axes = ("row", "col")

    def place(k, h, yy, xx):
        return (k * 2 + h) * n_col + yy * side + xx

    def shifted(e, gather):
        pairs = []
        for k in range(n_row // 2):
            for h in range(2):
                for yy in range(side):
                    for xx in range(side):
                        if (h == 0) == gather:
                            to = (yy, (xx + e) % side)
                        else:
                            to = ((yy + e) % side, xx)
                        pairs.append((place(k, h, yy, xx), place(k, h, *to)))
        return pairs

    r_pieces = [r_vals] + [lax.ppermute(r_vals, axes, shifted(e, True)) for e in range(1, side)]

    same, other = [], []
    for a in range(side):
        for b in range(side):
            for c in range(side):
                for d in range(side):
                    k = a * side + b
                    to_even = (c * side + b, 0, a, d)
                    to_odd = (a * side + d, 1, c, b)
                    same.append((place(k, 0, c, d), place(*to_even)))
                    same.append((place(k, 1, c, d), place(*to_odd)))
                    other.append((place(k, 1, c, d), place(*to_even)))
                    other.append((place(k, 0, c, d), place(*to_odd)))
    s_same = lax.ppermute(s_vals, axes, same)
    s_other = lax.ppermute(s_vals, axes, other)
    s_held = jnp.concatenate(
        [jnp.where(along, s_same, s_other), jnp.where(along, s_other, s_same)], axis=0
    )
    s_pieces = [s_held]
    for d in range(1, n_col):
        pairs = [
            ((k * 2 + h), (((k + d) % n_col) * 2 + h)) for k in range(n_col) for h in range(2)
        ]
        s_pieces.append(lax.ppermute(s_held, "row", pairs))

    flat = n_col & (n_col - 1) == 0
    partner = [(col ^ e) if flat else (col + e) % n_col for e in range(n_col)]
    origin = [(col ^ e) if flat else (col - e) % n_col for e in range(n_col)]
    t_flags = lax.dynamic_slice_in_dim(t_pattern, (row * n_col + col) * ap_tiles, ap_tiles, 1)
    turned = pl.pallas_call(
        functools.partial(turn_kernel, n_col, c_width),
        out_shape=[jax.ShapeDtypeStruct((a_part, c_width), jnp.bfloat16)] * n_col,
        grid_spec=pltpu.PrefetchScalarGridSpec(
            num_scalar_prefetch=2,
            grid=(1,),
            in_specs=[pl.BlockSpec(t_vals.shape, lambda i, p, f: (0, 0))],
            out_specs=[pl.BlockSpec((a_part, c_width), lambda i, p, f: (0, 0))] * n_col,
        ),
        compiler_params=params(),
        cost_estimate=pl.CostEstimate(
            flops=0, bytes_accessed=4 * a_part * c_width * n_col, transcendentals=0
        ),
    )(jnp.stack(partner).astype(jnp.int32), t_flags, t_vals)
    held = lax.optimization_barrier(tuple(r_pieces[1:]) + tuple(turned))
    r_pieces = r_pieces[:1] + list(held[: side - 1])
    turned = held[side - 1 :]
    mirrors = [turned[0]]
    for e in range(1, n_col):
        pairs = [(j, (j ^ e) if flat else (j + e) % n_col) for j in range(n_col)]
        mirrors.append(lax.ppermute(turned[e], "col", pairs))

    flags = (lax.dynamic_slice_in_dim(r_pattern, row * a_tiles, a_tiles, 0), s_pattern)

    def places(target):
        spots, blocks = [], []
        for e in range(side):
            g = (gather_at - e) % side
            k = jnp.where(along, target * side + g, g * side + target)
            spots.append((line - k) % n_col)
            blocks.append(jnp.where(along, y * side + g, g * side + x))
        to = jnp.where(along, target * side + x, y * side + target)
        return jnp.stack(spots + blocks + [to]).astype(jnp.int32)

    block = a_part
    work = 2 * a_rows * side * b_width * c_width
    coded = []
    for e in range(1, side):
        codes = part_product(
            coded_kernel, places((target_at + e) % side), flags, r_pieces, s_pieces,
            block, block + STRIP, jnp.int16, 16 * work,
        )
        coded.append(lax.ppermute(codes, axes, shifted(e, False)))
    own = part_product(
        own_kernel, places(target_at), flags, r_pieces, s_pieces, block, block, jnp.float32, work // 16
    )

    at = lambda i, p: (p[i], 0)
    return pl.pallas_call(
        functools.partial(join_kernel, side - 1),
        out_shape=jax.ShapeDtypeStruct((a_rows, c_width), jnp.bfloat16),
        grid_spec=pltpu.PrefetchScalarGridSpec(
            num_scalar_prefetch=1,
            grid=(n_col,),
            in_specs=[pl.BlockSpec((block, c_width), at)]
            + [pl.BlockSpec((block + STRIP, c_width), at)] * (side - 1)
            + [pl.BlockSpec((block, c_width), lambda i, p: (0, 0))] * n_col,
            out_specs=pl.BlockSpec((block, c_width), at),
        ),
        compiler_params=params(),
        cost_estimate=pl.CostEstimate(
            flops=0, bytes_accessed=(8 + 2 * side) * a_rows * c_width, transcendentals=0
        ),
    )(jnp.stack(origin).astype(jnp.int32), own, *coded, *mirrors)


def solution(mesh):
    placed = (P("row", "col"), P("row", "col"), P(None, ("row", "col")), P(), P(), P())
    n_row, n_col = mesh.shape["row"], mesh.shape["col"]
    return jax.shard_map(
        functools.partial(body, n_row, n_col),
        mesh=mesh,
        in_specs=placed,
        out_specs=P("row", "col"),
        check_vma=False,
    )
```

```python
import functools
import math

import jax
import jax.numpy as jnp
from jax import lax
from jax.experimental import pallas as pl
from jax.experimental.pallas import tpu as pltpu
from jax.sharding import PartitionSpec as P

BLK = 128
STRIP = 16
LEVELS = 32767.0
FINE = 64.0
VMEM = 24 * 1024 * 1024


def masked(values, flag):
    return values * jnp.full((1, BLK), flag, jnp.float32).astype(jnp.bfloat16)


def masked_tiles(ref, flags, tile_row, tile_col):
    rows, cols = ref.shape
    bands = []
    for t in range(rows // BLK):
        tiles = [
            masked(
                ref[t * BLK : (t + 1) * BLK, u * BLK : (u + 1) * BLK],
                flags[tile_row + t, tile_col + u].astype(jnp.float32),
            )
            for u in range(cols // BLK)
        ]
        bands.append(jnp.concatenate(tiles, axis=1) if len(tiles) > 1 else tiles[0])
    return jnp.concatenate(bands, axis=0) if len(bands) > 1 else bands[0]


def product(pieces, places, r_flags, s_flags, r_refs, s_refs, held):
    rows, width = r_refs[0].shape
    cols = held.shape[2]
    b_tiles, c_tiles = width // BLK, cols // BLK

    @pl.when(pl.program_id(0) == 0)
    def _():
        for e in range(pieces):
            for d, s_ref in enumerate(s_refs):

                @pl.when(places[e] == d)
                def _(e=e, s_ref=s_ref):
                    held[e] = masked_tiles(
                        s_ref, s_flags, places[pieces + e] * b_tiles, places[2 * pieces] * c_tiles
                    )

    total = None
    for e in range(pieces):
        first = pl.program_id(0) * (rows // BLK)
        left = masked_tiles(r_refs[e], r_flags, first, places[pieces + e] * b_tiles)
        term = jnp.dot(left, held[e], preferred_element_type=jnp.float32)
        total = term if total is None else total + term
    return total


def own_kernel(pieces, places, r_flags, s_flags, *refs):
    *ins, out, held = refs
    out[...] = product(pieces, places, r_flags, s_flags, ins[:pieces], ins[pieces:], held)


def coded_kernel(pieces, places, r_flags, s_flags, *refs):
    *ins, out, held = refs
    total = product(pieces, places, r_flags, s_flags, ins[:pieces], ins[pieces:], held)
    rows, cols = total.shape
    group = rows // STRIP
    strip_row = lax.broadcasted_iota(jnp.int32, (STRIP, cols), 0)
    strip = jnp.zeros((STRIP, cols), jnp.float32)
    for g in range(STRIP):
        part = total[g * group : (g + 1) * group]
        top = jnp.max(jnp.max(jnp.abs(part), axis=0, keepdims=True), axis=1, keepdims=True)
        level = jnp.ceil(jnp.log2(jnp.maximum(top, 1e-30)) * FINE) + 1.0
        gain = jnp.exp2(level * (-1.0 / FINE)) * LEVELS
        code = jnp.clip(jnp.round(part * gain), -LEVELS, LEVELS)
        out[g * group : (g + 1) * group] = code.astype(jnp.int16)
        strip = jnp.where(strip_row == g, level, strip)
    out[rows:] = strip.astype(jnp.int16)


def join_kernel(parts, places, own, *refs):
    coded, mirrors, out = refs[:parts], refs[parts:-1], refs[-1]
    rows = own.shape[0]
    group = rows // STRIP
    for e, mirror in enumerate(mirrors):

        @pl.when(pl.program_id(0) == e)
        def _(mirror=mirror):
            for g in range(STRIP):
                at = slice(g * group, (g + 1) * group)
                total = own[at]
                for codes in coded:
                    level = codes[rows:].astype(jnp.float32)[g : g + 1]
                    total += codes[at].astype(jnp.float32) * (
                        jnp.exp2(level * (1.0 / FINE)) * (1.0 / LEVELS)
                    )
                out[at] = (total * mirror[at].astype(jnp.float32)).astype(jnp.bfloat16)


def turn_kernel(pieces, width, places, flags, t_ref, *outs):
    a_width = t_ref.shape[1]
    for e in range(pieces):
        to = places[e]
        for t in range(width // BLK):
            start = pl.multiple_of(to * width + t * BLK, BLK)
            for u in range(a_width // BLK):
                tile = masked(
                    t_ref[pl.ds(start, BLK), u * BLK : (u + 1) * BLK],
                    flags[to * (width // BLK) + t, u].astype(jnp.float32),
                )
                outs[e][u * BLK : (u + 1) * BLK, t * BLK : (t + 1) * BLK] = tile.T


def params(**kwargs):
    return pltpu.CompilerParams(vmem_limit_bytes=VMEM, **kwargs)


def part_product(kernel, places, flags, r_pieces, s_pieces, block, out_rows, dtype, cost):
    pieces = len(r_pieces)
    a_rows, width = r_pieces[0].shape
    cols = s_pieces[0].shape[1]
    steps = a_rows // block
    row_block = lambda i, *_: (i, 0)
    return pl.pallas_call(
        functools.partial(kernel, pieces),
        out_shape=jax.ShapeDtypeStruct((steps * out_rows, cols), dtype),
        grid_spec=pltpu.PrefetchScalarGridSpec(
            num_scalar_prefetch=3,
            grid=(steps,),
            in_specs=[pl.BlockSpec((block, width), row_block)] * pieces
            + [pl.BlockSpec((width, cols), lambda i, *_: (0, 0))] * len(s_pieces),
            out_specs=pl.BlockSpec((out_rows, cols), row_block),
            scratch_shapes=[pltpu.VMEM((pieces, width, cols), jnp.bfloat16)],
        ),
        compiler_params=params(),
        cost_estimate=pl.CostEstimate(flops=cost, bytes_accessed=0, transcendentals=0),
    )(places, *flags, *r_pieces, *s_pieces)


def body(n_row, n_col, r_vals, s_vals, t_vals, r_pattern, s_pattern, t_pattern):
    side = math.isqrt(n_col)
    row = lax.axis_index("row")
    col = lax.axis_index("col")
    line, kind = row // 2, row % 2
    y, x = col // side, col % side
    a_rows, b_width = r_vals.shape
    b_rows, c_width = s_vals.shape
    a_part = t_vals.shape[1]
    a_tiles, ap_tiles = a_rows // BLK, a_part // BLK
    along = kind == 0
    gather_at = jnp.where(along, x, y)
    target_at = jnp.where(along, y, x)
    axes = ("row", "col")

    def place(k, h, yy, xx):
        return (k * 2 + h) * n_col + yy * side + xx

    def shifted(e, gather):
        pairs = []
        for k in range(n_row // 2):
            for h in range(2):
                for yy in range(side):
                    for xx in range(side):
                        if (h == 0) == gather:
                            to = (yy, (xx + e) % side)
                        else:
                            to = ((yy + e) % side, xx)
                        pairs.append((place(k, h, yy, xx), place(k, h, *to)))
        return pairs

    same, other = [], []
    for a in range(side):
        for b in range(side):
            for c in range(side):
                for d in range(side):
                    k = a * side + b
                    to_even = (c * side + b, 0, a, d)
                    to_odd = (a * side + d, 1, c, b)
                    same.append((place(k, 0, c, d), place(*to_even)))
                    same.append((place(k, 1, c, d), place(*to_odd)))
                    other.append((place(k, 1, c, d), place(*to_even)))
                    other.append((place(k, 0, c, d), place(*to_odd)))
    s_same = lax.ppermute(s_vals, axes, same)
    s_other = lax.ppermute(s_vals, axes, other)
    r_sent, s_same, s_other = lax.optimization_barrier((r_vals, s_same, s_other))
    r_pieces = [r_vals] + [lax.ppermute(r_sent, axes, shifted(e, True)) for e in range(1, side)]
    s_held = jnp.concatenate(
        [jnp.where(along, s_same, s_other), jnp.where(along, s_other, s_same)], axis=0
    )
    s_pieces = [s_held]
    for d in range(1, n_col):
        pairs = [
            ((k * 2 + h), (((k + d) % n_col) * 2 + h)) for k in range(n_col) for h in range(2)
        ]
        s_pieces.append(lax.ppermute(s_held, "row", pairs))

    flat = n_col & (n_col - 1) == 0
    partner = [(col ^ e) if flat else (col + e) % n_col for e in range(n_col)]
    origin = [(col ^ e) if flat else (col - e) % n_col for e in range(n_col)]
    t_flags = lax.dynamic_slice_in_dim(t_pattern, (row * n_col + col) * ap_tiles, ap_tiles, 1)
    turned = pl.pallas_call(
        functools.partial(turn_kernel, n_col, c_width),
        out_shape=[pltpu.HBM((a_part, c_width), jnp.bfloat16)] * n_col,
        grid_spec=pltpu.PrefetchScalarGridSpec(
            num_scalar_prefetch=2,
            grid=(1,),
            in_specs=[pl.BlockSpec(t_vals.shape, lambda i, p, f: (0, 0))],
            out_specs=[pl.BlockSpec((a_part, c_width), lambda i, p, f: (0, 0))] * n_col,
        ),
        compiler_params=params(),
        cost_estimate=pl.CostEstimate(
            flops=0, bytes_accessed=4 * a_part * c_width * n_col, transcendentals=0
        ),
    )(jnp.stack(partner).astype(jnp.int32), t_flags, t_vals)
    held = lax.optimization_barrier(tuple(r_pieces[1:]) + tuple(turned))
    r_pieces = r_pieces[:1] + list(held[: side - 1])
    turned = held[side - 1 :]
    mirrors = [turned[0]]
    for e in range(1, n_col):
        pairs = [(j, (j ^ e) if flat else (j + e) % n_col) for j in range(n_col)]
        mirrors.append(lax.ppermute(turned[e], "col", pairs))

    flags = (lax.dynamic_slice_in_dim(r_pattern, row * a_tiles, a_tiles, 0), s_pattern)

    def places(target):
        spots, blocks = [], []
        for e in range(side):
            g = (gather_at - e) % side
            k = jnp.where(along, target * side + g, g * side + target)
            spots.append((line - k) % n_col)
            blocks.append(jnp.where(along, y * side + g, g * side + x))
        to = jnp.where(along, target * side + x, y * side + target)
        return jnp.stack(spots + blocks + [to]).astype(jnp.int32)

    block = a_part
    work = 2 * a_rows * side * b_width * c_width
    coded = []
    for e in range(1, side):
        codes = part_product(
            coded_kernel, places((target_at + e) % side), flags, r_pieces, s_pieces,
            block, block + STRIP, jnp.int16, work // 16,
        )
        ready = lax.optimization_barrier((codes, *mirrors[1:-1]))
        mirrors[1:-1] = ready[1:]
        coded.append(lax.ppermute(ready[0], axes, shifted(e, False)))
    own = part_product(
        own_kernel, places(target_at), flags, r_pieces, s_pieces, block, block, jnp.float32, work // 16
    )

    at = lambda i, p: (p[i], 0)
    return pl.pallas_call(
        functools.partial(join_kernel, side - 1),
        out_shape=jax.ShapeDtypeStruct((a_rows, c_width), jnp.bfloat16),
        grid_spec=pltpu.PrefetchScalarGridSpec(
            num_scalar_prefetch=1,
            grid=(n_col,),
            in_specs=[pl.BlockSpec((block, c_width), at)]
            + [pl.BlockSpec((block + STRIP, c_width), at)] * (side - 1)
            + [pl.BlockSpec((block, c_width), lambda i, p: (0, 0))] * n_col,
            out_specs=pl.BlockSpec((block, c_width), at),
        ),
        compiler_params=params(),
        cost_estimate=pl.CostEstimate(
            flops=0, bytes_accessed=(8 + 2 * side) * a_rows * c_width, transcendentals=0
        ),
    )(jnp.stack(origin).astype(jnp.int32), own, *coded, *mirrors)


def solution(mesh):
    placed = (P("row", "col"), P("row", "col"), P(None, ("row", "col")), P(), P(), P())
    n_row, n_col = mesh.shape["row"], mesh.shape["col"]
    return jax.shard_map(
        functools.partial(body, n_row, n_col),
        mesh=mesh,
        in_specs=placed,
        out_specs=P("row", "col"),
        check_vma=False,
    )
```

```python
import functools
import math

import jax
import jax.numpy as jnp
from jax import lax
from jax.experimental import pallas as pl
from jax.experimental.pallas import tpu as pltpu
from jax.sharding import PartitionSpec as P

BLK = 128
STRIP = 16
LEVELS = 32767.0
FINE = 64.0
VMEM = 63 * 1024 * 1024


def masked(values, flag):
    return values * jnp.full((1, BLK), flag, jnp.float32).astype(jnp.bfloat16)


def masked_tiles(ref, flags, tile_row, tile_col):
    rows, cols = ref.shape
    bands = []
    for t in range(rows // BLK):
        tiles = [
            masked(
                ref[t * BLK : (t + 1) * BLK, u * BLK : (u + 1) * BLK],
                flags[tile_row + t, tile_col + u].astype(jnp.float32),
            )
            for u in range(cols // BLK)
        ]
        bands.append(jnp.concatenate(tiles, axis=1) if len(tiles) > 1 else tiles[0])
    return jnp.concatenate(bands, axis=0) if len(bands) > 1 else bands[0]


def product(pieces, places, r_flags, s_flags, r_refs, s_refs, held, first=0):
    rows, width = r_refs[0].shape
    cols = held.shape[2]
    b_tiles, c_tiles = width // BLK, cols // BLK

    @pl.when(pl.program_id(0) == 0)
    def _():
        for e in range(pieces):
            for d, s_ref in enumerate(s_refs):

                @pl.when(places[e] == d)
                def _(e=e, s_ref=s_ref):
                    held[e] = masked_tiles(
                        s_ref, s_flags, places[pieces + e] * b_tiles, places[2 * pieces] * c_tiles
                    )

    total = None
    for e in range(pieces):
        tile_row = (pl.program_id(0) + first) * (rows // BLK)
        left = masked_tiles(r_refs[e], r_flags, tile_row, places[pieces + e] * b_tiles)
        term = jnp.dot(left, held[e], preferred_element_type=jnp.float32)
        total = term if total is None else total + term
    return total


def own_kernel(pieces, places, r_flags, s_flags, t_flags, *refs):
    *ins, out, mirror, held = refs
    count = (len(ins) - pieces) // 2
    r_refs, s_refs, t_refs = ins[:pieces], ins[pieces : pieces + count], ins[pieces + count :]
    step = pl.program_id(0)
    a_width, c_width = mirror.shape
    for e, t_ref in enumerate(t_refs):

        @pl.when(places[2 * pieces + 1 + step] == e)
        def _(t_ref=t_ref):
            for t in range(c_width // BLK):
                for u in range(a_width // BLK):
                    tile = masked(
                        t_ref[t * BLK : (t + 1) * BLK, u * BLK : (u + 1) * BLK],
                        t_flags[t, step * (a_width // BLK) + u].astype(jnp.float32),
                    )
                    mirror[u * BLK : (u + 1) * BLK, t * BLK : (t + 1) * BLK] = tile.T

    out[...] = product(pieces, places, r_flags, s_flags, r_refs, s_refs, held)


def coded_kernel(pieces, first, places, r_flags, s_flags, *refs):
    *ins, out, held = refs
    total = product(pieces, places, r_flags, s_flags, ins[:pieces], ins[pieces:], held, first)
    rows, cols = total.shape
    group = rows // STRIP
    strip_row = lax.broadcasted_iota(jnp.int32, (STRIP, cols), 0)
    strip = jnp.zeros((STRIP, cols), jnp.float32)
    for g in range(STRIP):
        part = total[g * group : (g + 1) * group]
        top = jnp.max(jnp.max(jnp.abs(part), axis=0, keepdims=True), axis=1, keepdims=True)
        level = jnp.ceil(jnp.log2(jnp.maximum(top, 1e-30)) * FINE) + 1.0
        gain = jnp.exp2(level * (-1.0 / FINE)) * LEVELS
        code = jnp.clip(jnp.round(part * gain), -LEVELS, LEVELS)
        out[g * group : (g + 1) * group] = code.astype(jnp.int16)
        strip = jnp.where(strip_row == g, level, strip)
    out[rows:] = strip.astype(jnp.int16)


def join_kernel(parts, own, mirror, *refs):
    out = refs[-1]
    rows = own.shape[0]
    group = rows // STRIP
    for g in range(STRIP):
        at = slice(g * group, (g + 1) * group)
        total = own[at]
        for codes in refs[:parts]:
            level = codes[rows:].astype(jnp.float32)[g : g + 1]
            total += codes[at].astype(jnp.float32) * (
                jnp.exp2(level * (1.0 / FINE)) * (1.0 / LEVELS)
            )
        out[at] = (total * mirror[at].astype(jnp.float32)).astype(jnp.bfloat16)


def params(**kwargs):
    return pltpu.CompilerParams(vmem_limit_bytes=VMEM, **kwargs)


def whole(shape):
    return pl.BlockSpec(shape, lambda i, *_: (0, 0))


def cost(flops, bytes_accessed):
    return pl.CostEstimate(flops=flops, bytes_accessed=bytes_accessed, transcendentals=0)


def coded_product(places, flags, r_pieces, s_pieces, block, first, steps):
    pieces = len(r_pieces)
    width = r_pieces[0].shape[1]
    cols = s_pieces[0].shape[1]
    return pl.pallas_call(
        functools.partial(coded_kernel, pieces, first),
        out_shape=jax.ShapeDtypeStruct((steps * (block + STRIP), cols), jnp.int16),
        grid_spec=pltpu.PrefetchScalarGridSpec(
            num_scalar_prefetch=3,
            grid=(steps,),
            in_specs=[pl.BlockSpec((block, width), lambda i, *_: (i + first, 0))] * pieces
            + [whole((width, cols))] * len(s_pieces),
            out_specs=pl.BlockSpec((block + STRIP, cols), lambda i, *_: (i, 0)),
            scratch_shapes=[pltpu.VMEM((pieces, width, cols), jnp.bfloat16)],
        ),
        compiler_params=params(),
        cost_estimate=cost(2 * steps * block * pieces * width * cols // 16, 0),
    )(places, *flags, *r_pieces, *s_pieces)


def own_product(places, flags, r_pieces, s_pieces, t_vals, t_pieces, col, block):
    pieces = len(r_pieces)
    a_rows, width = r_pieces[0].shape
    cols = s_pieces[0].shape[1]
    by_step = lambda i, *_: (i, 0)
    last = 2 * pieces + 1 + a_rows // block
    places = jnp.concatenate([places, col[None].astype(jnp.int32)])
    return pl.pallas_call(
        functools.partial(own_kernel, pieces),
        out_shape=[
            jax.ShapeDtypeStruct((a_rows, cols), jnp.float32),
            jax.ShapeDtypeStruct((a_rows, cols), jnp.bfloat16),
        ],
        grid_spec=pltpu.PrefetchScalarGridSpec(
            num_scalar_prefetch=4,
            grid=(a_rows // block,),
            in_specs=[pl.BlockSpec((block, width), by_step)] * pieces
            + [whole((width, cols))] * len(s_pieces)
            + [pl.BlockSpec((cols, block), lambda i, p, *_: (p[last], 0))]
            + [whole((cols, block))] * len(t_pieces),
            out_specs=[pl.BlockSpec((block, cols), by_step)] * 2,
            scratch_shapes=[pltpu.VMEM((pieces, width, cols), jnp.bfloat16)],
        ),
        compiler_params=params(),
        cost_estimate=cost(2 * a_rows * pieces * width * cols // 16, 0),
    )(places, *flags, *r_pieces, *s_pieces, t_vals, *t_pieces)


def join(own, mirror, coded, block, first, steps, before):
    rows, cols = own.shape
    here = pl.BlockSpec((block, cols), lambda i: (i + first, 0))
    kernel = functools.partial(join_kernel, len(coded))
    aliases, carried = {}, ()
    if before is not None:
        aliases, carried = {2 + len(coded): 0}, (before,)
    return pl.pallas_call(
        kernel,
        out_shape=jax.ShapeDtypeStruct((rows, cols), jnp.bfloat16),
        grid=(steps,),
        in_specs=[here, here]
        + [pl.BlockSpec((block + STRIP, cols), lambda i: (i, 0))] * len(coded)
        + [pl.BlockSpec(memory_space=pl.ANY)] * len(carried),
        out_specs=here,
        input_output_aliases=aliases,
        compiler_params=params(),
        cost_estimate=cost(0, 0),
    )(own, mirror, *coded, *carried)


def body(n_row, n_col, r_vals, s_vals, t_vals, r_pattern, s_pattern, t_pattern):
    side = math.isqrt(n_col)
    row = lax.axis_index("row")
    col = lax.axis_index("col")
    line, kind = row // 2, row % 2
    y, x = col // side, col % side
    a_rows, b_width = r_vals.shape
    b_rows, c_width = s_vals.shape
    a_part = t_vals.shape[1]
    a_tiles, ap_tiles = a_rows // BLK, a_part // BLK
    along = kind == 0
    gather_at = jnp.where(along, x, y)
    target_at = jnp.where(along, y, x)
    axes = ("row", "col")

    def place(k, h, yy, xx):
        return (k * 2 + h) * n_col + yy * side + xx

    def shifted(e, gather):
        pairs = []
        for k in range(n_row // 2):
            for h in range(2):
                for yy in range(side):
                    for xx in range(side):
                        if (h == 0) == gather:
                            to = (yy, (xx + e) % side)
                        else:
                            to = ((yy + e) % side, xx)
                        pairs.append((place(k, h, yy, xx), place(k, h, *to)))
        return pairs

    r_pieces = [r_vals] + [
        lax.ppermute(r_vals, axes, shifted(e, True)) for e in range(1, side)
    ]

    same, other = [], []
    for a in range(side):
        for b in range(side):
            for c in range(side):
                for d in range(side):
                    k = a * side + b
                    to_even = (c * side + b, 0, a, d)
                    to_odd = (a * side + d, 1, c, b)
                    same.append((place(k, 0, c, d), place(*to_even)))
                    same.append((place(k, 1, c, d), place(*to_odd)))
                    other.append((place(k, 1, c, d), place(*to_even)))
                    other.append((place(k, 0, c, d), place(*to_odd)))
    s_same = lax.ppermute(s_vals, axes, same)
    s_other = lax.ppermute(s_vals, axes, other)
    s_held = jnp.concatenate(
        [jnp.where(along, s_same, s_other), jnp.where(along, s_other, s_same)], axis=0
    )
    s_pieces = [s_held]
    for d in range(1, n_col):
        pairs = [
            ((k * 2 + h), (((k + d) % n_col) * 2 + h)) for k in range(n_col) for h in range(2)
        ]
        s_pieces.append(lax.ppermute(s_held, "row", pairs))

    flat = n_col & (n_col - 1) == 0
    t_pieces = []
    for e in range(1, n_col):
        pairs = [(j, (j ^ e) if flat else (j + e) % n_col) for j in range(n_col)]
        to = (col ^ e) if flat else (col + e) % n_col
        sent = lax.dynamic_slice_in_dim(t_vals, to * c_width, c_width, 0)
        t_pieces.append(lax.ppermute(sent, "col", pairs))
    c_tiles = c_width // BLK
    t_flags = lax.dynamic_slice(
        t_pattern, (col * c_tiles, row * a_tiles), (c_tiles, a_tiles)
    )

    flags = (lax.dynamic_slice_in_dim(r_pattern, row * a_tiles, a_tiles, 0), s_pattern)

    def places(target):
        spots, blocks = [], []
        for e in range(side):
            g = (gather_at - e) % side
            k = jnp.where(along, target * side + g, g * side + target)
            spots.append((line - k) % n_col)
            blocks.append(jnp.where(along, y * side + g, g * side + x))
        to = jnp.where(along, target * side + x, y * side + target)
        return jnp.stack(spots + blocks + [to]).astype(jnp.int32)

    block = a_part
    blocks = a_rows // block
    chunks = 2 if blocks % 2 == 0 else 1
    steps = blocks // chunks
    coded = []
    for chunk in range(chunks):
        if chunk:
            held = lax.optimization_barrier((*r_pieces[1:], *t_pieces))
            r_pieces[1:], t_pieces = held[: side - 1], list(held[side - 1 :])
        parts = []
        for e in range(1, side):
            codes = coded_product(
                places((target_at + e) % side), flags, r_pieces, s_pieces,
                block, chunk * steps, steps,
            )
            parts.append(lax.ppermute(codes, axes, shifted(e, False)))
        coded.append(parts)
    order = [(col ^ o) if flat else (col - o) % n_col for o in range(n_col)]
    own, mirror = own_product(
        jnp.concatenate([places(target_at), jnp.stack(order).astype(jnp.int32)]),
        (*flags, t_flags), r_pieces, s_pieces, t_vals, t_pieces, col, block,
    )
    out = None
    for chunk in range(chunks):
        out = join(own, mirror, coded[chunk], block, chunk * steps, steps, out)
    return out


def solution(mesh):
    placed = (P("row", "col"), P("row", "col"), P(None, ("row", "col")), P(), P(), P())
    n_row, n_col = mesh.shape["row"], mesh.shape["col"]
    return jax.shard_map(
        functools.partial(body, n_row, n_col),
        mesh=mesh,
        in_specs=placed,
        out_specs=P("row", "col"),
        check_vma=False,
    )
```

```python
import functools
import math

import jax
import jax.numpy as jnp
from jax import lax
from jax.experimental import pallas as pl
from jax.experimental.pallas import tpu as pltpu
from jax.sharding import PartitionSpec as P

BLK = 128
STRIP = 16
LEVELS = 32767.0
FINE = 64.0
VMEM = 63 * 1024 * 1024


def masked(values, flag):
    return values * jnp.full((1, BLK), flag.astype(jnp.float32)).astype(jnp.bfloat16)


def joined_tiles(grid):
    bands = [jnp.concatenate(t, axis=1) if len(t) > 1 else t[0] for t in grid]
    return jnp.concatenate(bands, axis=0) if len(bands) > 1 else bands[0]


def whole(shape):
    return pl.BlockSpec(shape, lambda i, *_: (0,) * len(shape))


def cost(flops, bytes_accessed):
    return pl.CostEstimate(flops=flops, bytes_accessed=bytes_accessed, transcendentals=0)


def params():
    return pltpu.CompilerParams(vmem_limit_bytes=VMEM)


def order_kernel(side, places, flags, *refs):
    *pieces, out = refs
    _, width, cols = out.shape
    slots = side * side
    b_tiles, c_tiles = width // BLK, cols // BLK

    def one(n, carry):
        slot, rest = n // (b_tiles * c_tiles), n % (b_tiles * c_tiles)
        t, u = rest // c_tiles, rest % c_tiles
        flag = flags[places[slots + slot] * b_tiles + t, places[2 * slots + slot // side] * c_tiles + u]
        down = pl.ds(pl.multiple_of(t * BLK, BLK), BLK)
        over = pl.ds(pl.multiple_of(u * BLK, BLK), BLK)
        total = None
        for d, piece in enumerate(pieces):
            term = masked(piece[down, over], jnp.where(places[slot] == d, flag, 0))
            total = term if total is None else total + term
        out[slot, down, over] = total
        return carry

    lax.fori_loop(0, slots * b_tiles * c_tiles, one, 0)


def order_pieces(side, places, flags, pieces):
    shape = (side * side, *pieces[0].shape)
    return pl.pallas_call(
        functools.partial(order_kernel, side),
        out_shape=jax.ShapeDtypeStruct(shape, jnp.bfloat16),
        grid_spec=pltpu.PrefetchScalarGridSpec(
            num_scalar_prefetch=2,
            grid=(1,),
            in_specs=[whole(pieces[0].shape)] * len(pieces),
            out_specs=whole(shape),
        ),
        compiler_params=params(),
        cost_estimate=cost(0, 0),
    )(places, flags, *pieces)


def band_product(pieces, table, first, n, rows, r_refs, s_ref):
    width = r_refs[0].shape[1]
    b_tiles = width // BLK
    b_all = table[pieces]
    total = None
    for e in range(pieces):
        grid = []
        for t in range(rows // BLK):
            down = pl.ds(pl.multiple_of(n * rows + t * BLK, BLK), BLK)
            at = (first + n * (rows // BLK) + t) * b_all + table[e] * b_tiles + pieces + 1
            grid.append(
                [masked(r_refs[e][down, u * BLK : (u + 1) * BLK], table[at + u]) for u in range(b_tiles)]
            )
        term = jnp.dot(joined_tiles(grid), s_ref[e], preferred_element_type=jnp.float32)
        total = term if total is None else total + term
    return total


def coded_kernel(pieces, first, band, table, *refs):
    *r_refs, s_ref, out = refs
    rows, cols = r_refs[0].shape[0], s_ref.shape[2]
    group = rows // STRIP
    tile_row = (pl.program_id(0) + first) * (rows // BLK)
    strip_row = lax.broadcasted_iota(jnp.int32, (STRIP, cols), 0)

    def one(n, strip):
        total = band_product(pieces, table, tile_row, n, band, r_refs, s_ref)
        for g in range(band // group):
            part = total[g * group : (g + 1) * group]
            top = jnp.max(jnp.max(jnp.abs(part), axis=0, keepdims=True), axis=1, keepdims=True)
            level = jnp.ceil(jnp.log2(jnp.maximum(top, 1e-30)) * FINE) + 1.0
            gain = jnp.exp2(level * (-1.0 / FINE)) * LEVELS
            code = jnp.clip(jnp.round(part * gain), -LEVELS, LEVELS)
            down = pl.ds(pl.multiple_of(n * band + g * group, group), group)
            out[down] = code.astype(jnp.int16)
            strip = jnp.where(strip_row == n * (band // group) + g, level, strip)
        return strip

    strip = lax.fori_loop(0, rows // band, one, jnp.zeros((STRIP, cols), jnp.float32))
    out[rows:] = strip.astype(jnp.int16)


def coded_product(table, r_pieces, s_eff, target, block, first, steps):
    pieces = len(r_pieces)
    width, cols = s_eff.shape[1:]
    return pl.pallas_call(
        functools.partial(coded_kernel, pieces, first, min(block, 2 * BLK)),
        out_shape=jax.ShapeDtypeStruct((steps * (block + STRIP), cols), jnp.int16),
        grid_spec=pltpu.PrefetchScalarGridSpec(
            num_scalar_prefetch=1,
            grid=(steps,),
            in_specs=[pl.BlockSpec((block, width), lambda i, *_: (i + first, 0))] * pieces
            + [pl.BlockSpec((pieces, width, cols), lambda i, *_: (target, 0, 0))],
            out_specs=pl.BlockSpec((block + STRIP, cols), lambda i, *_: (i, 0)),
        ),
        compiler_params=params(),
        cost_estimate=cost(2 * steps * block * pieces * width * cols // 16, 0),
    )(table, *r_pieces, s_eff)


def own_kernel(pieces, band, table, order, *refs):
    r_refs, s_ref = refs[:pieces], refs[pieces]
    *t_refs, out, mirror = refs[pieces + 1 :]
    rows = out.shape[0]
    a_part = t_refs[0].shape[0]
    step = pl.program_id(0)
    for j in range(rows // a_part):
        for e, t_ref in enumerate(t_refs):

            @pl.when(order[step * (rows // a_part) + j] == e)
            def _(j=j, t_ref=t_ref):
                mirror[j * a_part : (j + 1) * a_part] = t_ref[...]

    def one(n, carry):
        down = pl.ds(pl.multiple_of(n * band, band), band)
        out[down] = band_product(pieces, table, step * (rows // BLK), n, band, r_refs, s_ref)
        return carry

    lax.fori_loop(0, rows // band, one, 0)


def own_product(table, order, r_pieces, s_eff, t_pieces, block):
    pieces = len(r_pieces)
    a_rows, width = r_pieces[0].shape
    cols = s_eff.shape[2]
    by_step = lambda i, *_: (i, 0)
    return pl.pallas_call(
        functools.partial(own_kernel, pieces, min(block, 2 * BLK)),
        out_shape=[
            jax.ShapeDtypeStruct((a_rows, cols), jnp.float32),
            jax.ShapeDtypeStruct((a_rows, cols), jnp.bfloat16),
        ],
        grid_spec=pltpu.PrefetchScalarGridSpec(
            num_scalar_prefetch=2,
            grid=(a_rows // block,),
            in_specs=[pl.BlockSpec((block, width), by_step)] * pieces
            + [pl.BlockSpec((pieces, width, cols), lambda i, *_: (0, 0, 0))]
            + [whole(t.shape) for t in t_pieces],
            out_specs=[pl.BlockSpec((block, cols), by_step)] * 2,
        ),
        compiler_params=params(),
        cost_estimate=cost(2 * a_rows * pieces * width * cols // 16, 0),
    )(table, order, *r_pieces, s_eff, *t_pieces)


def join_kernel(parts, own, mirror, *refs):
    gains, out = refs[-1], refs[-2]
    rows = own.shape[0]
    group = rows // STRIP
    for k in range(parts):
        level = refs[k][rows:].astype(jnp.float32)
        gains[k] = jnp.exp2(level * (1.0 / FINE)) * (1.0 / LEVELS)

    def one(g, carry):
        at = pl.ds(pl.multiple_of(g * group, group), group)
        total = own[at]
        for k in range(parts):
            total += refs[k][at].astype(jnp.float32) * gains[k, pl.ds(g, 1)]
        out[at] = (total * mirror[at].astype(jnp.float32)).astype(jnp.bfloat16)
        return carry

    lax.fori_loop(0, STRIP, one, 0)


def join(own, mirror, coded, block, first, steps, before):
    rows, cols = own.shape
    here = pl.BlockSpec((block, cols), lambda i: (i + first, 0))
    aliases, carried = {}, ()
    if before is not None:
        aliases, carried = {2 + len(coded): 0}, (before,)
    return pl.pallas_call(
        functools.partial(join_kernel, len(coded)),
        out_shape=jax.ShapeDtypeStruct((rows, cols), jnp.bfloat16),
        grid=(steps,),
        in_specs=[here, here]
        + [pl.BlockSpec((block + STRIP, cols), lambda i: (i, 0))] * len(coded)
        + [pl.BlockSpec(memory_space=pl.ANY)] * len(carried),
        out_specs=here,
        scratch_shapes=[pltpu.VMEM((len(coded), STRIP, cols), jnp.float32)],
        input_output_aliases=aliases,
        compiler_params=params(),
        cost_estimate=cost(0, 0),
    )(own, mirror, *coded, *carried)


def turn_kernel(pieces, width, places, flags, t_ref, *outs):
    a_width = t_ref.shape[1]
    for e in range(pieces):

        def one(t, carry, e=e):
            start = pl.multiple_of(places[e] * width + t * BLK, BLK)
            over = pl.ds(pl.multiple_of(t * BLK, BLK), BLK)
            for u in range(a_width // BLK):
                tile = masked(
                    t_ref[pl.ds(start, BLK), u * BLK : (u + 1) * BLK],
                    flags[places[e] * (width // BLK) + t, u],
                )
                outs[e][u * BLK : (u + 1) * BLK, over] = tile.T
            return carry

        lax.fori_loop(0, width // BLK, one, 0)


def turn(places, flags, t_vals, c_width):
    pieces = t_vals.shape[0] // c_width
    shape = (t_vals.shape[1], c_width)
    return pl.pallas_call(
        functools.partial(turn_kernel, pieces, c_width),
        out_shape=[jax.ShapeDtypeStruct(shape, jnp.bfloat16)] * pieces,
        grid_spec=pltpu.PrefetchScalarGridSpec(
            num_scalar_prefetch=2,
            grid=(1,),
            in_specs=[whole(t_vals.shape)],
            out_specs=[whole(shape)] * pieces,
        ),
        compiler_params=params(),
        cost_estimate=cost(0, 4 * t_vals.size),
    )(places, flags, t_vals)


def body(n_row, n_col, r_vals, s_vals, t_vals, r_pattern, s_pattern, t_pattern):
    side = math.isqrt(n_col)
    row = lax.axis_index("row")
    col = lax.axis_index("col")
    line, kind = row // 2, row % 2
    y, x = col // side, col % side
    a_rows, b_width = r_vals.shape
    c_width = s_vals.shape[1]
    a_part = t_vals.shape[1]
    a_tiles, ap_tiles = a_rows // BLK, a_part // BLK
    along = kind == 0
    gather_at = jnp.where(along, x, y)
    target_at = jnp.where(along, y, x)
    axes = ("row", "col")

    def place(k, h, yy, xx):
        return (k * 2 + h) * n_col + yy * side + xx

    def shifted(e, gather):
        pairs = []
        for k in range(n_row // 2):
            for h in range(2):
                for yy in range(side):
                    for xx in range(side):
                        if (h == 0) == gather:
                            to = (yy, (xx + e) % side)
                        else:
                            to = ((yy + e) % side, xx)
                        pairs.append((place(k, h, yy, xx), place(k, h, *to)))
        return pairs

    r_pieces = [r_vals] + [lax.ppermute(r_vals, axes, shifted(e, True)) for e in range(1, side)]

    same, other = [], []
    for a in range(side):
        for b in range(side):
            for c in range(side):
                for d in range(side):
                    k = a * side + b
                    to_even = (c * side + b, 0, a, d)
                    to_odd = (a * side + d, 1, c, b)
                    same.append((place(k, 0, c, d), place(*to_even)))
                    same.append((place(k, 1, c, d), place(*to_odd)))
                    other.append((place(k, 1, c, d), place(*to_even)))
                    other.append((place(k, 0, c, d), place(*to_odd)))
    s_same = lax.ppermute(s_vals, axes, same)
    s_other = lax.ppermute(s_vals, axes, other)
    s_held = jnp.concatenate(
        [jnp.where(along, s_same, s_other), jnp.where(along, s_other, s_same)], axis=0
    )
    s_pieces = [s_held]
    for d in range(1, n_col):
        pairs = [
            ((k * 2 + h), (((k + d) % n_col) * 2 + h)) for k in range(n_col) for h in range(2)
        ]
        s_pieces.append(lax.ppermute(s_held, "row", pairs))
    spots, blocks, targets = [], [], []
    for t in range(side):
        target = (target_at + t) % side
        for e in range(side):
            g = (gather_at - e) % side
            k = jnp.where(along, target * side + g, g * side + target)
            spots.append((line - k) % n_col)
            blocks.append(jnp.where(along, y * side + g, g * side + x))
        targets.append(jnp.where(along, target * side + x, y * side + target))
    s_eff = order_pieces(
        side, jnp.stack(spots + blocks + targets).astype(jnp.int32), s_pattern, s_pieces
    )

    flat = n_col & (n_col - 1) == 0
    partner = [(col ^ e) if flat else (col + e) % n_col for e in range(n_col)]
    t_flags = lax.dynamic_slice_in_dim(t_pattern, (row * n_col + col) * ap_tiles, ap_tiles, 1)
    turned = turn(jnp.stack(partner).astype(jnp.int32), t_flags, t_vals, c_width)
    held = lax.optimization_barrier((*r_pieces[1:], *turned[1:]))
    r_pieces[1:], sent = held[: side - 1], held[side - 1 :]
    t_pieces = [turned[0]]
    for e in range(1, n_col):
        pairs = [(j, (j ^ e) if flat else (j + e) % n_col) for j in range(n_col)]
        t_pieces.append(lax.ppermute(sent[e - 1], "col", pairs))

    b_tiles = r_pattern.shape[1]
    r_flags = lax.dynamic_slice_in_dim(r_pattern, row * a_tiles, a_tiles, 0)
    table = jnp.concatenate(
        [jnp.stack(blocks[:side] + [jnp.int32(b_tiles)]).astype(jnp.int32), r_flags.reshape(-1)]
    )
    block = max(a_part, math.gcd(a_rows, 4 * BLK))
    steps = a_rows // block
    chunks = 2 if steps % 2 == 0 else 1
    steps //= chunks
    coded = []
    for chunk in range(chunks):
        if chunk:
            held = lax.optimization_barrier((*r_pieces[1:], *t_pieces[1:]))
            r_pieces[1:], t_pieces[1:] = held[: side - 1], held[side - 1 :]
        parts = []
        for e in range(1, side):
            codes = coded_product(table, r_pieces, s_eff, e, block, chunk * steps, steps)
            parts.append(lax.ppermute(codes, axes, shifted(e, False)))
        coded.append(parts)
    order = [(col ^ o) if flat else (col - o) % n_col for o in range(n_col)]
    own, mirror = own_product(
        table, jnp.stack(order).astype(jnp.int32), r_pieces, s_eff, t_pieces, block
    )
    out = None
    for chunk in range(chunks):
        out = join(own, mirror, coded[chunk], block, chunk * steps, steps, out)
    return out


def solution(mesh):
    placed = (P("row", "col"), P("row", "col"), P(None, ("row", "col")), P(), P(), P())
    n_row, n_col = mesh.shape["row"], mesh.shape["col"]
    return jax.shard_map(
        functools.partial(body, n_row, n_col),
        mesh=mesh,
        in_specs=placed,
        out_specs=P("row", "col"),
        check_vma=False,
    )
```

```python
import functools
import math

import jax
import jax.numpy as jnp
from jax import lax
from jax.experimental import pallas as pl
from jax.experimental.pallas import tpu as pltpu
from jax.sharding import PartitionSpec as P

BLK = 128
STRIP = 16
LEVELS = 32767.0
FINE = 64.0
VMEM = 63 * 1024 * 1024


def masked(values, flag):
    return values * jnp.full((1, BLK), flag.astype(jnp.float32)).astype(jnp.bfloat16)


def joined_tiles(grid):
    bands = [jnp.concatenate(t, axis=1) if len(t) > 1 else t[0] for t in grid]
    return jnp.concatenate(bands, axis=0) if len(bands) > 1 else bands[0]


def whole(shape):
    return pl.BlockSpec(shape, lambda i, *_: (0,) * len(shape))


def cost(flops, bytes_accessed):
    return pl.CostEstimate(flops=flops, bytes_accessed=bytes_accessed, transcendentals=0)


def params(limit=VMEM):
    return pltpu.CompilerParams(vmem_limit_bytes=limit)


class Table:
    def __init__(self, ref, pieces, a_tiles, b_all, c_all):
        self.ref, self.pieces = ref, pieces
        self.b_all, self.c_all = b_all, c_all
        self.r_at = 2 * pieces + 1
        self.s_at = self.r_at + a_tiles * b_all

    def block(self, e):
        return self.ref[e]

    def spot(self, e):
        return self.ref[self.pieces + e]

    def target(self):
        return self.ref[2 * self.pieces]

    def r_flag(self, a, b):
        return self.ref[self.r_at + a * self.b_all + b]

    def s_flag(self, b, c):
        return self.ref[self.s_at + b * self.c_all + c]


def take_s(table, s_refs, held):
    width, cols = s_refs[0].shape
    b_tiles, c_tiles = width // BLK, cols // BLK
    for e in range(table.pieces):
        for t in range(b_tiles):
            for u in range(c_tiles):
                flag = table.s_flag(table.block(e) * b_tiles + t, table.target() * c_tiles + u)
                down, over = slice(t * BLK, (t + 1) * BLK), slice(u * BLK, (u + 1) * BLK)
                total = None
                for d, s_ref in enumerate(s_refs):
                    term = masked(s_ref[down, over], jnp.where(table.spot(e) == d, flag, 0))
                    total = term if total is None else total + term
                held[e * width + t * BLK : e * width + (t + 1) * BLK, over] = total


def product(table, first, r_refs, s_refs, held):
    @pl.when(pl.program_id(0) == 0)
    def _():
        take_s(table, s_refs, held)

    rows, width = r_refs[0].shape
    b_tiles = width // BLK
    grid = []
    for t in range(rows // BLK):
        a = (pl.program_id(0) + first) * (rows // BLK) + t
        grid.append(
            [
                masked(
                    r_refs[e][t * BLK : (t + 1) * BLK, u * BLK : (u + 1) * BLK],
                    table.r_flag(a, table.block(e) * b_tiles + u),
                )
                for e in range(table.pieces)
                for u in range(b_tiles)
            ]
        )
    return jnp.dot(joined_tiles(grid), held[...], preferred_element_type=jnp.float32)


def coded_kernel(sizes, first, numbers, *refs):
    *ins, out, held = refs
    pieces = sizes[0]
    total = product(Table(numbers, *sizes), first, ins[:pieces], ins[pieces:], held)
    rows, cols = total.shape
    group = rows // STRIP
    strip_row = lax.broadcasted_iota(jnp.int32, (STRIP, cols), 0)
    strip = jnp.zeros((STRIP, cols), jnp.float32)
    for g in range(STRIP):
        part = total[g * group : (g + 1) * group]
        top = jnp.max(jnp.max(jnp.abs(part), axis=0, keepdims=True), axis=1, keepdims=True)
        level = jnp.ceil(jnp.log2(jnp.maximum(top, 1e-30)) * FINE) + 1.0
        gain = jnp.exp2(level * (-1.0 / FINE)) * LEVELS
        code = jnp.clip(jnp.round(part * gain), -LEVELS, LEVELS)
        out[g * group : (g + 1) * group] = code.astype(jnp.int16)
        strip = jnp.where(strip_row == g, level, strip)
    out[rows:] = strip.astype(jnp.int16)


def coded_product(sizes, table, r_pieces, s_pieces, block, first, steps):
    pieces = len(r_pieces)
    width, cols = s_pieces[0].shape
    return pl.pallas_call(
        functools.partial(coded_kernel, sizes, first),
        out_shape=jax.ShapeDtypeStruct((steps * (block + STRIP), cols), jnp.int16),
        grid_spec=pltpu.PrefetchScalarGridSpec(
            num_scalar_prefetch=1,
            grid=(steps,),
            in_specs=[pl.BlockSpec((block, width), lambda i, *_: (i + first, 0))] * pieces
            + [whole((width, cols))] * len(s_pieces),
            out_specs=pl.BlockSpec((block + STRIP, cols), lambda i, *_: (i, 0)),
            scratch_shapes=[pltpu.VMEM((pieces * width, cols), jnp.bfloat16)],
        ),
        compiler_params=params(),
        cost_estimate=cost(2 * steps * block * pieces * width * cols // 16, 0),
    )(table, *r_pieces, *s_pieces)


def own_kernel(sizes, count, numbers, order, *refs):
    *ins, out, mirror, held = refs
    pieces = sizes[0]
    r_refs, s_refs, t_refs = ins[:pieces], ins[pieces : pieces + count], ins[pieces + count :]
    rows = out.shape[0]
    a_part = t_refs[0].shape[0]
    for j in range(rows // a_part):
        for e, t_ref in enumerate(t_refs):

            @pl.when(order[pl.program_id(0) * (rows // a_part) + j] == e)
            def _(j=j, t_ref=t_ref):
                mirror[j * a_part : (j + 1) * a_part] = t_ref[...]

    out[...] = product(Table(numbers, *sizes), 0, r_refs, s_refs, held)


def own_product(sizes, table, order, r_pieces, s_pieces, t_pieces, block):
    pieces = len(r_pieces)
    a_rows, width = r_pieces[0].shape
    cols = s_pieces[0].shape[1]
    by_step = lambda i, *_: (i, 0)
    return pl.pallas_call(
        functools.partial(own_kernel, sizes, len(s_pieces)),
        out_shape=[pltpu.HBM((a_rows, cols), jnp.float32), pltpu.HBM((a_rows, cols), jnp.bfloat16)],
        grid_spec=pltpu.PrefetchScalarGridSpec(
            num_scalar_prefetch=2,
            grid=(a_rows // block,),
            in_specs=[pl.BlockSpec((block, width), by_step)] * pieces
            + [whole((width, cols))] * len(s_pieces)
            + [whole(t.shape) for t in t_pieces],
            out_specs=[pl.BlockSpec((block, cols), by_step)] * 2,
            scratch_shapes=[pltpu.VMEM((pieces * width, cols), jnp.bfloat16)],
        ),
        compiler_params=params(),
        cost_estimate=cost(2 * a_rows * pieces * width * cols // 16, 0),
    )(table, order, *r_pieces, *s_pieces, *t_pieces)


def join_kernel(parts, own, mirror, *refs):
    gains, out = refs[-1], refs[-2]
    rows = own.shape[0]
    group = rows // STRIP
    for k in range(parts):
        level = refs[k][rows:].astype(jnp.float32)
        gains[k] = jnp.exp2(level * (1.0 / FINE)) * (1.0 / LEVELS)

    def one(g, carry):
        at = pl.ds(pl.multiple_of(g * group, group), group)
        total = own[at]
        for k in range(parts):
            total += refs[k][at].astype(jnp.float32) * gains[k, pl.ds(g, 1)]
        out[at] = (total * mirror[at].astype(jnp.float32)).astype(jnp.bfloat16)
        return carry

    lax.fori_loop(0, STRIP, one, 0)


def join(own, mirror, coded, block, first, steps, before):
    rows, cols = own.shape
    here = pl.BlockSpec((block, cols), lambda i: (i + first, 0))
    aliases, carried = {}, ()
    if before is not None:
        aliases, carried = {2 + len(coded): 0}, (before,)
    return pl.pallas_call(
        functools.partial(join_kernel, len(coded)),
        out_shape=jax.ShapeDtypeStruct((rows, cols), jnp.bfloat16),
        grid=(steps,),
        in_specs=[here, here]
        + [pl.BlockSpec((block + STRIP, cols), lambda i: (i, 0))] * len(coded)
        + [pl.BlockSpec(memory_space=pl.ANY)] * len(carried),
        out_specs=here,
        scratch_shapes=[pltpu.VMEM((len(coded), STRIP, cols), jnp.float32)],
        input_output_aliases=aliases,
        compiler_params=params(48 * 1024 * 1024),
        cost_estimate=cost(0, 0),
    )(own, mirror, *coded, *carried)


def turn_kernel(pieces, width, places, flags, t_ref, *outs):
    a_width = t_ref.shape[1]
    for e in range(pieces):

        def one(t, carry, e=e):
            start = pl.multiple_of(places[e] * width + t * BLK, BLK)
            over = pl.ds(pl.multiple_of(t * BLK, BLK), BLK)
            for u in range(a_width // BLK):
                tile = masked(
                    t_ref[pl.ds(start, BLK), u * BLK : (u + 1) * BLK],
                    flags[places[e] * (width // BLK) + t, u],
                )
                outs[e][u * BLK : (u + 1) * BLK, over] = tile.T
            return carry

        lax.fori_loop(0, width // BLK, one, 0)


def turn(places, flags, t_vals, c_width):
    pieces = t_vals.shape[0] // c_width
    shape = (t_vals.shape[1], c_width)
    return pl.pallas_call(
        functools.partial(turn_kernel, pieces, c_width),
        out_shape=[jax.ShapeDtypeStruct(shape, jnp.bfloat16)] * pieces,
        grid_spec=pltpu.PrefetchScalarGridSpec(
            num_scalar_prefetch=2,
            grid=(1,),
            in_specs=[whole(t_vals.shape)],
            out_specs=[whole(shape)] * pieces,
        ),
        compiler_params=params(),
        cost_estimate=cost(0, 4 * t_vals.size),
    )(places, flags, t_vals)


def body(n_row, n_col, r_vals, s_vals, t_vals, r_pattern, s_pattern, t_pattern):
    side = math.isqrt(n_col)
    row = lax.axis_index("row")
    col = lax.axis_index("col")
    line, kind = row // 2, row % 2
    y, x = col // side, col % side
    a_rows, b_width = r_vals.shape
    c_width = s_vals.shape[1]
    a_part = t_vals.shape[1]
    a_tiles, ap_tiles = a_rows // BLK, a_part // BLK
    along = kind == 0
    gather_at = jnp.where(along, x, y)
    target_at = jnp.where(along, y, x)
    axes = ("row", "col")

    def place(k, h, yy, xx):
        return (k * 2 + h) * n_col + yy * side + xx

    def shifted(e, gather):
        pairs = []
        for k in range(n_row // 2):
            for h in range(2):
                for yy in range(side):
                    for xx in range(side):
                        if (h == 0) == gather:
                            to = (yy, (xx + e) % side)
                        else:
                            to = ((yy + e) % side, xx)
                        pairs.append((place(k, h, yy, xx), place(k, h, *to)))
        return pairs

    r_pieces = [r_vals] + [lax.ppermute(r_vals, axes, shifted(e, True)) for e in range(1, side)]

    same, other = [], []
    for a in range(side):
        for b in range(side):
            for c in range(side):
                for d in range(side):
                    k = a * side + b
                    to_even = (c * side + b, 0, a, d)
                    to_odd = (a * side + d, 1, c, b)
                    same.append((place(k, 0, c, d), place(*to_even)))
                    same.append((place(k, 1, c, d), place(*to_odd)))
                    other.append((place(k, 1, c, d), place(*to_even)))
                    other.append((place(k, 0, c, d), place(*to_odd)))
    s_same = lax.ppermute(s_vals, axes, same)
    s_other = lax.ppermute(s_vals, axes, other)
    s_held = jnp.concatenate(
        [jnp.where(along, s_same, s_other), jnp.where(along, s_other, s_same)], axis=0
    )
    s_pieces = [s_held]
    for d in range(1, n_col):
        pairs = [
            ((k * 2 + h), (((k + d) % n_col) * 2 + h)) for k in range(n_col) for h in range(2)
        ]
        s_pieces.append(lax.ppermute(s_held, "row", pairs))
    flat = n_col & (n_col - 1) == 0
    partner = [(col ^ e) if flat else (col + e) % n_col for e in range(n_col)]
    t_flags = lax.dynamic_slice_in_dim(t_pattern, (row * n_col + col) * ap_tiles, ap_tiles, 1)
    turned = turn(jnp.stack(partner).astype(jnp.int32), t_flags, t_vals, c_width)
    held = lax.optimization_barrier((*r_pieces[1:], *turned[1:]))
    r_pieces[1:], sent = held[: side - 1], held[side - 1 :]
    t_pieces = [turned[0]]
    for e in range(1, n_col):
        pairs = [(j, (j ^ e) if flat else (j + e) % n_col) for j in range(n_col)]
        t_pieces.append(lax.ppermute(sent[e - 1], "col", pairs))

    r_flags = lax.dynamic_slice_in_dim(r_pattern, row * a_tiles, a_tiles, 0)
    flags = [r_flags.reshape(-1), s_pattern.reshape(-1)]
    sizes = (side, a_tiles, r_pattern.shape[1], s_pattern.shape[1])

    def table(target):
        spots, blocks = [], []
        for e in range(side):
            g = (gather_at - e) % side
            k = jnp.where(along, target * side + g, g * side + target)
            spots.append((line - k) % n_col)
            blocks.append(jnp.where(along, y * side + g, g * side + x))
        to = jnp.where(along, target * side + x, y * side + target)
        return jnp.concatenate([jnp.stack(blocks + spots + [to]).astype(jnp.int32), *flags])

    block = max(a_part, math.gcd(a_rows, 4 * BLK))
    steps = a_rows // block
    chunks = 2 if steps % 2 == 0 else 1
    steps //= chunks
    coded = []
    for chunk in range(chunks):
        if chunk:
            held = lax.optimization_barrier((*r_pieces[1:], *t_pieces[1:]))
            r_pieces[1:], t_pieces[1:] = held[: side - 1], held[side - 1 :]
        parts = []
        for e in range(1, side):
            codes = coded_product(
                sizes, table((target_at + e) % side), r_pieces, s_pieces,
                block, chunk * steps, steps,
            )
            parts.append(lax.ppermute(codes, axes, shifted(e, False)))
        coded.append(parts)
    order = [(col ^ o) if flat else (col - o) % n_col for o in range(n_col)]
    own, mirror = own_product(
        sizes, table(target_at), jnp.stack(order).astype(jnp.int32),
        r_pieces, s_pieces, t_pieces, block,
    )
    own, mirror = (pltpu.with_memory_space_constraint(v, pltpu.HBM) for v in (own, mirror))
    out = None
    for chunk in range(chunks):
        out = join(own, mirror, coded[chunk], block, chunk * steps, steps, out)
    return out


def solution(mesh):
    placed = (P("row", "col"), P("row", "col"), P(None, ("row", "col")), P(), P(), P())
    n_row, n_col = mesh.shape["row"], mesh.shape["col"]
    return jax.shard_map(
        functools.partial(body, n_row, n_col),
        mesh=mesh,
        in_specs=placed,
        out_specs=P("row", "col"),
        check_vma=False,
    )
```

```python
import functools
import math

import jax
import jax.numpy as jnp
from jax import lax
from jax.experimental import pallas as pl
from jax.experimental.pallas import tpu as pltpu
from jax.sharding import PartitionSpec as P

BLK = 128
STRIP = 16
LEVELS = 32767.0
FINE = 64.0
VMEM = 24 * 1024 * 1024


def masked(values, flag):
    return values * jnp.full((1, BLK), flag.astype(jnp.float32)).astype(jnp.bfloat16)


def joined_tiles(grid):
    bands = [jnp.concatenate(t, axis=1) if len(t) > 1 else t[0] for t in grid]
    return jnp.concatenate(bands, axis=0) if len(bands) > 1 else bands[0]


def whole(shape):
    return pl.BlockSpec(shape, lambda i, *_: (0,) * len(shape))


def cost(flops, bytes_accessed):
    return pl.CostEstimate(flops=flops, bytes_accessed=bytes_accessed, transcendentals=0)


def params(limit=VMEM):
    return pltpu.CompilerParams(vmem_limit_bytes=limit)


class Table:
    def __init__(self, ref, pieces, a_tiles, b_all, c_all):
        self.ref, self.pieces = ref, pieces
        self.b_all, self.c_all = b_all, c_all
        self.r_at = pieces * (pieces + 2)
        self.s_at = self.r_at + a_tiles * b_all

    def block(self, e):
        return self.ref[e]

    def spot(self, target, e):
        return self.ref[(target + 1) * self.pieces + e]

    def column(self, target):
        return self.ref[(self.pieces + 1) * self.pieces + target]

    def r_flag(self, a, b):
        return self.ref[self.r_at + a * self.b_all + b]

    def s_flag(self, b, c):
        return self.ref[self.s_at + b * self.c_all + c]


def select_copy(choice, sources, target, sem):
    for d, source in enumerate(sources):

        @pl.when(choice == d)
        def _(source=source):
            pltpu.make_async_copy(source, target, sem).start()

    return pltpu.make_async_copy(sources[0], target, sem)


def products(table, target, first, r_refs, s_refs, r_buf, s_buf, r_sem, s_sem, use):
    pieces, blocks, block, width = r_buf.shape
    cols = s_buf.shape[1]
    b_tiles, c_tiles = width // BLK, cols // BLK

    def r_copy(e, n):
        rows = pl.ds(pl.multiple_of(first + n * block, block), block)
        return pltpu.make_async_copy(r_refs[e].at[rows], r_buf.at[e, n], r_sem.at[e, n])

    waits = [
        select_copy(table.spot(target, e), s_refs, s_buf.at[pl.ds(e * width, width)], s_sem.at[e])
        for e in range(pieces)
    ]
    for n in range(blocks):
        for e in range(pieces):
            r_copy(e, n).start()
    for e in range(pieces):
        waits[e].wait()
        for t in range(b_tiles):
            for u in range(c_tiles):
                flag = table.s_flag(table.block(e) * b_tiles + t, table.column(target) * c_tiles + u)
                down = slice(e * width + t * BLK, e * width + (t + 1) * BLK)
                over = slice(u * BLK, (u + 1) * BLK)
                s_buf[down, over] = masked(s_buf[down, over], flag)

    def one(n, carry):
        for e in range(pieces):
            r_copy(e, n).wait()
        grid = []
        for t in range(block // BLK):
            a = first // BLK + n * (block // BLK) + t
            grid.append(
                [
                    masked(
                        r_buf[e, n, t * BLK : (t + 1) * BLK, u * BLK : (u + 1) * BLK],
                        table.r_flag(a, table.block(e) * b_tiles + u),
                    )
                    for e in range(pieces)
                    for u in range(b_tiles)
                ]
            )
        use(n, jnp.dot(joined_tiles(grid), s_buf[...], preferred_element_type=jnp.float32))
        return carry

    lax.fori_loop(0, blocks, one, 0)


def encode(total, out):
    rows, cols = total.shape
    group = rows // STRIP
    strip_row = lax.broadcasted_iota(jnp.int32, (STRIP, cols), 0)
    strip = jnp.zeros((STRIP, cols), jnp.float32)
    for g in range(STRIP):
        part = total[g * group : (g + 1) * group]
        top = jnp.max(jnp.max(jnp.abs(part), axis=0, keepdims=True), axis=1, keepdims=True)
        level = jnp.ceil(jnp.log2(jnp.maximum(top, 1e-30)) * FINE) + 1.0
        gain = jnp.exp2(level * (-1.0 / FINE)) * LEVELS
        code = jnp.clip(jnp.round(part * gain), -LEVELS, LEVELS)
        out[g * group : (g + 1) * group] = code.astype(jnp.int16)
        strip = jnp.where(strip_row == g, level, strip)
    out[rows:] = strip.astype(jnp.int16)


def product_kernel(sizes, target, first, coded, numbers, *refs):
    *ins, out, r_buf, s_buf, o_buf, r_sem, s_sem, o_sem = refs
    pieces, blocks = r_buf.shape[:2]

    def o_copy(n):
        return pltpu.make_async_copy(o_buf.at[n], out.at[n], o_sem.at[n])

    def use(n, total):
        if coded:
            encode(total, o_buf.at[n])
        else:
            o_buf[n] = total
        o_copy(n).start()

    products(
        Table(numbers, *sizes), target, first, ins[:pieces], ins[pieces:],
        r_buf, s_buf, r_sem, s_sem, use,
    )
    for n in range(blocks):
        o_copy(n).wait()


def product(sizes, table, r_pieces, s_pieces, target, block, first, blocks, coded):
    pieces = len(r_pieces)
    width, cols = s_pieces[0].shape
    dtype = jnp.int16 if coded else jnp.float32
    shape = (blocks, block + (STRIP if coded else 0), cols)
    return pl.pallas_call(
        functools.partial(product_kernel, sizes, target, first, coded),
        out_shape=jax.ShapeDtypeStruct(shape, dtype),
        grid_spec=pltpu.PrefetchScalarGridSpec(
            num_scalar_prefetch=1,
            grid=(1,),
            in_specs=[pl.BlockSpec(memory_space=pl.ANY)] * (pieces + len(s_pieces)),
            out_specs=pl.BlockSpec(memory_space=pl.ANY),
            scratch_shapes=[
                pltpu.VMEM((pieces, blocks, block, width), jnp.bfloat16),
                pltpu.VMEM((pieces * width, cols), jnp.bfloat16),
                pltpu.VMEM(shape, dtype),
                pltpu.SemaphoreType.DMA((pieces, blocks)),
                pltpu.SemaphoreType.DMA((pieces,)),
                pltpu.SemaphoreType.DMA((blocks,)),
            ],
        ),
        compiler_params=params(),
        cost_estimate=cost(2 * blocks * block * pieces * width * cols // 16, 0),
    )(table, *r_pieces, *s_pieces)


def join_kernel(parts, pieces, first, order, own, *refs):
    codes, t_refs = refs[:parts], refs[parts : parts + pieces]
    out, own_buf, code_buf, t_buf, o_buf, gains, own_sem, code_sem, t_sem, o_sem = refs[-10:]
    blocks, block, cols = own_buf.shape
    split = t_sem.shape[1]
    a_part = block // split
    group = block // STRIP
    waits = []
    for n in range(blocks):
        copies = [pltpu.make_async_copy(own.at[first + n], own_buf.at[n], own_sem.at[n])]
        for k in range(parts):
            copies.append(
                pltpu.make_async_copy(codes[k].at[n], code_buf.at[k, n], code_sem.at[k, n])
            )
        for copy in copies:
            copy.start()
        for j in range(split):
            copies.append(
                select_copy(
                    order[(first + n) * split + j], t_refs,
                    t_buf.at[n, pl.ds(j * a_part, a_part)], t_sem.at[n, j],
                )
            )
        waits.append(copies)
    outs = []
    for n in range(blocks):
        for copy in waits[n]:
            copy.wait()
        for k in range(parts):
            level = code_buf[k, n, block:].astype(jnp.float32)
            gains[k] = jnp.exp2(level * (1.0 / FINE)) * (1.0 / LEVELS)
        for g in range(STRIP):
            at = slice(g * group, (g + 1) * group)
            total = own_buf[n, at]
            for k in range(parts):
                total += code_buf[k, n, at].astype(jnp.float32) * gains[k, g : g + 1]
            o_buf[n, at] = (total * t_buf[n, at].astype(jnp.float32)).astype(jnp.bfloat16)
        rows = pl.ds((first + n) * block, block)
        outs.append(pltpu.make_async_copy(o_buf.at[n], out.at[rows], o_sem.at[n]))
        outs[-1].start()
    for copy in outs:
        copy.wait()


def join(order, own, coded, t_pieces, first, blocks, before):
    steps, block, cols = own.shape
    parts, pieces = len(coded), len(t_pieces)
    split = block // t_pieces[0].shape[0]
    aliases, carried = {}, ()
    if before is not None:
        aliases, carried = {2 + parts + pieces: 0}, (before,)
    return pl.pallas_call(
        functools.partial(join_kernel, parts, pieces, first),
        out_shape=jax.ShapeDtypeStruct((steps * block, cols), jnp.bfloat16),
        grid_spec=pltpu.PrefetchScalarGridSpec(
            num_scalar_prefetch=1,
            grid=(1,),
            in_specs=[pl.BlockSpec(memory_space=pl.ANY)] * (1 + parts + pieces + len(carried)),
            out_specs=pl.BlockSpec(memory_space=pl.ANY),
            scratch_shapes=[
                pltpu.VMEM((blocks, block, cols), jnp.float32),
                pltpu.VMEM((parts, blocks, block + STRIP, cols), jnp.int16),
                pltpu.VMEM((blocks, block, cols), jnp.bfloat16),
                pltpu.VMEM((blocks, block, cols), jnp.bfloat16),
                pltpu.VMEM((parts, STRIP, cols), jnp.float32),
                pltpu.SemaphoreType.DMA((blocks,)),
                pltpu.SemaphoreType.DMA((parts, blocks)),
                pltpu.SemaphoreType.DMA((blocks, split)),
                pltpu.SemaphoreType.DMA((blocks,)),
            ],
        ),
        input_output_aliases=aliases,
        compiler_params=params(),
        cost_estimate=cost(0, 0),
    )(order, own, *coded, *t_pieces, *carried)


def turn_kernel(pieces, width, places, flags, t_ref, *outs):
    a_width = t_ref.shape[1]
    for e in range(pieces):

        def one(t, carry, e=e):
            start = pl.multiple_of(places[e] * width + t * BLK, BLK)
            over = pl.ds(pl.multiple_of(t * BLK, BLK), BLK)
            for u in range(a_width // BLK):
                tile = masked(
                    t_ref[pl.ds(start, BLK), u * BLK : (u + 1) * BLK],
                    flags[places[e] * (width // BLK) + t, u],
                )
                outs[e][u * BLK : (u + 1) * BLK, over] = tile.T
            return carry

        lax.fori_loop(0, width // BLK, one, 0)


def turn(places, flags, t_vals, c_width):
    pieces = t_vals.shape[0] // c_width
    shape = (t_vals.shape[1], c_width)
    return pl.pallas_call(
        functools.partial(turn_kernel, pieces, c_width),
        out_shape=[jax.ShapeDtypeStruct(shape, jnp.bfloat16)] * pieces,
        grid_spec=pltpu.PrefetchScalarGridSpec(
            num_scalar_prefetch=2,
            grid=(1,),
            in_specs=[whole(t_vals.shape)],
            out_specs=[whole(shape)] * pieces,
        ),
        compiler_params=params(),
        cost_estimate=cost(0, 4 * t_vals.size),
    )(places, flags, t_vals)


def body(n_row, n_col, r_vals, s_vals, t_vals, r_pattern, s_pattern, t_pattern):
    side = math.isqrt(n_col)
    row = lax.axis_index("row")
    col = lax.axis_index("col")
    line, kind = row // 2, row % 2
    y, x = col // side, col % side
    a_rows, b_width = r_vals.shape
    c_width = s_vals.shape[1]
    a_part = t_vals.shape[1]
    a_tiles, ap_tiles = a_rows // BLK, a_part // BLK
    along = kind == 0
    gather_at = jnp.where(along, x, y)
    target_at = jnp.where(along, y, x)
    axes = ("row", "col")

    def place(k, h, yy, xx):
        return (k * 2 + h) * n_col + yy * side + xx

    def shifted(e, gather):
        pairs = []
        for k in range(n_row // 2):
            for h in range(2):
                for yy in range(side):
                    for xx in range(side):
                        if (h == 0) == gather:
                            to = (yy, (xx + e) % side)
                        else:
                            to = ((yy + e) % side, xx)
                        pairs.append((place(k, h, yy, xx), place(k, h, *to)))
        return pairs

    r_pieces = [r_vals] + [lax.ppermute(r_vals, axes, shifted(e, True)) for e in range(1, side)]

    same, other = [], []
    for a in range(side):
        for b in range(side):
            for c in range(side):
                for d in range(side):
                    k = a * side + b
                    to_even = (c * side + b, 0, a, d)
                    to_odd = (a * side + d, 1, c, b)
                    same.append((place(k, 0, c, d), place(*to_even)))
                    same.append((place(k, 1, c, d), place(*to_odd)))
                    other.append((place(k, 1, c, d), place(*to_even)))
                    other.append((place(k, 0, c, d), place(*to_odd)))
    s_same = lax.ppermute(s_vals, axes, same)
    s_other = lax.ppermute(s_vals, axes, other)
    s_held = jnp.concatenate(
        [jnp.where(along, s_same, s_other), jnp.where(along, s_other, s_same)], axis=0
    )
    s_pieces = [s_held]
    for d in range(1, n_col):
        pairs = [
            ((k * 2 + h), (((k + d) % n_col) * 2 + h)) for k in range(n_col) for h in range(2)
        ]
        s_pieces.append(lax.ppermute(s_held, "row", pairs))
    flat = n_col & (n_col - 1) == 0
    partner = [(col ^ e) if flat else (col + e) % n_col for e in range(n_col)]
    t_flags = lax.dynamic_slice_in_dim(t_pattern, (row * n_col + col) * ap_tiles, ap_tiles, 1)
    turned = turn(jnp.stack(partner).astype(jnp.int32), t_flags, t_vals, c_width)
    held = lax.optimization_barrier((*r_pieces[1:], *turned[1:]))
    r_pieces[1:], sent = held[: side - 1], held[side - 1 :]
    t_pieces = [turned[0]]
    for e in range(1, n_col):
        pairs = [(j, (j ^ e) if flat else (j + e) % n_col) for j in range(n_col)]
        t_pieces.append(lax.ppermute(sent[e - 1], "col", pairs))

    r_flags = lax.dynamic_slice_in_dim(r_pattern, row * a_tiles, a_tiles, 0)
    flags = [r_flags.reshape(-1), s_pattern.reshape(-1)]
    sizes = (side, a_tiles, r_pattern.shape[1], s_pattern.shape[1])

    blocks, spots, targets = [], [], []
    for e in range(side):
        g = (gather_at - e) % side
        blocks.append(jnp.where(along, y * side + g, g * side + x))
    for t in range(side):
        target = (target_at + t) % side
        for e in range(side):
            g = (gather_at - e) % side
            k = jnp.where(along, target * side + g, g * side + target)
            spots.append((line - k) % n_col)
        targets.append(jnp.where(along, target * side + x, y * side + target))
    table = jnp.concatenate([jnp.stack(blocks + spots + targets).astype(jnp.int32), *flags])

    block = max(a_part, math.gcd(a_rows, 4 * BLK))
    steps = a_rows // block
    chunks = 2 if steps % 2 == 0 else 1
    steps //= chunks
    coded = []
    for chunk in range(chunks):
        parts = []
        for e in range(1, side):
            codes = product(
                sizes, table, r_pieces, s_pieces, e, block, chunk * steps * block, steps, True
            )
            if chunk:
                codes, *t_pieces[1:] = lax.optimization_barrier((codes, *t_pieces[1:]))
            parts.append(lax.ppermute(codes, axes, shifted(e, False)))
        coded.append(parts)
    own = product(sizes, table, r_pieces, s_pieces, 0, block, 0, steps * chunks, False)
    order = [(col ^ o) if flat else (col - o) % n_col for o in range(n_col)]
    order = jnp.stack(order).astype(jnp.int32)
    out = None
    for chunk in range(chunks):
        out = join(order, own, coded[chunk], t_pieces, chunk * steps, steps, out)
    return out


def solution(mesh):
    placed = (P("row", "col"), P("row", "col"), P(None, ("row", "col")), P(), P(), P())
    n_row, n_col = mesh.shape["row"], mesh.shape["col"]
    return jax.shard_map(
        functools.partial(body, n_row, n_col),
        mesh=mesh,
        in_specs=placed,
        out_specs=P("row", "col"),
        check_vma=False,
    )
```

```python
import functools
import math

import jax
import jax.numpy as jnp
from jax import lax
from jax.experimental import pallas as pl
from jax.experimental.pallas import tpu as pltpu
from jax.sharding import PartitionSpec as P

BLK = 128
STRIP = 16
LEVELS = 32767.0
FINE = 64.0
VMEM = 24 * 1024 * 1024


def masked(values, flag):
    return values * jnp.full((1, BLK), flag.astype(jnp.float32)).astype(jnp.bfloat16)


def joined_tiles(grid):
    bands = [jnp.concatenate(t, axis=1) if len(t) > 1 else t[0] for t in grid]
    return jnp.concatenate(bands, axis=0) if len(bands) > 1 else bands[0]


def whole(shape):
    return pl.BlockSpec(shape, lambda i, *_: (0,) * len(shape))


def cost(flops, bytes_accessed):
    return pl.CostEstimate(flops=flops, bytes_accessed=bytes_accessed, transcendentals=0)


def params(limit=VMEM):
    return pltpu.CompilerParams(vmem_limit_bytes=limit)


class Table:
    def __init__(self, ref, pieces, a_tiles, b_all, c_all):
        self.ref, self.pieces = ref, pieces
        self.b_all, self.c_all = b_all, c_all
        self.r_at = pieces * (pieces + 2)
        self.s_at = self.r_at + a_tiles * b_all

    def block(self, e):
        return self.ref[e]

    def spot(self, target, e):
        return self.ref[(target + 1) * self.pieces + e]

    def column(self, target):
        return self.ref[(self.pieces + 1) * self.pieces + target]

    def r_flag(self, a, b):
        return self.ref[self.r_at + a * self.b_all + b]

    def s_flag(self, b, c):
        return self.ref[self.s_at + b * self.c_all + c]


def select_copy(choice, sources, target, sem):
    for d, source in enumerate(sources):

        @pl.when(choice == d)
        def _(source=source):
            pltpu.make_async_copy(source, target, sem).start()

    return pltpu.make_async_copy(sources[0], target, sem)


def products(table, target, first, r_refs, s_refs, r_buf, s_buf, r_sem, s_sem, use):
    pieces, blocks, block, width = r_buf.shape
    cols = s_buf.shape[1]
    b_tiles, c_tiles = width // BLK, cols // BLK

    def r_copy(e, n):
        rows = pl.ds(pl.multiple_of(first + n * block, block), block)
        return pltpu.make_async_copy(r_refs[e].at[rows], r_buf.at[e, n], r_sem.at[e, n])

    waits = [
        select_copy(table.spot(target, e), s_refs, s_buf.at[pl.ds(e * width, width)], s_sem.at[e])
        for e in range(pieces)
    ]
    for n in range(blocks):
        for e in range(pieces):
            r_copy(e, n).start()
    for e in range(pieces):
        waits[e].wait()
        for t in range(b_tiles):
            for u in range(c_tiles):
                flag = table.s_flag(table.block(e) * b_tiles + t, table.column(target) * c_tiles + u)
                down = slice(e * width + t * BLK, e * width + (t + 1) * BLK)
                over = slice(u * BLK, (u + 1) * BLK)
                s_buf[down, over] = masked(s_buf[down, over], flag)

    def one(n, carry):
        for e in range(pieces):
            r_copy(e, n).wait()
        grid = []
        for t in range(block // BLK):
            a = first // BLK + n * (block // BLK) + t
            grid.append(
                [
                    masked(
                        r_buf[e, n, t * BLK : (t + 1) * BLK, u * BLK : (u + 1) * BLK],
                        table.r_flag(a, table.block(e) * b_tiles + u),
                    )
                    for e in range(pieces)
                    for u in range(b_tiles)
                ]
            )
        use(n, jnp.dot(joined_tiles(grid), s_buf[...], preferred_element_type=jnp.float32))
        return carry

    lax.fori_loop(0, blocks, one, 0)


def encode(total, out):
    rows, cols = total.shape
    group = rows // STRIP
    strip_row = lax.broadcasted_iota(jnp.int32, (STRIP, cols), 0)
    strip = jnp.zeros((STRIP, cols), jnp.float32)
    for g in range(STRIP):
        part = total[g * group : (g + 1) * group]
        top = jnp.max(jnp.max(jnp.abs(part), axis=0, keepdims=True), axis=1, keepdims=True)
        level = jnp.ceil(jnp.log2(jnp.maximum(top, 1e-30)) * FINE) + 1.0
        gain = jnp.exp2(level * (-1.0 / FINE)) * LEVELS
        code = jnp.clip(jnp.round(part * gain), -LEVELS, LEVELS)
        out[g * group : (g + 1) * group] = code.astype(jnp.int16)
        strip = jnp.where(strip_row == g, level, strip)
    out[rows:] = strip.astype(jnp.int16)


def coded_kernel(sizes, target, first, numbers, *refs):
    *ins, out, r_buf, s_buf, r_sem, s_sem = refs
    pieces = r_buf.shape[0]

    def use(n, total):
        encode(total, out.at[n])

    products(
        Table(numbers, *sizes), target, first, ins[:pieces], ins[pieces:],
        r_buf, s_buf, r_sem, s_sem, use,
    )


def own_kernel(sizes, count, numbers, order, *refs):
    *ins, out, mirror, r_buf, s_buf, r_sem, s_sem, t_sem = refs
    pieces = r_buf.shape[0]
    t_refs = ins[pieces + count :]
    blocks, block, _ = mirror.shape
    a_part = t_refs[0].shape[0]
    split = block // a_part
    waits = []
    for o in range(blocks * split):
        rows = pl.ds(o % split * a_part, a_part)
        waits.append(select_copy(order[o], t_refs, mirror.at[o // split, rows], t_sem.at[o]))

    def use(n, total):
        out[n] = total

    products(
        Table(numbers, *sizes), 0, 0, ins[:pieces], ins[pieces : pieces + count],
        r_buf, s_buf, r_sem, s_sem, use,
    )
    for wait in waits:
        wait.wait()


SCALARS = pl.BlockSpec(memory_space=pltpu.SMEM)
ANYWHERE = pl.BlockSpec(memory_space=pl.ANY)
INSIDE = pl.BlockSpec(memory_space=pltpu.VMEM)


def product_scratch(pieces, blocks, block, width, cols):
    return [
        pltpu.VMEM((pieces, blocks, block, width), jnp.bfloat16),
        pltpu.VMEM((pieces * width, cols), jnp.bfloat16),
        pltpu.SemaphoreType.DMA((pieces, blocks)),
        pltpu.SemaphoreType.DMA((pieces,)),
    ]


def coded_product(sizes, table, r_pieces, s_pieces, target, block, first, blocks):
    pieces = len(r_pieces)
    width, cols = s_pieces[0].shape
    return pl.pallas_call(
        functools.partial(coded_kernel, sizes, target, first),
        out_shape=pltpu.VMEM((blocks, block + STRIP, cols), jnp.int16),
        in_specs=[SCALARS] + [ANYWHERE] * (pieces + len(s_pieces)),
        out_specs=INSIDE,
        scratch_shapes=product_scratch(pieces, blocks, block, width, cols),
        compiler_params=params(),
        cost_estimate=cost(2 * blocks * block * pieces * width * cols // 16, 0),
    )(table, *r_pieces, *s_pieces)


def own_product(sizes, table, order, r_pieces, s_pieces, t_pieces, block):
    pieces = len(r_pieces)
    width, cols = s_pieces[0].shape
    blocks = r_pieces[0].shape[0] // block
    return pl.pallas_call(
        functools.partial(own_kernel, sizes, len(s_pieces)),
        out_shape=[
            pltpu.VMEM((blocks, block, cols), jnp.float32),
            pltpu.VMEM((blocks, block, cols), jnp.bfloat16),
        ],
        in_specs=[SCALARS] * 2 + [ANYWHERE] * (pieces + len(s_pieces) + len(t_pieces)),
        out_specs=[INSIDE] * 2,
        scratch_shapes=product_scratch(pieces, blocks, block, width, cols)
        + [pltpu.SemaphoreType.DMA((len(t_pieces),))],
        compiler_params=params(),
        cost_estimate=cost(2 * blocks * block * pieces * width * cols // 16, 0),
    )(table, order, *r_pieces, *s_pieces, *t_pieces)


def join_kernel(parts, first, own, mirror, *refs):
    codes = refs[:parts]
    out, o_buf, gains, o_sem = refs[-4:]
    blocks, block, cols = o_buf.shape
    group = block // STRIP
    outs = []
    for n in range(blocks):
        for k in range(parts):
            level = codes[k][n, block:].astype(jnp.float32)
            gains[k] = jnp.exp2(level * (1.0 / FINE)) * (1.0 / LEVELS)
        for half in range(2):
            for g in range(half * STRIP // 2, (half + 1) * STRIP // 2):
                at = slice(g * group, (g + 1) * group)
                total = own[first + n, at]
                for k in range(parts):
                    total += codes[k][n, at].astype(jnp.float32) * gains[k, g : g + 1]
                factor = mirror[first + n, at].astype(jnp.float32)
                o_buf[n, at] = (total * factor).astype(jnp.bfloat16)
            here = pl.ds(half * block // 2, block // 2)
            rows = pl.ds((first + n) * block + half * block // 2, block // 2)
            outs.append(
                pltpu.make_async_copy(o_buf.at[n, here], out.at[rows], o_sem.at[n, half])
            )
            outs[-1].start()
    for copy in outs:
        copy.wait()


def in_vmem(values):
    return pltpu.with_memory_space_constraint(values, pltpu.VMEM)


def join(own, mirror, coded, first, before):
    steps, block, cols = own.shape
    blocks = coded[0].shape[0]
    aliases, carried = {}, ()
    if before is not None:
        aliases, carried = {2 + len(coded): 0}, (before,)
    return pl.pallas_call(
        functools.partial(join_kernel, len(coded), first),
        out_shape=jax.ShapeDtypeStruct((steps * block, cols), jnp.bfloat16),
        in_specs=[INSIDE] * (2 + len(coded)) + [ANYWHERE] * len(carried),
        out_specs=ANYWHERE,
        scratch_shapes=[
            pltpu.VMEM((blocks, block, cols), jnp.bfloat16),
            pltpu.VMEM((len(coded), STRIP, cols), jnp.float32),
            pltpu.SemaphoreType.DMA((blocks, 2)),
        ],
        input_output_aliases=aliases,
        compiler_params=params(),
        cost_estimate=cost(0, 0),
    )(own, mirror, *[in_vmem(codes) for codes in coded], *carried)


def turn_kernel(pieces, width, places, flags, t_ref, *outs):
    a_width = t_ref.shape[1]
    for e in range(pieces):

        def one(t, carry, e=e):
            start = pl.multiple_of(places[e] * width + t * BLK, BLK)
            over = pl.ds(pl.multiple_of(t * BLK, BLK), BLK)
            for u in range(a_width // BLK):
                tile = masked(
                    t_ref[pl.ds(start, BLK), u * BLK : (u + 1) * BLK],
                    flags[places[e] * (width // BLK) + t, u],
                )
                outs[e][u * BLK : (u + 1) * BLK, over] = tile.T
            return carry

        lax.fori_loop(0, width // BLK, one, 0)


def turn(places, flags, t_vals, c_width):
    pieces = t_vals.shape[0] // c_width
    shape = (t_vals.shape[1], c_width)
    return pl.pallas_call(
        functools.partial(turn_kernel, pieces, c_width),
        out_shape=[jax.ShapeDtypeStruct(shape, jnp.bfloat16)] * pieces,
        grid_spec=pltpu.PrefetchScalarGridSpec(
            num_scalar_prefetch=2,
            grid=(1,),
            in_specs=[whole(t_vals.shape)],
            out_specs=[whole(shape)] * pieces,
        ),
        compiler_params=params(),
        cost_estimate=cost(0, 4 * t_vals.size),
    )(places, flags, t_vals)


def body(n_row, n_col, r_vals, s_vals, t_vals, r_pattern, s_pattern, t_pattern):
    side = math.isqrt(n_col)
    row = lax.axis_index("row")
    col = lax.axis_index("col")
    line, kind = row // 2, row % 2
    y, x = col // side, col % side
    a_rows, b_width = r_vals.shape
    c_width = s_vals.shape[1]
    a_part = t_vals.shape[1]
    a_tiles, ap_tiles = a_rows // BLK, a_part // BLK
    along = kind == 0
    gather_at = jnp.where(along, x, y)
    target_at = jnp.where(along, y, x)
    axes = ("row", "col")

    def place(k, h, yy, xx):
        return (k * 2 + h) * n_col + yy * side + xx

    def shifted(e, gather):
        pairs = []
        for k in range(n_row // 2):
            for h in range(2):
                for yy in range(side):
                    for xx in range(side):
                        if (h == 0) == gather:
                            to = (yy, (xx + e) % side)
                        else:
                            to = ((yy + e) % side, xx)
                        pairs.append((place(k, h, yy, xx), place(k, h, *to)))
        return pairs

    r_pieces = [r_vals] + [lax.ppermute(r_vals, axes, shifted(e, True)) for e in range(1, side)]

    same, other = [], []
    for a in range(side):
        for b in range(side):
            for c in range(side):
                for d in range(side):
                    k = a * side + b
                    to_even = (c * side + b, 0, a, d)
                    to_odd = (a * side + d, 1, c, b)
                    same.append((place(k, 0, c, d), place(*to_even)))
                    same.append((place(k, 1, c, d), place(*to_odd)))
                    other.append((place(k, 1, c, d), place(*to_even)))
                    other.append((place(k, 0, c, d), place(*to_odd)))
    s_same = lax.ppermute(s_vals, axes, same)
    s_other = lax.ppermute(s_vals, axes, other)
    s_held = jnp.concatenate(
        [jnp.where(along, s_same, s_other), jnp.where(along, s_other, s_same)], axis=0
    )
    s_pieces = [s_held]
    for d in range(1, n_col):
        pairs = [
            ((k * 2 + h), (((k + d) % n_col) * 2 + h)) for k in range(n_col) for h in range(2)
        ]
        s_pieces.append(lax.ppermute(s_held, "row", pairs))
    flat = n_col & (n_col - 1) == 0
    partner = [(col ^ e) if flat else (col + e) % n_col for e in range(n_col)]
    t_flags = lax.dynamic_slice_in_dim(t_pattern, (row * n_col + col) * ap_tiles, ap_tiles, 1)
    turned = turn(jnp.stack(partner).astype(jnp.int32), t_flags, t_vals, c_width)
    held = lax.optimization_barrier((*r_pieces[1:], *turned[1:-1]))
    r_pieces[1:], sent = held[: side - 1], [*held[side - 1 :], turned[-1]]
    t_pieces = [turned[0]]
    for e in range(1, n_col):
        pairs = [(j, (j ^ e) if flat else (j + e) % n_col) for j in range(n_col)]
        t_pieces.append(lax.ppermute(sent[e - 1], "col", pairs))

    r_flags = lax.dynamic_slice_in_dim(r_pattern, row * a_tiles, a_tiles, 0)
    flags = [r_flags.reshape(-1), s_pattern.reshape(-1)]
    sizes = (side, a_tiles, r_pattern.shape[1], s_pattern.shape[1])

    blocks, spots, targets = [], [], []
    for e in range(side):
        g = (gather_at - e) % side
        blocks.append(jnp.where(along, y * side + g, g * side + x))
    for t in range(side):
        target = (target_at + t) % side
        for e in range(side):
            g = (gather_at - e) % side
            k = jnp.where(along, target * side + g, g * side + target)
            spots.append((line - k) % n_col)
        targets.append(jnp.where(along, target * side + x, y * side + target))
    table = jnp.concatenate([jnp.stack(blocks + spots + targets).astype(jnp.int32), *flags])

    block = max(a_part, math.gcd(a_rows, 4 * BLK))
    steps = a_rows // block
    chunks = 2 if steps % 2 == 0 else 1
    steps //= chunks
    coded = []
    for chunk in range(chunks):
        parts = []
        for e in range(1, side):
            codes = coded_product(
                sizes, table, r_pieces, s_pieces, e, block, chunk * steps * block, steps
            )
            if chunk:
                codes, *t_pieces[1:] = lax.optimization_barrier((codes, *t_pieces[1:]))
            parts.append(lax.ppermute(codes, axes, shifted(e, False)))
        coded.append(parts)
    order = [(col ^ o) if flat else (col - o) % n_col for o in range(n_col)]
    own, mirror = own_product(
        sizes, table, jnp.stack(order).astype(jnp.int32), r_pieces, s_pieces, t_pieces, block
    )
    own, mirror = in_vmem(own), in_vmem(mirror)
    out = None
    for chunk in range(chunks):
        out = join(own, mirror, coded[chunk], chunk * steps, out)
    return out


def solution(mesh):
    placed = (P("row", "col"), P("row", "col"), P(None, ("row", "col")), P(), P(), P())
    n_row, n_col = mesh.shape["row"], mesh.shape["col"]
    return jax.shard_map(
        functools.partial(body, n_row, n_col),
        mesh=mesh,
        in_specs=placed,
        out_specs=P("row", "col"),
        check_vma=False,
    )
```

```python
import functools
import math

import jax
import jax.numpy as jnp
from jax import lax
from jax.experimental import pallas as pl
from jax.experimental.pallas import tpu as pltpu
from jax.sharding import PartitionSpec as P

BLK = 128
STRIP = 16
LEVELS = 32767.0
FINE = 64.0
VMEM = 24 * 1024 * 1024


def masked(values, flag):
    return values * jnp.full((1, BLK), flag.astype(jnp.float32)).astype(jnp.bfloat16)


def joined_tiles(grid):
    bands = [jnp.concatenate(t, axis=1) if len(t) > 1 else t[0] for t in grid]
    return jnp.concatenate(bands, axis=0) if len(bands) > 1 else bands[0]


def whole(shape):
    return pl.BlockSpec(shape, lambda i, *_: (0,) * len(shape))


def cost(flops, bytes_accessed):
    return pl.CostEstimate(flops=flops, bytes_accessed=bytes_accessed, transcendentals=0)


def params(limit=VMEM):
    return pltpu.CompilerParams(vmem_limit_bytes=limit)


class Table:
    def __init__(self, ref, pieces, a_tiles, b_all, c_all):
        self.ref, self.pieces = ref, pieces
        self.b_all, self.c_all = b_all, c_all
        self.r_at = pieces * (pieces + 2)
        self.s_at = self.r_at + a_tiles * b_all

    def block(self, e):
        return self.ref[e]

    def spot(self, target, e):
        return self.ref[(target + 1) * self.pieces + e]

    def column(self, target):
        return self.ref[(self.pieces + 1) * self.pieces + target]

    def r_flag(self, a, b):
        return self.ref[self.r_at + a * self.b_all + b]

    def s_flag(self, b, c):
        return self.ref[self.s_at + b * self.c_all + c]


def select_copy(choice, sources, target, sem):
    for d, source in enumerate(sources):

        @pl.when(choice == d)
        def _(source=source):
            pltpu.make_async_copy(source, target, sem).start()

    return pltpu.make_async_copy(sources[0], target, sem)


def products(table, target, first, r_refs, s_refs, r_buf, s_buf, r_sem, s_sem, use):
    pieces, blocks, block, width = r_buf.shape
    cols = s_buf.shape[1]
    b_tiles, c_tiles = width // BLK, cols // BLK
    parts = (len(r_refs) - 1) // (pieces - 1)

    def r_copy(e, n):
        if e == 0:
            source = r_refs[0].at[pl.ds(first + n * block, block)]
        else:
            per = blocks // parts
            ref = r_refs[1 + (e - 1) * parts + n // per]
            source = ref.at[pl.ds(n % per * block, block)]
        return pltpu.make_async_copy(source, r_buf.at[e, n], r_sem.at[e, n])

    def r_wait(e, n):
        source = r_refs[min(e, 1)].at[pl.ds(0, block)]
        pltpu.make_async_copy(source, r_buf.at[e, n], r_sem.at[e, n]).wait()

    waits = [
        select_copy(table.spot(target, e), s_refs, s_buf.at[pl.ds(e * width, width)], s_sem.at[e])
        for e in range(pieces)
    ]
    for n in range(blocks):
        for e in range(pieces):
            r_copy(e, n).start()
    for e in range(pieces):
        waits[e].wait()
        for t in range(b_tiles):
            for u in range(c_tiles):
                flag = table.s_flag(table.block(e) * b_tiles + t, table.column(target) * c_tiles + u)
                down = slice(e * width + t * BLK, e * width + (t + 1) * BLK)
                over = slice(u * BLK, (u + 1) * BLK)
                s_buf[down, over] = masked(s_buf[down, over], flag)

    def one(n, carry):
        for e in range(pieces):
            r_wait(e, n)
        grid = []
        for t in range(block // BLK):
            a = first // BLK + n * (block // BLK) + t
            grid.append(
                [
                    masked(
                        r_buf[e, n, t * BLK : (t + 1) * BLK, u * BLK : (u + 1) * BLK],
                        table.r_flag(a, table.block(e) * b_tiles + u),
                    )
                    for e in range(pieces)
                    for u in range(b_tiles)
                ]
            )
        use(n, jnp.dot(joined_tiles(grid), s_buf[...], preferred_element_type=jnp.float32))
        return carry

    lax.fori_loop(0, blocks, one, 0)


def encode(total, out):
    rows, cols = total.shape
    group = rows // STRIP
    strip_row = lax.broadcasted_iota(jnp.int32, (STRIP, cols), 0)
    strip = jnp.zeros((STRIP, cols), jnp.float32)
    for g in range(STRIP):
        part = total[g * group : (g + 1) * group]
        top = jnp.max(jnp.max(jnp.abs(part), axis=0, keepdims=True), axis=1, keepdims=True)
        level = jnp.ceil(jnp.log2(jnp.maximum(top, 1e-30)) * FINE) + 1.0
        gain = jnp.exp2(level * (-1.0 / FINE)) * LEVELS
        code = jnp.clip(jnp.round(part * gain), -LEVELS, LEVELS)
        out[g * group : (g + 1) * group] = code.astype(jnp.int16)
        strip = jnp.where(strip_row == g, level, strip)
    out[rows:] = strip.astype(jnp.int16)


def coded_kernel(sizes, n_s, target, first, numbers, *refs):
    *ins, out, r_buf, s_buf, r_sem, s_sem = refs
    count = len(ins) - n_s

    def use(n, total):
        encode(total, out.at[n])

    products(
        Table(numbers, *sizes), target, first, ins[:count], ins[count:],
        r_buf, s_buf, r_sem, s_sem, use,
    )


def own_kernel(sizes, n_s, n_t, numbers, order, *refs):
    *ins, out, mirror, r_buf, s_buf, r_sem, s_sem, t_sem = refs
    count = len(ins) - n_s - n_t
    t_refs = ins[count + n_s :]
    blocks, block, _ = mirror.shape
    a_part = t_refs[0].shape[0]
    split = block // a_part
    waits = []
    for o in range(blocks * split):
        rows = pl.ds(o % split * a_part, a_part)
        waits.append(select_copy(order[o], t_refs, mirror.at[o // split, rows], t_sem.at[o]))

    def use(n, total):
        out[n] = total

    products(
        Table(numbers, *sizes), 0, 0, ins[:count], ins[count : count + n_s],
        r_buf, s_buf, r_sem, s_sem, use,
    )
    for wait in waits:
        wait.wait()


SCALARS = pl.BlockSpec(memory_space=pltpu.SMEM)
ANYWHERE = pl.BlockSpec(memory_space=pl.ANY)
INSIDE = pl.BlockSpec(memory_space=pltpu.VMEM)


def product_scratch(pieces, blocks, block, width, cols):
    return [
        pltpu.VMEM((pieces, blocks, block, width), jnp.bfloat16),
        pltpu.VMEM((pieces * width, cols), jnp.bfloat16),
        pltpu.SemaphoreType.DMA((pieces, blocks)),
        pltpu.SemaphoreType.DMA((pieces,)),
    ]


def coded_product(sizes, table, r_vals, r_parts, s_pieces, target, block, first, blocks):
    pieces = 1 + len(r_parts)
    width, cols = s_pieces[0].shape
    return pl.pallas_call(
        functools.partial(coded_kernel, sizes, len(s_pieces), target, first),
        out_shape=pltpu.VMEM((blocks, block + STRIP, cols), jnp.int16),
        in_specs=[SCALARS] + [ANYWHERE] * (pieces + len(s_pieces)),
        out_specs=INSIDE,
        scratch_shapes=product_scratch(pieces, blocks, block, width, cols),
        compiler_params=params(),
        cost_estimate=cost(2 * blocks * block * pieces * width * cols // 16, 0),
    )(table, r_vals, *r_parts, *s_pieces)


def own_product(sizes, table, order, r_vals, r_halves, s_pieces, t_pieces, block):
    pieces = 1 + len(r_halves[0])
    width, cols = s_pieces[0].shape
    blocks = r_vals.shape[0] // block
    r_parts = [half[e] for e in range(pieces - 1) for half in r_halves]
    return pl.pallas_call(
        functools.partial(own_kernel, sizes, len(s_pieces), len(t_pieces)),
        out_shape=[
            pltpu.VMEM((blocks, block, cols), jnp.float32),
            pltpu.VMEM((blocks, block, cols), jnp.bfloat16),
        ],
        in_specs=[SCALARS] * 2
        + [ANYWHERE] * (1 + len(r_parts) + len(s_pieces) + len(t_pieces)),
        out_specs=[INSIDE] * 2,
        scratch_shapes=product_scratch(pieces, blocks, block, width, cols)
        + [pltpu.SemaphoreType.DMA((len(t_pieces),))],
        compiler_params=params(),
        cost_estimate=cost(2 * blocks * block * pieces * width * cols // 16, 0),
    )(table, order, r_vals, *r_parts, *s_pieces, *t_pieces)


def join_kernel(parts, first, own, mirror, *refs):
    codes = refs[:parts]
    out, o_buf, gains, o_sem = refs[-4:]
    blocks, block, cols = o_buf.shape
    group = block // STRIP
    outs = []
    for n in range(blocks):
        for k in range(parts):
            level = codes[k][n, block:].astype(jnp.float32)
            gains[k] = jnp.exp2(level * (1.0 / FINE)) * (1.0 / LEVELS)
        for half in range(2):
            for g in range(half * STRIP // 2, (half + 1) * STRIP // 2):
                at = slice(g * group, (g + 1) * group)
                total = own[first + n, at]
                for k in range(parts):
                    total += codes[k][n, at].astype(jnp.float32) * gains[k, g : g + 1]
                factor = mirror[first + n, at].astype(jnp.float32)
                o_buf[n, at] = (total * factor).astype(jnp.bfloat16)
            here = pl.ds(half * block // 2, block // 2)
            rows = pl.ds((first + n) * block + half * block // 2, block // 2)
            outs.append(
                pltpu.make_async_copy(o_buf.at[n, here], out.at[rows], o_sem.at[n, half])
            )
            outs[-1].start()
    for copy in outs:
        copy.wait()


def in_vmem(values):
    return pltpu.with_memory_space_constraint(values, pltpu.VMEM)


def join(own, mirror, coded, first, before):
    steps, block, cols = own.shape
    blocks = coded[0].shape[0]
    aliases, carried = {}, ()
    if before is not None:
        aliases, carried = {2 + len(coded): 0}, (before,)
    return pl.pallas_call(
        functools.partial(join_kernel, len(coded), first),
        out_shape=jax.ShapeDtypeStruct((steps * block, cols), jnp.bfloat16),
        in_specs=[INSIDE] * (2 + len(coded)) + [ANYWHERE] * len(carried),
        out_specs=ANYWHERE,
        scratch_shapes=[
            pltpu.VMEM((blocks, block, cols), jnp.bfloat16),
            pltpu.VMEM((len(coded), STRIP, cols), jnp.float32),
            pltpu.SemaphoreType.DMA((blocks, 2)),
        ],
        input_output_aliases=aliases,
        compiler_params=params(),
        cost_estimate=cost(0, 0),
    )(own, mirror, *[in_vmem(codes) for codes in coded], *carried)


def turn_kernel(pieces, width, places, flags, t_ref, *outs):
    a_width = t_ref.shape[1]
    for e in range(pieces):

        def one(t, carry, e=e):
            start = pl.multiple_of(places[e] * width + t * BLK, BLK)
            over = pl.ds(pl.multiple_of(t * BLK, BLK), BLK)
            for u in range(a_width // BLK):
                tile = masked(
                    t_ref[pl.ds(start, BLK), u * BLK : (u + 1) * BLK],
                    flags[places[e] * (width // BLK) + t, u],
                )
                outs[e][u * BLK : (u + 1) * BLK, over] = tile.T
            return carry

        lax.fori_loop(0, width // BLK, one, 0)


def turn(places, flags, t_vals, c_width):
    pieces = t_vals.shape[0] // c_width
    shape = (t_vals.shape[1], c_width)
    return pl.pallas_call(
        functools.partial(turn_kernel, pieces, c_width),
        out_shape=[jax.ShapeDtypeStruct(shape, jnp.bfloat16)] * pieces,
        grid_spec=pltpu.PrefetchScalarGridSpec(
            num_scalar_prefetch=2,
            grid=(1,),
            in_specs=[whole(t_vals.shape)],
            out_specs=[whole(shape)] * pieces,
        ),
        compiler_params=params(),
        cost_estimate=cost(0, 4 * t_vals.size),
    )(places, flags, t_vals)


def body(n_row, n_col, r_vals, s_vals, t_vals, r_pattern, s_pattern, t_pattern):
    side = math.isqrt(n_col)
    row = lax.axis_index("row")
    col = lax.axis_index("col")
    line, kind = row // 2, row % 2
    y, x = col // side, col % side
    a_rows, b_width = r_vals.shape
    c_width = s_vals.shape[1]
    a_part = t_vals.shape[1]
    a_tiles, ap_tiles = a_rows // BLK, a_part // BLK
    along = kind == 0
    gather_at = jnp.where(along, x, y)
    target_at = jnp.where(along, y, x)
    axes = ("row", "col")

    def place(k, h, yy, xx):
        return (k * 2 + h) * n_col + yy * side + xx

    def shifted(e, gather):
        pairs = []
        for k in range(n_row // 2):
            for h in range(2):
                for yy in range(side):
                    for xx in range(side):
                        if (h == 0) == gather:
                            to = (yy, (xx + e) % side)
                        else:
                            to = ((yy + e) % side, xx)
                        pairs.append((place(k, h, yy, xx), place(k, h, *to)))
        return pairs

    block = max(a_part, math.gcd(a_rows, 4 * BLK))
    chunks = 2 if a_rows // block % 2 == 0 else 1
    steps = a_rows // block // chunks
    r_halves = []
    for chunk in range(chunks):
        sent = r_vals[chunk * steps * block : (chunk + 1) * steps * block]
        r_halves.append([lax.ppermute(sent, axes, shifted(e, True)) for e in range(1, side)])

    same, other = [], []
    for a in range(side):
        for b in range(side):
            for c in range(side):
                for d in range(side):
                    k = a * side + b
                    to_even = (c * side + b, 0, a, d)
                    to_odd = (a * side + d, 1, c, b)
                    same.append((place(k, 0, c, d), place(*to_even)))
                    same.append((place(k, 1, c, d), place(*to_odd)))
                    other.append((place(k, 1, c, d), place(*to_even)))
                    other.append((place(k, 0, c, d), place(*to_odd)))
    s_same = lax.ppermute(s_vals, axes, same)
    s_other = lax.ppermute(s_vals, axes, other)
    s_held = jnp.concatenate(
        [jnp.where(along, s_same, s_other), jnp.where(along, s_other, s_same)], axis=0
    )
    s_pieces = [s_held]
    for d in range(1, n_col):
        pairs = [
            ((k * 2 + h), (((k + d) % n_col) * 2 + h)) for k in range(n_col) for h in range(2)
        ]
        s_pieces.append(lax.ppermute(s_held, "row", pairs))
    flat = n_col & (n_col - 1) == 0
    partner = [(col ^ e) if flat else (col + e) % n_col for e in range(n_col)]
    t_flags = lax.dynamic_slice_in_dim(t_pattern, (row * n_col + col) * ap_tiles, ap_tiles, 1)
    turned = turn(jnp.stack(partner).astype(jnp.int32), t_flags, t_vals, c_width)
    held = lax.optimization_barrier((*r_halves[0], *turned[1:-1]))
    r_halves[0], sent = list(held[: side - 1]), [*held[side - 1 :], turned[-1]]
    t_pieces = [turned[0]]
    for e in range(1, n_col):
        pairs = [(j, (j ^ e) if flat else (j + e) % n_col) for j in range(n_col)]
        t_pieces.append(lax.ppermute(sent[e - 1], "col", pairs))

    r_flags = lax.dynamic_slice_in_dim(r_pattern, row * a_tiles, a_tiles, 0)
    flags = [r_flags.reshape(-1), s_pattern.reshape(-1)]
    sizes = (side, a_tiles, r_pattern.shape[1], s_pattern.shape[1])

    blocks, spots, targets = [], [], []
    for e in range(side):
        g = (gather_at - e) % side
        blocks.append(jnp.where(along, y * side + g, g * side + x))
    for t in range(side):
        target = (target_at + t) % side
        for e in range(side):
            g = (gather_at - e) % side
            k = jnp.where(along, target * side + g, g * side + target)
            spots.append((line - k) % n_col)
        targets.append(jnp.where(along, target * side + x, y * side + target))
    table = jnp.concatenate([jnp.stack(blocks + spots + targets).astype(jnp.int32), *flags])

    coded = []
    for chunk in range(chunks):
        parts = []
        for e in range(1, side):
            codes = coded_product(
                sizes, table, r_vals, r_halves[chunk], s_pieces, e,
                block, chunk * steps * block, steps,
            )
            if chunk:
                codes, *t_pieces[1:] = lax.optimization_barrier((codes, *t_pieces[1:]))
            parts.append(lax.ppermute(codes, axes, shifted(e, False)))
        coded.append(parts)
    order = [(col ^ o) if flat else (col - o) % n_col for o in range(n_col)]
    own, mirror = own_product(
        sizes, table, jnp.stack(order).astype(jnp.int32), r_vals, r_halves, s_pieces, t_pieces, block
    )
    own, mirror = in_vmem(own), in_vmem(mirror)
    out = None
    for chunk in range(chunks):
        out = join(own, mirror, coded[chunk], chunk * steps, out)
    return out


def solution(mesh):
    placed = (P("row", "col"), P("row", "col"), P(None, ("row", "col")), P(), P(), P())
    n_row, n_col = mesh.shape["row"], mesh.shape["col"]
    return jax.shard_map(
        functools.partial(body, n_row, n_col),
        mesh=mesh,
        in_specs=placed,
        out_specs=P("row", "col"),
        check_vma=False,
    )
```

```python
import functools
import math

import jax
import jax.numpy as jnp
from jax import lax
from jax.experimental import pallas as pl
from jax.experimental.pallas import tpu as pltpu
from jax.sharding import PartitionSpec as P

BLK = 128
STRIP = 16
LEVELS = 32767.0
FINE = 64.0
VMEM = 24 * 1024 * 1024


def masked(values, flag):
    return values * jnp.full((1, BLK), flag.astype(jnp.float32)).astype(jnp.bfloat16)


def joined_tiles(grid):
    bands = [jnp.concatenate(t, axis=1) if len(t) > 1 else t[0] for t in grid]
    return jnp.concatenate(bands, axis=0) if len(bands) > 1 else bands[0]


def whole(shape):
    return pl.BlockSpec(shape, lambda i, *_: (0,) * len(shape))


def cost(flops, bytes_accessed):
    return pl.CostEstimate(flops=flops, bytes_accessed=bytes_accessed, transcendentals=0)


def params(limit=VMEM):
    return pltpu.CompilerParams(vmem_limit_bytes=limit)


class Table:
    def __init__(self, ref, pieces, a_tiles, b_all, c_all):
        self.ref, self.pieces = ref, pieces
        self.b_all, self.c_all = b_all, c_all
        self.r_at = pieces * (pieces + 2)
        self.s_at = self.r_at + a_tiles * b_all

    def block(self, e):
        return self.ref[e]

    def spot(self, target, e):
        return self.ref[(target + 1) * self.pieces + e]

    def column(self, target):
        return self.ref[(self.pieces + 1) * self.pieces + target]

    def r_flag(self, a, b):
        return self.ref[self.r_at + a * self.b_all + b]

    def s_flag(self, b, c):
        return self.ref[self.s_at + b * self.c_all + c]


def select_copy(choice, sources, target, sem):
    for d, source in enumerate(sources):

        @pl.when(choice == d)
        def _(source=source):
            pltpu.make_async_copy(source, target, sem).start()

    return pltpu.make_async_copy(sources[0], target, sem)


def products(table, target, first, r_refs, s_ref, r_buf, s_buf, r_sem, s_sem, use):
    pieces, blocks, block, width = r_buf.shape
    cols = s_buf.shape[1]
    b_tiles, c_tiles = width // BLK, cols // BLK

    def r_copy(e, n):
        rows = pl.ds(pl.multiple_of(first + n * block, block), block)
        return pltpu.make_async_copy(r_refs[e].at[rows], r_buf.at[e, n], r_sem.at[e, n])

    waits = [
        pltpu.make_async_copy(
            s_ref.at[table.spot(target, e)], s_buf.at[pl.ds(e * width, width)], s_sem.at[e]
        )
        for e in range(pieces)
    ]
    for wait in waits:
        wait.start()
    for n in range(blocks):
        for e in range(pieces):
            r_copy(e, n).start()
    for e in range(pieces):
        waits[e].wait()
        for t in range(b_tiles):
            for u in range(c_tiles):
                flag = table.s_flag(table.block(e) * b_tiles + t, table.column(target) * c_tiles + u)
                down = slice(e * width + t * BLK, e * width + (t + 1) * BLK)
                over = slice(u * BLK, (u + 1) * BLK)
                s_buf[down, over] = masked(s_buf[down, over], flag)

    def one(n, carry):
        for e in range(pieces):
            r_copy(e, n).wait()
        grid = []
        for t in range(block // BLK):
            a = first // BLK + n * (block // BLK) + t
            grid.append(
                [
                    masked(
                        r_buf[e, n, t * BLK : (t + 1) * BLK, u * BLK : (u + 1) * BLK],
                        table.r_flag(a, table.block(e) * b_tiles + u),
                    )
                    for e in range(pieces)
                    for u in range(b_tiles)
                ]
            )
        use(n, jnp.dot(joined_tiles(grid), s_buf[...], preferred_element_type=jnp.float32))
        return carry

    lax.fori_loop(0, blocks, one, 0)


def encode(total, out):
    rows, cols = total.shape
    group = rows // STRIP
    strip_row = lax.broadcasted_iota(jnp.int32, (STRIP, cols), 0)
    strip = jnp.zeros((STRIP, cols), jnp.float32)
    for g in range(STRIP):
        part = total[g * group : (g + 1) * group]
        top = jnp.max(jnp.max(jnp.abs(part), axis=0, keepdims=True), axis=1, keepdims=True)
        level = jnp.ceil(jnp.log2(jnp.maximum(top, 1e-30)) * FINE) + 1.0
        gain = jnp.exp2(level * (-1.0 / FINE)) * LEVELS
        code = jnp.clip(jnp.round(part * gain), -LEVELS, LEVELS)
        out[g * group : (g + 1) * group] = code.astype(jnp.int16)
        strip = jnp.where(strip_row == g, level, strip)
    out[rows:] = strip.astype(jnp.int16)


def coded_kernel(sizes, target, first, numbers, *refs):
    *ins, out, r_buf, s_buf, r_sem, s_sem = refs
    pieces = r_buf.shape[0]

    def use(n, total):
        encode(total, out.at[n])

    products(
        Table(numbers, *sizes), target, first, ins[:pieces], ins[pieces],
        r_buf, s_buf, r_sem, s_sem, use,
    )


def own_kernel(sizes, numbers, order, *refs):
    *ins, out, mirror, r_buf, s_buf, r_sem, s_sem, t_sem = refs
    pieces = r_buf.shape[0]
    t_refs = ins[pieces + 1 :]
    blocks, block, _ = mirror.shape
    a_part = t_refs[0].shape[0]
    split = block // a_part
    waits = []
    for o in range(blocks * split):
        rows = pl.ds(o % split * a_part, a_part)
        waits.append(select_copy(order[o], t_refs, mirror.at[o // split, rows], t_sem.at[o]))

    def use(n, total):
        out[n] = total

    products(
        Table(numbers, *sizes), 0, 0, ins[:pieces], ins[pieces],
        r_buf, s_buf, r_sem, s_sem, use,
    )
    for wait in waits:
        wait.wait()


SCALARS = pl.BlockSpec(memory_space=pltpu.SMEM)
ANYWHERE = pl.BlockSpec(memory_space=pl.ANY)
INSIDE = pl.BlockSpec(memory_space=pltpu.VMEM)


def product_scratch(pieces, blocks, block, width, cols):
    return [
        pltpu.VMEM((pieces, blocks, block, width), jnp.bfloat16),
        pltpu.VMEM((pieces * width, cols), jnp.bfloat16),
        pltpu.SemaphoreType.DMA((pieces, blocks)),
        pltpu.SemaphoreType.DMA((pieces,)),
    ]


def coded_product(sizes, table, r_pieces, s_line, target, block, first, blocks):
    pieces = len(r_pieces)
    width, cols = s_line.shape[1:]
    return pl.pallas_call(
        functools.partial(coded_kernel, sizes, target, first),
        out_shape=pltpu.VMEM((blocks, block + STRIP, cols), jnp.int16),
        in_specs=[SCALARS] + [ANYWHERE] * (pieces + 1),
        out_specs=INSIDE,
        scratch_shapes=product_scratch(pieces, blocks, block, width, cols),
        compiler_params=params(),
        cost_estimate=cost(2 * blocks * block * pieces * width * cols // 16, 0),
    )(table, *r_pieces, s_line)


def own_product(sizes, table, order, r_pieces, s_line, t_pieces, block):
    pieces = len(r_pieces)
    width, cols = s_line.shape[1:]
    blocks = r_pieces[0].shape[0] // block
    return pl.pallas_call(
        functools.partial(own_kernel, sizes),
        out_shape=[
            pltpu.VMEM((blocks, block, cols), jnp.float32),
            pltpu.VMEM((blocks, block, cols), jnp.bfloat16),
        ],
        in_specs=[SCALARS] * 2 + [ANYWHERE] * (pieces + 1 + len(t_pieces)),
        out_specs=[INSIDE] * 2,
        scratch_shapes=product_scratch(pieces, blocks, block, width, cols)
        + [pltpu.SemaphoreType.DMA((len(t_pieces),))],
        compiler_params=params(),
        cost_estimate=cost(2 * blocks * block * pieces * width * cols // 16, 0),
    )(table, order, *r_pieces, s_line, *t_pieces)


def join_kernel(parts, first, own, mirror, *refs):
    codes = refs[:parts]
    out, o_buf, gains, o_sem = refs[-4:]
    blocks, block, cols = o_buf.shape
    group = block // STRIP
    outs = []
    for n in range(blocks):
        for k in range(parts):
            level = codes[k][n, block:].astype(jnp.float32)
            gains[k] = jnp.exp2(level * (1.0 / FINE)) * (1.0 / LEVELS)
        for half in range(2):
            for g in range(half * STRIP // 2, (half + 1) * STRIP // 2):
                at = slice(g * group, (g + 1) * group)
                total = own[first + n, at]
                for k in range(parts):
                    total += codes[k][n, at].astype(jnp.float32) * gains[k, g : g + 1]
                factor = mirror[first + n, at].astype(jnp.float32)
                o_buf[n, at] = (total * factor).astype(jnp.bfloat16)
            here = pl.ds(half * block // 2, block // 2)
            rows = pl.ds((first + n) * block + half * block // 2, block // 2)
            outs.append(
                pltpu.make_async_copy(o_buf.at[n, here], out.at[rows], o_sem.at[n, half])
            )
            outs[-1].start()
    for copy in outs:
        copy.wait()


def in_vmem(values):
    return pltpu.with_memory_space_constraint(values, pltpu.VMEM)


def join(own, mirror, coded, first, before):
    steps, block, cols = own.shape
    blocks = coded[0].shape[0]
    aliases, carried = {}, ()
    if before is not None:
        aliases, carried = {2 + len(coded): 0}, (before,)
    return pl.pallas_call(
        functools.partial(join_kernel, len(coded), first),
        out_shape=jax.ShapeDtypeStruct((steps * block, cols), jnp.bfloat16),
        in_specs=[INSIDE] * (2 + len(coded)) + [ANYWHERE] * len(carried),
        out_specs=ANYWHERE,
        scratch_shapes=[
            pltpu.VMEM((blocks, block, cols), jnp.bfloat16),
            pltpu.VMEM((len(coded), STRIP, cols), jnp.float32),
            pltpu.SemaphoreType.DMA((blocks, 2)),
        ],
        input_output_aliases=aliases,
        compiler_params=params(),
        cost_estimate=cost(0, 0),
    )(own, mirror, *[in_vmem(codes) for codes in coded], *carried)


def turn_kernel(pieces, width, places, flags, t_ref, *outs):
    a_width = t_ref.shape[1]
    for e in range(pieces):

        def one(t, carry, e=e):
            start = pl.multiple_of(places[e] * width + t * BLK, BLK)
            over = pl.ds(pl.multiple_of(t * BLK, BLK), BLK)
            for u in range(a_width // BLK):
                tile = masked(
                    t_ref[pl.ds(start, BLK), u * BLK : (u + 1) * BLK],
                    flags[places[e] * (width // BLK) + t, u],
                )
                outs[e][u * BLK : (u + 1) * BLK, over] = tile.T
            return carry

        lax.fori_loop(0, width // BLK, one, 0)


def turn(places, flags, t_vals, c_width):
    pieces = t_vals.shape[0] // c_width
    shape = (t_vals.shape[1], c_width)
    return pl.pallas_call(
        functools.partial(turn_kernel, pieces, c_width),
        out_shape=[jax.ShapeDtypeStruct(shape, jnp.bfloat16)] * pieces,
        grid_spec=pltpu.PrefetchScalarGridSpec(
            num_scalar_prefetch=2,
            grid=(1,),
            in_specs=[whole(t_vals.shape)],
            out_specs=[whole(shape)] * pieces,
        ),
        compiler_params=params(),
        cost_estimate=cost(0, 4 * t_vals.size),
    )(places, flags, t_vals)


def body(n_row, n_col, r_vals, s_vals, t_vals, r_pattern, s_pattern, t_pattern):
    side = math.isqrt(n_col)
    row = lax.axis_index("row")
    col = lax.axis_index("col")
    kind = row % 2
    y, x = col // side, col % side
    a_rows, b_width = r_vals.shape
    c_width = s_vals.shape[1]
    a_part = t_vals.shape[1]
    a_tiles, ap_tiles = a_rows // BLK, a_part // BLK
    along = kind == 0
    gather_at = jnp.where(along, x, y)
    target_at = jnp.where(along, y, x)
    axes = ("row", "col")

    def place(k, h, yy, xx):
        return (k * 2 + h) * n_col + yy * side + xx

    def shifted(e, gather):
        pairs = []
        for k in range(n_row // 2):
            for h in range(2):
                for yy in range(side):
                    for xx in range(side):
                        if (h == 0) == gather:
                            to = (yy, (xx + e) % side)
                        else:
                            to = ((yy + e) % side, xx)
                        pairs.append((place(k, h, yy, xx), place(k, h, *to)))
        return pairs

    r_pieces = [r_vals] + [lax.ppermute(r_vals, axes, shifted(e, True)) for e in range(1, side)]

    same, other = [], []
    for a in range(side):
        for b in range(side):
            for c in range(side):
                for d in range(side):
                    k = a * side + b
                    to_even = (c * side + b, 0, a, d)
                    to_odd = (a * side + d, 1, c, b)
                    same.append((place(k, 0, c, d), place(*to_even)))
                    same.append((place(k, 1, c, d), place(*to_odd)))
                    other.append((place(k, 1, c, d), place(*to_even)))
                    other.append((place(k, 0, c, d), place(*to_odd)))
    s_same = lax.ppermute(s_vals, axes, same)
    s_other = lax.ppermute(s_vals, axes, other)
    s_held = jnp.concatenate(
        [jnp.where(along, s_same, s_other), jnp.where(along, s_other, s_same)], axis=0
    )
    lines = [[k * 2 + h for k in range(n_row // 2)] for h in range(2)]
    s_line = lax.all_gather(s_held, "row", axis=0, axis_index_groups=lines)
    s_line = pltpu.with_memory_space_constraint(s_line, pltpu.HBM)

    flat = n_col & (n_col - 1) == 0
    partner = [(col ^ e) if flat else (col + e) % n_col for e in range(n_col)]
    t_flags = lax.dynamic_slice_in_dim(t_pattern, (row * n_col + col) * ap_tiles, ap_tiles, 1)
    turned = turn(jnp.stack(partner).astype(jnp.int32), t_flags, t_vals, c_width)
    t_pieces = [turned[0]]
    for e in range(1, n_col):
        pairs = [(j, (j ^ e) if flat else (j + e) % n_col) for j in range(n_col)]
        t_pieces.append(lax.ppermute(turned[e], "col", pairs))

    r_flags = lax.dynamic_slice_in_dim(r_pattern, row * a_tiles, a_tiles, 0)
    flags = [r_flags.reshape(-1), s_pattern.reshape(-1)]
    sizes = (side, a_tiles, r_pattern.shape[1], s_pattern.shape[1])

    blocks, spots, targets = [], [], []
    for e in range(side):
        g = (gather_at - e) % side
        blocks.append(jnp.where(along, y * side + g, g * side + x))
    for t in range(side):
        target = (target_at + t) % side
        for e in range(side):
            g = (gather_at - e) % side
            k = jnp.where(along, target * side + g, g * side + target)
            spots.append(k)
        targets.append(jnp.where(along, target * side + x, y * side + target))
    table = jnp.concatenate([jnp.stack(blocks + spots + targets).astype(jnp.int32), *flags])

    block = max(a_part, math.gcd(a_rows, 4 * BLK))
    steps = a_rows // block
    chunks = 2 if steps % 2 == 0 else 1
    steps //= chunks
    coded = []
    for chunk in range(chunks):
        parts = []
        for e in range(1, side):
            codes = coded_product(
                sizes, table, r_pieces, s_line, e, block, chunk * steps * block, steps
            )
            if chunk:
                codes, *t_pieces[1:] = lax.optimization_barrier((codes, *t_pieces[1:]))
            parts.append(lax.ppermute(codes, axes, shifted(e, False)))
        coded.append(parts)
    order = [(col ^ o) if flat else (col - o) % n_col for o in range(n_col)]
    own, mirror = own_product(
        sizes, table, jnp.stack(order).astype(jnp.int32), r_pieces, s_line, t_pieces, block
    )
    own, mirror = in_vmem(own), in_vmem(mirror)
    out = None
    for chunk in range(chunks):
        out = join(own, mirror, coded[chunk], chunk * steps, out)
    return out


def solution(mesh):
    placed = (P("row", "col"), P("row", "col"), P(None, ("row", "col")), P(), P(), P())
    n_row, n_col = mesh.shape["row"], mesh.shape["col"]
    return jax.shard_map(
        functools.partial(body, n_row, n_col),
        mesh=mesh,
        in_specs=placed,
        out_specs=P("row", "col"),
        check_vma=False,
    )
```

```python
import functools
import math

import jax
import jax.numpy as jnp
from jax import lax
from jax.experimental import pallas as pl
from jax.experimental.pallas import tpu as pltpu
from jax.sharding import PartitionSpec as P

BLK = 128
STRIP = 16
LEVELS = 32767.0
FINE = 64.0
VMEM = 24 * 1024 * 1024


def masked(values, flag):
    return values * jnp.full((1, BLK), flag.astype(jnp.float32)).astype(jnp.bfloat16)


def joined_tiles(grid):
    bands = [jnp.concatenate(t, axis=1) if len(t) > 1 else t[0] for t in grid]
    return jnp.concatenate(bands, axis=0) if len(bands) > 1 else bands[0]


def whole(shape):
    return pl.BlockSpec(shape, lambda i, *_: (0,) * len(shape))


def cost(flops, bytes_accessed):
    return pl.CostEstimate(flops=flops, bytes_accessed=bytes_accessed, transcendentals=0)


def params(limit=VMEM):
    return pltpu.CompilerParams(vmem_limit_bytes=limit)


class Table:
    def __init__(self, ref, pieces, a_tiles, b_all, c_all):
        self.ref, self.pieces = ref, pieces
        self.b_all, self.c_all = b_all, c_all
        self.r_at = pieces * (pieces + 2)
        self.s_at = self.r_at + a_tiles * b_all

    def block(self, e):
        return self.ref[e]

    def spot(self, target, e):
        return self.ref[(target + 1) * self.pieces + e]

    def column(self, target):
        return self.ref[(self.pieces + 1) * self.pieces + target]

    def r_flag(self, a, b):
        return self.ref[self.r_at + a * self.b_all + b]

    def s_flag(self, b, c):
        return self.ref[self.s_at + b * self.c_all + c]


def select_copy(choice, sources, target, sem):
    for d, source in enumerate(sources):

        @pl.when(choice == d)
        def _(source=source):
            pltpu.make_async_copy(source, target, sem).start()

    return pltpu.make_async_copy(sources[0], target, sem)


def products(table, target, first, r_refs, s_refs, r_buf, s_buf, r_sem, s_sem, use):
    pieces, blocks, block, width = r_buf.shape
    cols = s_buf.shape[1]
    b_tiles, c_tiles = width // BLK, cols // BLK

    def r_copy(e, n):
        rows = pl.ds(pl.multiple_of(first + n * block, block), block)
        return pltpu.make_async_copy(r_refs[e].at[rows], r_buf.at[e, n], r_sem.at[e, n])

    waits = [
        select_copy(table.spot(target, e), s_refs, s_buf.at[pl.ds(e * width, width)], s_sem.at[e])
        for e in range(pieces)
    ]
    for n in range(blocks):
        for e in range(pieces):
            r_copy(e, n).start()
    for e in range(pieces):
        waits[e].wait()
        for t in range(b_tiles):
            for u in range(c_tiles):
                flag = table.s_flag(table.block(e) * b_tiles + t, table.column(target) * c_tiles + u)
                down = slice(e * width + t * BLK, e * width + (t + 1) * BLK)
                over = slice(u * BLK, (u + 1) * BLK)
                s_buf[down, over] = masked(s_buf[down, over], flag)

    def one(n, carry):
        for e in range(pieces):
            r_copy(e, n).wait()
        grid = []
        for t in range(block // BLK):
            a = first // BLK + n * (block // BLK) + t
            grid.append(
                [
                    masked(
                        r_buf[e, n, t * BLK : (t + 1) * BLK, u * BLK : (u + 1) * BLK],
                        table.r_flag(a, table.block(e) * b_tiles + u),
                    )
                    for e in range(pieces)
                    for u in range(b_tiles)
                ]
            )
        use(n, jnp.dot(joined_tiles(grid), s_buf[...], preferred_element_type=jnp.float32))
        return carry

    lax.fori_loop(0, blocks, one, 0)


def encode(total, out):
    rows, cols = total.shape
    group = rows // STRIP
    strip_row = lax.broadcasted_iota(jnp.int32, (STRIP, cols), 0)
    strip = jnp.zeros((STRIP, cols), jnp.float32)
    for g in range(STRIP):
        part = total[g * group : (g + 1) * group]
        top = jnp.max(jnp.max(jnp.abs(part), axis=0, keepdims=True), axis=1, keepdims=True)
        level = jnp.ceil(jnp.log2(jnp.maximum(top, 1e-30)) * FINE) + 1.0
        gain = jnp.exp2(level * (-1.0 / FINE)) * LEVELS
        code = jnp.clip(jnp.round(part * gain), -LEVELS, LEVELS)
        out[g * group : (g + 1) * group] = code.astype(jnp.int16)
        strip = jnp.where(strip_row == g, level, strip)
    out[rows:] = strip.astype(jnp.int16)


def coded_kernel(sizes, target, first, numbers, *refs):
    *ins, out, r_buf, s_buf, r_sem, s_sem = refs
    pieces = r_buf.shape[0]

    def use(n, total):
        encode(total, out.at[n])

    products(
        Table(numbers, *sizes), target, first, ins[:pieces], ins[pieces:],
        r_buf, s_buf, r_sem, s_sem, use,
    )


def own_kernel(sizes, count, numbers, order, *refs):
    *ins, out, mirror, r_buf, s_buf, r_sem, s_sem, t_sem = refs
    pieces = r_buf.shape[0]
    t_refs = ins[pieces + count :]
    blocks, block, _ = mirror.shape
    a_part = t_refs[0].shape[0]
    split = block // a_part
    waits = []
    for o in range(blocks * split):
        rows = pl.ds(o % split * a_part, a_part)
        waits.append(select_copy(order[o], t_refs, mirror.at[o // split, rows], t_sem.at[o]))

    def use(n, total):
        out[n] = total

    products(
        Table(numbers, *sizes), 0, 0, ins[:pieces], ins[pieces : pieces + count],
        r_buf, s_buf, r_sem, s_sem, use,
    )
    for wait in waits:
        wait.wait()


SCALARS = pl.BlockSpec(memory_space=pltpu.SMEM)
ANYWHERE = pl.BlockSpec(memory_space=pl.ANY)
INSIDE = pl.BlockSpec(memory_space=pltpu.VMEM)


def product_scratch(pieces, blocks, block, width, cols):
    return [
        pltpu.VMEM((pieces, blocks, block, width), jnp.bfloat16),
        pltpu.VMEM((pieces * width, cols), jnp.bfloat16),
        pltpu.SemaphoreType.DMA((pieces, blocks)),
        pltpu.SemaphoreType.DMA((pieces,)),
    ]


def coded_product(sizes, table, r_pieces, s_pieces, target, block, first, blocks):
    pieces = len(r_pieces)
    width, cols = s_pieces[0].shape
    return pl.pallas_call(
        functools.partial(coded_kernel, sizes, target, first),
        out_shape=pltpu.VMEM((blocks, block + STRIP, cols), jnp.int16),
        in_specs=[SCALARS] + [ANYWHERE] * (pieces + len(s_pieces)),
        out_specs=INSIDE,
        scratch_shapes=product_scratch(pieces, blocks, block, width, cols),
        compiler_params=params(),
        cost_estimate=cost(2 * blocks * block * pieces * width * cols // 16, 0),
    )(table, *r_pieces, *s_pieces)


def own_product(sizes, table, order, r_pieces, s_pieces, t_pieces, block):
    pieces = len(r_pieces)
    width, cols = s_pieces[0].shape
    blocks = r_pieces[0].shape[0] // block
    return pl.pallas_call(
        functools.partial(own_kernel, sizes, len(s_pieces)),
        out_shape=[
            pltpu.VMEM((blocks, block, cols), jnp.float32),
            pltpu.VMEM((blocks, block, cols), jnp.bfloat16),
        ],
        in_specs=[SCALARS] * 2 + [ANYWHERE] * (pieces + len(s_pieces) + len(t_pieces)),
        out_specs=[INSIDE] * 2,
        scratch_shapes=product_scratch(pieces, blocks, block, width, cols)
        + [pltpu.SemaphoreType.DMA((len(t_pieces),))],
        compiler_params=params(),
        cost_estimate=cost(2 * blocks * block * pieces * width * cols // 16, 0),
    )(table, order, *r_pieces, *s_pieces, *t_pieces)


def join_kernel(parts, first, own, mirror, *refs):
    codes = refs[:parts]
    out, o_buf, gains, o_sem = refs[-4:]
    blocks, block, cols = o_buf.shape
    group = block // STRIP
    outs = []
    for n in range(blocks):
        for k in range(parts):
            level = codes[k][n, block:].astype(jnp.float32)
            gains[k] = jnp.exp2(level * (1.0 / FINE)) * (1.0 / LEVELS)
        for half in range(2):
            for g in range(half * STRIP // 2, (half + 1) * STRIP // 2):
                at = slice(g * group, (g + 1) * group)
                total = own[first + n, at]
                for k in range(parts):
                    total += codes[k][n, at].astype(jnp.float32) * gains[k, g : g + 1]
                factor = mirror[first + n, at].astype(jnp.float32)
                o_buf[n, at] = (total * factor).astype(jnp.bfloat16)
            here = pl.ds(half * block // 2, block // 2)
            rows = pl.ds((first + n) * block + half * block // 2, block // 2)
            outs.append(
                pltpu.make_async_copy(o_buf.at[n, here], out.at[rows], o_sem.at[n, half])
            )
            outs[-1].start()
    for copy in outs:
        copy.wait()


def in_vmem(values):
    return pltpu.with_memory_space_constraint(values, pltpu.VMEM)


def join(own, mirror, coded, first, before):
    steps, block, cols = own.shape
    blocks = coded[0].shape[0]
    aliases, carried = {}, ()
    if before is not None:
        aliases, carried = {2 + len(coded): 0}, (before,)
    return pl.pallas_call(
        functools.partial(join_kernel, len(coded), first),
        out_shape=jax.ShapeDtypeStruct((steps * block, cols), jnp.bfloat16),
        in_specs=[INSIDE] * (2 + len(coded)) + [ANYWHERE] * len(carried),
        out_specs=ANYWHERE,
        scratch_shapes=[
            pltpu.VMEM((blocks, block, cols), jnp.bfloat16),
            pltpu.VMEM((len(coded), STRIP, cols), jnp.float32),
            pltpu.SemaphoreType.DMA((blocks, 2)),
        ],
        input_output_aliases=aliases,
        compiler_params=params(),
        cost_estimate=cost(0, 0),
    )(own, mirror, *[in_vmem(codes) for codes in coded], *carried)


def turn_kernel(pieces, width, places, flags, t_ref, *outs):
    a_width = t_ref.shape[1]
    for e in range(pieces):

        def one(t, carry, e=e):
            start = pl.multiple_of(places[e] * width + t * BLK, BLK)
            over = pl.ds(pl.multiple_of(t * BLK, BLK), BLK)
            for u in range(a_width // BLK):
                tile = masked(
                    t_ref[pl.ds(start, BLK), u * BLK : (u + 1) * BLK],
                    flags[places[e] * (width // BLK) + t, u],
                )
                outs[e][u * BLK : (u + 1) * BLK, over] = tile.T
            return carry

        lax.fori_loop(0, width // BLK, one, 0)


def turn(places, flags, t_vals, c_width):
    pieces = t_vals.shape[0] // c_width
    shape = (t_vals.shape[1], c_width)
    return pl.pallas_call(
        functools.partial(turn_kernel, pieces, c_width),
        out_shape=[jax.ShapeDtypeStruct(shape, jnp.bfloat16)] * pieces,
        grid_spec=pltpu.PrefetchScalarGridSpec(
            num_scalar_prefetch=2,
            grid=(1,),
            in_specs=[whole(t_vals.shape)],
            out_specs=[whole(shape)] * pieces,
        ),
        compiler_params=params(),
        cost_estimate=cost(0, 4 * t_vals.size),
    )(places, flags, t_vals)


def body(n_row, n_col, r_vals, s_vals, t_vals, r_pattern, s_pattern, t_pattern):
    side = math.isqrt(n_col)
    row = lax.axis_index("row")
    col = lax.axis_index("col")
    line, kind = row // 2, row % 2
    y, x = col // side, col % side
    a_rows, b_width = r_vals.shape
    c_width = s_vals.shape[1]
    a_part = t_vals.shape[1]
    a_tiles, ap_tiles = a_rows // BLK, a_part // BLK
    along = kind == 0
    gather_at = jnp.where(along, x, y)
    target_at = jnp.where(along, y, x)
    axes = ("row", "col")

    def place(k, h, yy, xx):
        return (k * 2 + h) * n_col + yy * side + xx

    def shifted(e, gather):
        pairs = []
        for k in range(n_row // 2):
            for h in range(2):
                for yy in range(side):
                    for xx in range(side):
                        if (h == 0) == gather:
                            to = (yy, (xx + e) % side)
                        else:
                            to = ((yy + e) % side, xx)
                        pairs.append((place(k, h, yy, xx), place(k, h, *to)))
        return pairs

    r_pieces = [r_vals] + [lax.ppermute(r_vals, axes, shifted(e, True)) for e in range(1, side)]

    same, other = [], []
    for a in range(side):
        for b in range(side):
            for c in range(side):
                for d in range(side):
                    k = a * side + b
                    to_even = (c * side + b, 0, a, d)
                    to_odd = (a * side + d, 1, c, b)
                    same.append((place(k, 0, c, d), place(*to_even)))
                    same.append((place(k, 1, c, d), place(*to_odd)))
                    other.append((place(k, 1, c, d), place(*to_even)))
                    other.append((place(k, 0, c, d), place(*to_odd)))
    s_same = lax.ppermute(s_vals, axes, same)
    s_other = lax.ppermute(s_vals, axes, other)
    s_held = jnp.concatenate(
        [jnp.where(along, s_same, s_other), jnp.where(along, s_other, s_same)], axis=0
    )
    flat = n_col & (n_col - 1) == 0

    def along_line(values, hop):
        pairs = [(k * 2 + h, hop(k) * 2 + h) for k in range(n_col) for h in range(2)]
        return lax.ppermute(values, "row", pairs)

    if flat:
        got = {0: s_held}
        bit = n_col // 2
        while bit:
            got |= {m | bit: along_line(v, lambda k, bit=bit: k ^ bit) for m, v in got.items()}
            bit //= 2
        s_pieces = [got[m] for m in range(n_col)]
    else:
        s_pieces = [s_held] + [
            along_line(s_held, lambda k, d=d: (k + d) % n_col) for d in range(1, n_col)
        ]

    partner = [(col ^ e) if flat else (col + e) % n_col for e in range(n_col)]
    t_flags = lax.dynamic_slice_in_dim(t_pattern, (row * n_col + col) * ap_tiles, ap_tiles, 1)
    turned = turn(jnp.stack(partner).astype(jnp.int32), t_flags, t_vals, c_width)
    first = n_col // 2
    held = lax.optimization_barrier((s_pieces[first], *turned[1:-1]))
    s_pieces[first], sent = held[0], [*held[1:], turned[-1]]
    t_pieces = [turned[0]]
    for e in range(1, n_col):
        pairs = [(j, (j ^ e) if flat else (j + e) % n_col) for j in range(n_col)]
        t_pieces.append(lax.ppermute(sent[e - 1], "col", pairs))

    r_flags = lax.dynamic_slice_in_dim(r_pattern, row * a_tiles, a_tiles, 0)
    flags = [r_flags.reshape(-1), s_pattern.reshape(-1)]
    sizes = (side, a_tiles, r_pattern.shape[1], s_pattern.shape[1])

    blocks, spots, targets = [], [], []
    for e in range(side):
        g = (gather_at - e) % side
        blocks.append(jnp.where(along, y * side + g, g * side + x))
    for t in range(side):
        target = (target_at + t) % side
        for e in range(side):
            g = (gather_at - e) % side
            k = jnp.where(along, target * side + g, g * side + target)
            spots.append((line ^ k) if flat else (line - k) % n_col)
        targets.append(jnp.where(along, target * side + x, y * side + target))
    table = jnp.concatenate([jnp.stack(blocks + spots + targets).astype(jnp.int32), *flags])

    block = max(a_part, math.gcd(a_rows, 4 * BLK))
    steps = a_rows // block
    chunks = 2 if steps % 2 == 0 else 1
    steps //= chunks
    coded = []
    for chunk in range(chunks):
        parts = []
        for e in range(1, side):
            codes = coded_product(
                sizes, table, r_pieces, s_pieces, e, block, chunk * steps * block, steps
            )
            if chunk:
                codes, *t_pieces[1:] = lax.optimization_barrier((codes, *t_pieces[1:]))
            parts.append(lax.ppermute(codes, axes, shifted(e, False)))
        coded.append(parts)
    order = [(col ^ o) if flat else (col - o) % n_col for o in range(n_col)]
    own, mirror = own_product(
        sizes, table, jnp.stack(order).astype(jnp.int32), r_pieces, s_pieces, t_pieces, block
    )
    own, mirror = in_vmem(own), in_vmem(mirror)
    out = None
    for chunk in range(chunks):
        out = join(own, mirror, coded[chunk], chunk * steps, out)
    return out


def solution(mesh):
    placed = (P("row", "col"), P("row", "col"), P(None, ("row", "col")), P(), P(), P())
    n_row, n_col = mesh.shape["row"], mesh.shape["col"]
    return jax.shard_map(
        functools.partial(body, n_row, n_col),
        mesh=mesh,
        in_specs=placed,
        out_specs=P("row", "col"),
        check_vma=False,
    )
```

```python
import functools
import math

import jax
import jax.numpy as jnp
from jax import lax
from jax.experimental import pallas as pl
from jax.experimental.pallas import tpu as pltpu
from jax.sharding import PartitionSpec as P

BLK = 128
STRIP = 16
LEVELS = 32767.0
FINE = 64.0
VMEM = 24 * 1024 * 1024


def masked(values, flag):
    return values * jnp.full((1, BLK), flag.astype(jnp.float32)).astype(jnp.bfloat16)


def joined_tiles(grid):
    bands = [jnp.concatenate(t, axis=1) if len(t) > 1 else t[0] for t in grid]
    return jnp.concatenate(bands, axis=0) if len(bands) > 1 else bands[0]


def whole(shape):
    return pl.BlockSpec(shape, lambda i, *_: (0,) * len(shape))


def cost(flops, bytes_accessed):
    return pl.CostEstimate(flops=flops, bytes_accessed=bytes_accessed, transcendentals=0)


def params(limit=VMEM):
    return pltpu.CompilerParams(vmem_limit_bytes=limit)


class Table:
    def __init__(self, ref, pieces, a_tiles, b_all, c_all):
        self.ref, self.pieces = ref, pieces
        self.b_all, self.c_all = b_all, c_all
        self.r_at = pieces * (pieces + 2)
        self.s_at = self.r_at + a_tiles * b_all

    def block(self, e):
        return self.ref[e]

    def spot(self, target, e):
        return self.ref[(target + 1) * self.pieces + e]

    def column(self, target):
        return self.ref[(self.pieces + 1) * self.pieces + target]

    def r_flag(self, a, b):
        return self.ref[self.r_at + a * self.b_all + b]

    def s_flag(self, b, c):
        return self.ref[self.s_at + b * self.c_all + c]


def select_copy(choice, sources, target, sem):
    for d, source in enumerate(sources):

        @pl.when(choice == d)
        def _(source=source):
            pltpu.make_async_copy(source, target, sem).start()

    return pltpu.make_async_copy(sources[0], target, sem)


def products(table, target, first, r_refs, s_refs, r_buf, s_buf, r_sem, s_sem, use):
    pieces, blocks, block, width = r_buf.shape
    cols = s_buf.shape[1]
    b_tiles, c_tiles = width // BLK, cols // BLK

    def r_copy(e, n):
        rows = pl.ds(pl.multiple_of(first + n * block, block), block)
        return pltpu.make_async_copy(r_refs[e].at[rows], r_buf.at[e, n], r_sem.at[e, n])

    waits = [
        select_copy(table.spot(target, e), s_refs, s_buf.at[pl.ds(e * width, width)], s_sem.at[e])
        for e in range(pieces)
    ]
    for n in range(blocks):
        for e in range(pieces):
            r_copy(e, n).start()
    for e in range(pieces):
        waits[e].wait()
        for t in range(b_tiles):
            for u in range(c_tiles):
                flag = table.s_flag(table.block(e) * b_tiles + t, table.column(target) * c_tiles + u)
                down = slice(e * width + t * BLK, e * width + (t + 1) * BLK)
                over = slice(u * BLK, (u + 1) * BLK)
                s_buf[down, over] = masked(s_buf[down, over], flag)

    def one(n, carry):
        for e in range(pieces):
            r_copy(e, n).wait()
        grid = []
        for t in range(block // BLK):
            a = first // BLK + n * (block // BLK) + t
            grid.append(
                [
                    masked(
                        r_buf[e, n, t * BLK : (t + 1) * BLK, u * BLK : (u + 1) * BLK],
                        table.r_flag(a, table.block(e) * b_tiles + u),
                    )
                    for e in range(pieces)
                    for u in range(b_tiles)
                ]
            )
        use(n, jnp.dot(joined_tiles(grid), s_buf[...], preferred_element_type=jnp.float32))
        return carry

    lax.fori_loop(0, blocks, one, 0)


def encode(total, out):
    rows, cols = total.shape
    group = rows // STRIP
    strip_row = lax.broadcasted_iota(jnp.int32, (STRIP, cols), 0)
    strip = jnp.zeros((STRIP, cols), jnp.float32)
    for g in range(STRIP):
        part = total[g * group : (g + 1) * group]
        top = jnp.max(jnp.max(jnp.abs(part), axis=0, keepdims=True), axis=1, keepdims=True)
        level = jnp.ceil(jnp.log2(jnp.maximum(top, 1e-30)) * FINE) + 1.0
        gain = jnp.exp2(level * (-1.0 / FINE)) * LEVELS
        code = jnp.clip(jnp.round(part * gain), -LEVELS, LEVELS)
        out[g * group : (g + 1) * group] = code.astype(jnp.int16)
        strip = jnp.where(strip_row == g, level, strip)
    out[rows:] = strip.astype(jnp.int16)


def coded_kernel(sizes, target, first, numbers, *refs):
    *ins, out, r_buf, s_buf, r_sem, s_sem = refs
    pieces = r_buf.shape[0]

    def use(n, total):
        encode(total, out.at[n])

    products(
        Table(numbers, *sizes), target, first, ins[:pieces], ins[pieces:],
        r_buf, s_buf, r_sem, s_sem, use,
    )


def own_kernel(sizes, count, numbers, order, *refs):
    *ins, out, mirror, r_buf, s_buf, r_sem, s_sem, t_sem = refs
    pieces = r_buf.shape[0]
    t_refs = ins[pieces + count :]
    blocks, block, _ = mirror.shape
    a_part = t_refs[0].shape[0]
    split = block // a_part
    waits = []
    for o in range(blocks * split):
        rows = pl.ds(o % split * a_part, a_part)
        waits.append(select_copy(order[o], t_refs, mirror.at[o // split, rows], t_sem.at[o]))

    def use(n, total):
        out[n] = total

    products(
        Table(numbers, *sizes), 0, 0, ins[:pieces], ins[pieces : pieces + count],
        r_buf, s_buf, r_sem, s_sem, use,
    )
    for wait in waits:
        wait.wait()


SCALARS = pl.BlockSpec(memory_space=pltpu.SMEM)
ANYWHERE = pl.BlockSpec(memory_space=pl.ANY)
INSIDE = pl.BlockSpec(memory_space=pltpu.VMEM)


def product_scratch(pieces, blocks, block, width, cols):
    return [
        pltpu.VMEM((pieces, blocks, block, width), jnp.bfloat16),
        pltpu.VMEM((pieces * width, cols), jnp.bfloat16),
        pltpu.SemaphoreType.DMA((pieces, blocks)),
        pltpu.SemaphoreType.DMA((pieces,)),
    ]


def coded_product(sizes, table, r_pieces, s_pieces, target, block, first, blocks):
    pieces = len(r_pieces)
    width, cols = s_pieces[0].shape
    return pl.pallas_call(
        functools.partial(coded_kernel, sizes, target, first),
        out_shape=pltpu.VMEM((blocks, block + STRIP, cols), jnp.int16),
        in_specs=[SCALARS] + [ANYWHERE] * (pieces + len(s_pieces)),
        out_specs=INSIDE,
        scratch_shapes=product_scratch(pieces, blocks, block, width, cols),
        compiler_params=params(),
        cost_estimate=cost(2 * blocks * block * pieces * width * cols // 16, 0),
    )(table, *r_pieces, *s_pieces)


def own_product(sizes, table, order, r_pieces, s_pieces, t_pieces, block):
    pieces = len(r_pieces)
    width, cols = s_pieces[0].shape
    blocks = r_pieces[0].shape[0] // block
    return pl.pallas_call(
        functools.partial(own_kernel, sizes, len(s_pieces)),
        out_shape=[
            pltpu.VMEM((blocks, block, cols), jnp.float32),
            pltpu.VMEM((blocks, block, cols), jnp.bfloat16),
        ],
        in_specs=[SCALARS] * 2 + [ANYWHERE] * (pieces + len(s_pieces) + len(t_pieces)),
        out_specs=[INSIDE] * 2,
        scratch_shapes=product_scratch(pieces, blocks, block, width, cols)
        + [pltpu.SemaphoreType.DMA((len(t_pieces),))],
        compiler_params=params(),
        cost_estimate=cost(2 * blocks * block * pieces * width * cols // 16, 0),
    )(table, order, *r_pieces, *s_pieces, *t_pieces)


def join_kernel(parts, first, own, mirror, *refs):
    codes = refs[:parts]
    out, o_buf, gains, o_sem = refs[-4:]
    blocks, block, cols = o_buf.shape
    group = block // STRIP
    outs = []
    for n in range(blocks):
        for k in range(parts):
            level = codes[k][n, block:].astype(jnp.float32)
            gains[k] = jnp.exp2(level * (1.0 / FINE)) * (1.0 / LEVELS)
        for half in range(2):
            for g in range(half * STRIP // 2, (half + 1) * STRIP // 2):
                at = slice(g * group, (g + 1) * group)
                total = own[first + n, at]
                for k in range(parts):
                    total += codes[k][n, at].astype(jnp.float32) * gains[k, g : g + 1]
                factor = mirror[first + n, at].astype(jnp.float32)
                o_buf[n, at] = (total * factor).astype(jnp.bfloat16)
            here = pl.ds(half * block // 2, block // 2)
            rows = pl.ds((first + n) * block + half * block // 2, block // 2)
            outs.append(
                pltpu.make_async_copy(o_buf.at[n, here], out.at[rows], o_sem.at[n, half])
            )
            outs[-1].start()
    for copy in outs:
        copy.wait()


def in_vmem(values):
    return pltpu.with_memory_space_constraint(values, pltpu.VMEM)


def join(own, mirror, coded, first, before):
    steps, block, cols = own.shape
    blocks = coded[0].shape[0]
    aliases, carried = {}, ()
    if before is not None:
        aliases, carried = {2 + len(coded): 0}, (before,)
    return pl.pallas_call(
        functools.partial(join_kernel, len(coded), first),
        out_shape=jax.ShapeDtypeStruct((steps * block, cols), jnp.bfloat16),
        in_specs=[INSIDE] * (2 + len(coded)) + [ANYWHERE] * len(carried),
        out_specs=ANYWHERE,
        scratch_shapes=[
            pltpu.VMEM((blocks, block, cols), jnp.bfloat16),
            pltpu.VMEM((len(coded), STRIP, cols), jnp.float32),
            pltpu.SemaphoreType.DMA((blocks, 2)),
        ],
        input_output_aliases=aliases,
        compiler_params=params(),
        cost_estimate=cost(0, 0),
    )(own, mirror, *[in_vmem(codes) for codes in coded], *carried)


def turn_kernel(pieces, width, places, flags, t_ref, *outs):
    a_width = t_ref.shape[1]
    for e in range(pieces):

        def one(t, carry, e=e):
            start = pl.multiple_of(places[e] * width + t * BLK, BLK)
            over = pl.ds(pl.multiple_of(t * BLK, BLK), BLK)
            for u in range(a_width // BLK):
                tile = masked(
                    t_ref[pl.ds(start, BLK), u * BLK : (u + 1) * BLK],
                    flags[places[e] * (width // BLK) + t, u],
                )
                outs[e][u * BLK : (u + 1) * BLK, over] = tile.T
            return carry

        lax.fori_loop(0, width // BLK, one, 0)


def turn(places, flags, t_vals, c_width):
    pieces = t_vals.shape[0] // c_width
    shape = (t_vals.shape[1], c_width)
    return pl.pallas_call(
        functools.partial(turn_kernel, pieces, c_width),
        out_shape=[jax.ShapeDtypeStruct(shape, jnp.bfloat16)] * pieces,
        grid_spec=pltpu.PrefetchScalarGridSpec(
            num_scalar_prefetch=2,
            grid=(1,),
            in_specs=[whole(t_vals.shape)],
            out_specs=[whole(shape)] * pieces,
        ),
        compiler_params=params(),
        cost_estimate=cost(0, 4 * t_vals.size),
    )(places, flags, t_vals)


def body(n_row, n_col, r_vals, s_vals, t_vals, r_pattern, s_pattern, t_pattern):
    side = math.isqrt(n_col)
    row = lax.axis_index("row")
    col = lax.axis_index("col")
    line, kind = row // 2, row % 2
    y, x = col // side, col % side
    a_rows, b_width = r_vals.shape
    c_width = s_vals.shape[1]
    a_part = t_vals.shape[1]
    a_tiles, ap_tiles = a_rows // BLK, a_part // BLK
    along = kind == 0
    gather_at = jnp.where(along, x, y)
    target_at = jnp.where(along, y, x)
    axes = ("row", "col")

    def place(k, h, yy, xx):
        return (k * 2 + h) * n_col + yy * side + xx

    def shifted(e, gather):
        pairs = []
        for k in range(n_row // 2):
            for h in range(2):
                for yy in range(side):
                    for xx in range(side):
                        if (h == 0) == gather:
                            to = (yy, (xx + e) % side)
                        else:
                            to = ((yy + e) % side, xx)
                        pairs.append((place(k, h, yy, xx), place(k, h, *to)))
        return pairs

    r_pieces = [r_vals] + [lax.ppermute(r_vals, axes, shifted(e, True)) for e in range(1, side)]

    flat = n_col & (n_col - 1) == 0
    partner = [(col ^ e) if flat else (col + e) % n_col for e in range(n_col)]
    t_flags = lax.dynamic_slice_in_dim(t_pattern, (row * n_col + col) * ap_tiles, ap_tiles, 1)
    turned = turn(jnp.stack(partner).astype(jnp.int32), t_flags, t_vals, c_width)
    same, other = [], []
    for a in range(side):
        for b in range(side):
            for c in range(side):
                for d in range(side):
                    k = a * side + b
                    to_even = (c * side + b, 0, a, d)
                    to_odd = (a * side + d, 1, c, b)
                    same.append((place(k, 0, c, d), place(*to_even)))
                    same.append((place(k, 1, c, d), place(*to_odd)))
                    other.append((place(k, 1, c, d), place(*to_even)))
                    other.append((place(k, 0, c, d), place(*to_odd)))
    s_same = lax.ppermute(s_vals, axes, same)
    s_other = lax.ppermute(s_vals, axes, other)
    s_held = jnp.concatenate(
        [jnp.where(along, s_same, s_other), jnp.where(along, s_other, s_same)], axis=0
    )
    def along_line(values, hop):
        pairs = [(k * 2 + h, hop(k) * 2 + h) for k in range(n_col) for h in range(2)]
        return lax.ppermute(values, "row", pairs)

    if flat:
        got = {0: s_held}
        bit = n_col // 2
        while bit:
            got |= {m | bit: along_line(v, lambda k, bit=bit: k ^ bit) for m, v in got.items()}
            if len(got) == 2:
                got[bit], *turned = lax.optimization_barrier((got[bit], *turned))
            bit //= 2
        s_pieces = [got[m] for m in range(n_col)]
    else:
        s_pieces = [s_held] + [
            along_line(s_held, lambda k, d=d: (k + d) % n_col) for d in range(1, n_col)
        ]

    t_pieces = [turned[0]]
    for e in range(1, n_col):
        pairs = [(j, (j ^ e) if flat else (j + e) % n_col) for j in range(n_col)]
        t_pieces.append(lax.ppermute(turned[e], "col", pairs))

    r_flags = lax.dynamic_slice_in_dim(r_pattern, row * a_tiles, a_tiles, 0)
    flags = [r_flags.reshape(-1), s_pattern.reshape(-1)]
    sizes = (side, a_tiles, r_pattern.shape[1], s_pattern.shape[1])

    blocks, spots, targets = [], [], []
    for e in range(side):
        g = (gather_at - e) % side
        blocks.append(jnp.where(along, y * side + g, g * side + x))
    for t in range(side):
        target = (target_at + t) % side
        for e in range(side):
            g = (gather_at - e) % side
            k = jnp.where(along, target * side + g, g * side + target)
            spots.append((line ^ k) if flat else (line - k) % n_col)
        targets.append(jnp.where(along, target * side + x, y * side + target))
    table = jnp.concatenate([jnp.stack(blocks + spots + targets).astype(jnp.int32), *flags])

    block = max(a_part, math.gcd(a_rows, 4 * BLK))
    steps = a_rows // block
    chunks = 2 if steps % 2 == 0 else 1
    steps //= chunks
    coded = []
    for chunk in range(chunks):
        parts = []
        for e in range(1, side):
            codes = coded_product(
                sizes, table, r_pieces, s_pieces, e, block, chunk * steps * block, steps
            )
            if chunk:
                codes, *t_pieces[1:] = lax.optimization_barrier((codes, *t_pieces[1:]))
            parts.append(lax.ppermute(codes, axes, shifted(e, False)))
        coded.append(parts)
    order = [(col ^ o) if flat else (col - o) % n_col for o in range(n_col)]
    own, mirror = own_product(
        sizes, table, jnp.stack(order).astype(jnp.int32), r_pieces, s_pieces, t_pieces, block
    )
    own, mirror = in_vmem(own), in_vmem(mirror)
    out = None
    for chunk in range(chunks):
        out = join(own, mirror, coded[chunk], chunk * steps, out)
    return out


def solution(mesh):
    placed = (P("row", "col"), P("row", "col"), P(None, ("row", "col")), P(), P(), P())
    n_row, n_col = mesh.shape["row"], mesh.shape["col"]
    return jax.shard_map(
        functools.partial(body, n_row, n_col),
        mesh=mesh,
        in_specs=placed,
        out_specs=P("row", "col"),
        check_vma=False,
    )
```

```python
import functools
import math

import jax
import jax.numpy as jnp
from jax import lax
from jax.experimental import pallas as pl
from jax.experimental.pallas import tpu as pltpu
from jax.sharding import PartitionSpec as P

BLK = 128
STRIP = 16
LEVELS = 32767.0
FINE = 64.0
VMEM = 24 * 1024 * 1024


def masked(values, flag):
    return values * jnp.full((1, BLK), flag.astype(jnp.float32)).astype(jnp.bfloat16)


def joined_tiles(grid):
    bands = [jnp.concatenate(t, axis=1) if len(t) > 1 else t[0] for t in grid]
    return jnp.concatenate(bands, axis=0) if len(bands) > 1 else bands[0]


def whole(shape):
    return pl.BlockSpec(shape, lambda i, *_: (0,) * len(shape))


def cost(flops, bytes_accessed):
    return pl.CostEstimate(flops=flops, bytes_accessed=bytes_accessed, transcendentals=0)


def params(limit=VMEM):
    return pltpu.CompilerParams(vmem_limit_bytes=limit)


class Table:
    def __init__(self, ref, pieces, a_tiles, b_all, c_all):
        self.ref, self.pieces = ref, pieces
        self.b_all, self.c_all = b_all, c_all
        self.r_at = pieces * (pieces + 2)
        self.s_at = self.r_at + a_tiles * b_all

    def block(self, e):
        return self.ref[e]

    def spot(self, target, e):
        return self.ref[(target + 1) * self.pieces + e]

    def column(self, target):
        return self.ref[(self.pieces + 1) * self.pieces + target]

    def r_flag(self, a, b):
        return self.ref[self.r_at + a * self.b_all + b]

    def s_flag(self, b, c):
        return self.ref[self.s_at + b * self.c_all + c]


def select_copy(choice, sources, target, sem):
    for d, source in enumerate(sources):

        @pl.when(choice == d)
        def _(source=source):
            pltpu.make_async_copy(source, target, sem).start()

    return pltpu.make_async_copy(sources[0], target, sem)


def products(table, target, first, r_refs, s_refs, r_buf, s_buf, r_sem, s_sem, use):
    pieces, blocks, block, width = r_buf.shape
    cols = s_buf.shape[1]
    b_tiles, c_tiles = width // BLK, cols // BLK

    def r_copy(e, n):
        rows = pl.ds(pl.multiple_of(first + n * block, block), block)
        return pltpu.make_async_copy(r_refs[e].at[rows], r_buf.at[e, n], r_sem.at[e, n])

    waits = [
        select_copy(table.spot(target, e), s_refs, s_buf.at[pl.ds(e * width, width)], s_sem.at[e])
        for e in range(pieces)
    ]
    for n in range(blocks):
        for e in range(pieces):
            r_copy(e, n).start()
    for e in range(pieces):
        waits[e].wait()
        for t in range(b_tiles):
            for u in range(c_tiles):
                flag = table.s_flag(table.block(e) * b_tiles + t, table.column(target) * c_tiles + u)
                down = slice(e * width + t * BLK, e * width + (t + 1) * BLK)
                over = slice(u * BLK, (u + 1) * BLK)
                s_buf[down, over] = masked(s_buf[down, over], flag)

    def one(n, carry):
        for e in range(pieces):
            r_copy(e, n).wait()
        grid = []
        for t in range(block // BLK):
            a = first // BLK + n * (block // BLK) + t
            grid.append(
                [
                    masked(
                        r_buf[e, n, t * BLK : (t + 1) * BLK, u * BLK : (u + 1) * BLK],
                        table.r_flag(a, table.block(e) * b_tiles + u),
                    )
                    for e in range(pieces)
                    for u in range(b_tiles)
                ]
            )
        use(n, jnp.dot(joined_tiles(grid), s_buf[...], preferred_element_type=jnp.float32))
        return carry

    lax.fori_loop(0, blocks, one, 0)


def encode(total, out):
    rows, cols = total.shape
    group = rows // STRIP
    strip_row = lax.broadcasted_iota(jnp.int32, (STRIP, cols), 0)
    strip = jnp.zeros((STRIP, cols), jnp.float32)
    for g in range(STRIP):
        part = total[g * group : (g + 1) * group]
        top = jnp.max(jnp.max(jnp.abs(part), axis=0, keepdims=True), axis=1, keepdims=True)
        level = jnp.ceil(jnp.log2(jnp.maximum(top, 1e-30)) * FINE) + 1.0
        gain = jnp.exp2(level * (-1.0 / FINE)) * LEVELS
        code = jnp.clip(jnp.round(part * gain), -LEVELS, LEVELS)
        out[g * group : (g + 1) * group] = code.astype(jnp.int16)
        strip = jnp.where(strip_row == g, level, strip)
    out[rows:] = strip.astype(jnp.int16)


def coded_kernel(sizes, target, first, numbers, *refs):
    *ins, out, r_buf, s_buf, r_sem, s_sem = refs
    pieces = r_buf.shape[0]

    def use(n, total):
        encode(total, out.at[n])

    products(
        Table(numbers, *sizes), target, first, ins[:pieces], ins[pieces:],
        r_buf, s_buf, r_sem, s_sem, use,
    )


def own_kernel(sizes, count, numbers, order, *refs):
    *ins, out, mirror, r_buf, s_buf, r_sem, s_sem, t_sem = refs
    pieces = r_buf.shape[0]
    t_refs = ins[pieces + count :]
    blocks, block, _ = mirror.shape
    a_part = t_refs[0].shape[0]
    split = block // a_part
    waits = []
    for o in range(blocks * split):
        rows = pl.ds(o % split * a_part, a_part)
        waits.append(select_copy(order[o], t_refs, mirror.at[o // split, rows], t_sem.at[o]))

    def use(n, total):
        out[n] = total

    products(
        Table(numbers, *sizes), 0, 0, ins[:pieces], ins[pieces : pieces + count],
        r_buf, s_buf, r_sem, s_sem, use,
    )
    for wait in waits:
        wait.wait()


SCALARS = pl.BlockSpec(memory_space=pltpu.SMEM)
ANYWHERE = pl.BlockSpec(memory_space=pl.ANY)
INSIDE = pl.BlockSpec(memory_space=pltpu.VMEM)


def product_scratch(pieces, blocks, block, width, cols):
    return [
        pltpu.VMEM((pieces, blocks, block, width), jnp.bfloat16),
        pltpu.VMEM((pieces * width, cols), jnp.bfloat16),
        pltpu.SemaphoreType.DMA((pieces, blocks)),
        pltpu.SemaphoreType.DMA((pieces,)),
    ]


def coded_product(sizes, table, r_pieces, s_pieces, target, block, first, blocks):
    pieces = len(r_pieces)
    width, cols = s_pieces[0].shape
    return pl.pallas_call(
        functools.partial(coded_kernel, sizes, target, first),
        out_shape=pltpu.VMEM((blocks, block + STRIP, cols), jnp.int16),
        in_specs=[SCALARS] + [ANYWHERE] * (pieces + len(s_pieces)),
        out_specs=INSIDE,
        scratch_shapes=product_scratch(pieces, blocks, block, width, cols),
        compiler_params=params(),
        cost_estimate=cost(2 * blocks * block * pieces * width * cols // 16, 0),
    )(table, *r_pieces, *s_pieces)


def own_product(sizes, table, order, r_pieces, s_pieces, t_pieces, block):
    pieces = len(r_pieces)
    width, cols = s_pieces[0].shape
    blocks = r_pieces[0].shape[0] // block
    return pl.pallas_call(
        functools.partial(own_kernel, sizes, len(s_pieces)),
        out_shape=[
            pltpu.VMEM((blocks, block, cols), jnp.float32),
            pltpu.VMEM((blocks, block, cols), jnp.bfloat16),
        ],
        in_specs=[SCALARS] * 2 + [ANYWHERE] * (pieces + len(s_pieces) + len(t_pieces)),
        out_specs=[INSIDE] * 2,
        scratch_shapes=product_scratch(pieces, blocks, block, width, cols)
        + [pltpu.SemaphoreType.DMA((len(t_pieces),))],
        compiler_params=params(),
        cost_estimate=cost(2 * blocks * block * pieces * width * cols // 16, 0),
    )(table, order, *r_pieces, *s_pieces, *t_pieces)


def join_kernel(parts, first, own, mirror, *refs):
    codes = refs[:parts]
    out, o_buf, gains, o_sem = refs[-4:]
    blocks, block, cols = o_buf.shape
    group = block // STRIP
    outs = []
    for n in range(blocks):
        for k in range(parts):
            level = codes[k][n, block:].astype(jnp.float32)
            gains[k] = jnp.exp2(level * (1.0 / FINE)) * (1.0 / LEVELS)
        for half in range(2):
            for g in range(half * STRIP // 2, (half + 1) * STRIP // 2):
                at = slice(g * group, (g + 1) * group)
                total = own[first + n, at]
                for k in range(parts):
                    total += codes[k][n, at].astype(jnp.float32) * gains[k, g : g + 1]
                factor = mirror[first + n, at].astype(jnp.float32)
                o_buf[n, at] = (total * factor).astype(jnp.bfloat16)
            here = pl.ds(half * block // 2, block // 2)
            rows = pl.ds((first + n) * block + half * block // 2, block // 2)
            outs.append(
                pltpu.make_async_copy(o_buf.at[n, here], out.at[rows], o_sem.at[n, half])
            )
            outs[-1].start()
    for copy in outs:
        copy.wait()


def in_vmem(values):
    return pltpu.with_memory_space_constraint(values, pltpu.VMEM)


def join(own, mirror, coded, first, before):
    steps, block, cols = own.shape
    blocks = coded[0].shape[0]
    aliases, carried = {}, ()
    if before is not None:
        aliases, carried = {2 + len(coded): 0}, (before,)
    return pl.pallas_call(
        functools.partial(join_kernel, len(coded), first),
        out_shape=jax.ShapeDtypeStruct((steps * block, cols), jnp.bfloat16),
        in_specs=[INSIDE] * (2 + len(coded)) + [ANYWHERE] * len(carried),
        out_specs=ANYWHERE,
        scratch_shapes=[
            pltpu.VMEM((blocks, block, cols), jnp.bfloat16),
            pltpu.VMEM((len(coded), STRIP, cols), jnp.float32),
            pltpu.SemaphoreType.DMA((blocks, 2)),
        ],
        input_output_aliases=aliases,
        compiler_params=params(),
        cost_estimate=cost(0, 0),
    )(own, mirror, *[in_vmem(codes) for codes in coded], *carried)


def turn_kernel(pieces, width, places, flags, t_ref, *outs):
    a_width = t_ref.shape[1]
    for e in range(pieces):

        def one(t, carry, e=e):
            start = pl.multiple_of(places[e] * width + t * BLK, BLK)
            over = pl.ds(pl.multiple_of(t * BLK, BLK), BLK)
            for u in range(a_width // BLK):
                tile = masked(
                    t_ref[pl.ds(start, BLK), u * BLK : (u + 1) * BLK],
                    flags[places[e] * (width // BLK) + t, u],
                )
                outs[e][u * BLK : (u + 1) * BLK, over] = tile.T
            return carry

        lax.fori_loop(0, width // BLK, one, 0)


def turn(places, flags, t_vals, c_width):
    pieces = t_vals.shape[0] // c_width
    shape = (t_vals.shape[1], c_width)
    return pl.pallas_call(
        functools.partial(turn_kernel, pieces, c_width),
        out_shape=[jax.ShapeDtypeStruct(shape, jnp.bfloat16)] * pieces,
        grid_spec=pltpu.PrefetchScalarGridSpec(
            num_scalar_prefetch=2,
            grid=(1,),
            in_specs=[whole(t_vals.shape)],
            out_specs=[whole(shape)] * pieces,
        ),
        compiler_params=params(),
        cost_estimate=cost(0, 4 * t_vals.size),
    )(places, flags, t_vals)


def body(n_row, n_col, r_vals, s_vals, t_vals, r_pattern, s_pattern, t_pattern):
    side = math.isqrt(n_col)
    row = lax.axis_index("row")
    col = lax.axis_index("col")
    line, kind = row // 2, row % 2
    y, x = col // side, col % side
    a_rows, b_width = r_vals.shape
    c_width = s_vals.shape[1]
    a_part = t_vals.shape[1]
    a_tiles, ap_tiles = a_rows // BLK, a_part // BLK
    along = kind == 1
    gather_at = jnp.where(along, x, y)
    target_at = jnp.where(along, y, x)
    axes = ("row", "col")

    def place(k, h, yy, xx):
        return (k * 2 + h) * n_col + yy * side + xx

    def shifted(e, gather):
        pairs = []
        for k in range(n_row // 2):
            for h in range(2):
                for yy in range(side):
                    for xx in range(side):
                        if (h == 1) == gather:
                            to = (yy, (xx + e) % side)
                        else:
                            to = ((yy + e) % side, xx)
                        pairs.append((place(k, h, yy, xx), place(k, h, *to)))
        return pairs

    r_pieces = [r_vals] + [lax.ppermute(r_vals, axes, shifted(e, True)) for e in range(1, side)]

    flat = n_col & (n_col - 1) == 0
    partner = [(col ^ e) if flat else (col + e) % n_col for e in range(n_col)]
    t_flags = lax.dynamic_slice_in_dim(t_pattern, (row * n_col + col) * ap_tiles, ap_tiles, 1)
    turned = turn(jnp.stack(partner).astype(jnp.int32), t_flags, t_vals, c_width)
    same, other = [], []
    for a in range(side):
        for b in range(side):
            for c in range(side):
                for d in range(side):
                    k = a * side + b
                    to_odd = (c * side + b, 1, a, d)
                    to_even = (a * side + d, 0, c, b)
                    same.append((place(k, 0, c, d), place(*to_even)))
                    same.append((place(k, 1, c, d), place(*to_odd)))
                    other.append((place(k, 1, c, d), place(*to_even)))
                    other.append((place(k, 0, c, d), place(*to_odd)))
    s_same = lax.ppermute(s_vals, axes, same)
    s_other = lax.ppermute(s_vals, axes, other)
    s_held = jnp.concatenate(
        [jnp.where(along, s_other, s_same), jnp.where(along, s_same, s_other)], axis=0
    )

    def along_line(values, hop):
        pairs = [(k * 2 + h, hop(k) * 2 + h) for k in range(n_col) for h in range(2)]
        return lax.ppermute(values, "row", pairs)

    if flat:
        got = {0: s_held}
        bit = n_col // 2
        while bit:
            got |= {m | bit: along_line(v, lambda k, bit=bit: k ^ bit) for m, v in got.items()}
            if len(got) == 2:
                got[bit], *turned = lax.optimization_barrier((got[bit], *turned))
            bit //= 2
        s_pieces = [got[m] for m in range(n_col)]
    else:
        s_pieces = [s_held] + [
            along_line(s_held, lambda k, d=d: (k + d) % n_col) for d in range(1, n_col)
        ]

    t_pieces = [turned[0]]
    for e in range(1, n_col):
        pairs = [(j, (j ^ e) if flat else (j + e) % n_col) for j in range(n_col)]
        t_pieces.append(lax.ppermute(turned[e], "col", pairs))

    r_flags = lax.dynamic_slice_in_dim(r_pattern, row * a_tiles, a_tiles, 0)
    flags = [r_flags.reshape(-1), s_pattern.reshape(-1)]
    sizes = (side, a_tiles, r_pattern.shape[1], s_pattern.shape[1])

    blocks, spots, targets = [], [], []
    for e in range(side):
        g = (gather_at - e) % side
        blocks.append(jnp.where(along, y * side + g, g * side + x))
    for t in range(side):
        target = (target_at + t) % side
        for e in range(side):
            g = (gather_at - e) % side
            k = jnp.where(along, target * side + g, g * side + target)
            spots.append((line ^ k) if flat else (line - k) % n_col)
        targets.append(jnp.where(along, target * side + x, y * side + target))
    table = jnp.concatenate([jnp.stack(blocks + spots + targets).astype(jnp.int32), *flags])

    block = max(a_part, math.gcd(a_rows, 4 * BLK))
    steps = a_rows // block
    chunks = 2 if steps % 2 == 0 else 1
    steps //= chunks
    coded = []
    for chunk in range(chunks):
        parts = []
        for e in range(1, side):
            codes = coded_product(
                sizes, table, r_pieces, s_pieces, e, block, chunk * steps * block, steps
            )
            if chunk:
                codes, *t_pieces[1:] = lax.optimization_barrier((codes, *t_pieces[1:]))
            parts.append(lax.ppermute(codes, axes, shifted(e, False)))
        coded.append(parts)
    order = [(col ^ o) if flat else (col - o) % n_col for o in range(n_col)]
    own, mirror = own_product(
        sizes, table, jnp.stack(order).astype(jnp.int32), r_pieces, s_pieces, t_pieces, block
    )
    own, mirror = in_vmem(own), in_vmem(mirror)
    out = None
    for chunk in range(chunks):
        out = join(own, mirror, coded[chunk], chunk * steps, out)
    return out


def plain_body(r_vals, s_vals, t_vals, r_pattern, s_pattern, t_pattern):
    row, col = lax.axis_index("row"), lax.axis_index("col")
    s_all = lax.all_gather(s_vals, "row", axis=0, tiled=True)
    r_all = lax.all_gather(r_vals, "col", axis=1, tiled=True)
    t_all = lax.all_to_all(t_vals, "col", split_axis=0, concat_axis=1, tiled=True)
    a_tiles, c_tiles = r_vals.shape[0] // BLK, s_vals.shape[1] // BLK

    def spread(flags):
        return jnp.repeat(jnp.repeat(flags.astype(jnp.bfloat16), BLK, axis=0), BLK, axis=1)

    r_flags = lax.dynamic_slice_in_dim(r_pattern, row * a_tiles, a_tiles, 0)
    s_flags = lax.dynamic_slice_in_dim(s_pattern, col * c_tiles, c_tiles, 1)
    t_flags = lax.dynamic_slice(t_pattern, (col * c_tiles, row * a_tiles), (c_tiles, a_tiles))
    paths = jnp.dot(
        r_all * spread(r_flags), s_all * spread(s_flags), preferred_element_type=jnp.float32
    )
    mirror = (t_all * spread(t_flags)).T
    return (paths * mirror.astype(jnp.float32)).astype(jnp.bfloat16)


def solution(mesh):
    placed = (P("row", "col"), P("row", "col"), P(None, ("row", "col")), P(), P(), P())
    n_row, n_col = mesh.shape["row"], mesh.shape["col"]
    fits = n_row == 2 * n_col and math.isqrt(n_col) ** 2 == n_col > 1
    return jax.shard_map(
        functools.partial(body, n_row, n_col) if fits else plain_body,
        mesh=mesh,
        in_specs=placed,
        out_specs=P("row", "col"),
        check_vma=False,
    )
```

```python
import functools
import math

import jax
import jax.numpy as jnp
from jax import lax
from jax.experimental import pallas as pl
from jax.experimental.pallas import tpu as pltpu
from jax.sharding import PartitionSpec as P

BLK = 128
STRIP = 16
LEVELS = 32767.0
FINE = 64.0
VMEM = 24 * 1024 * 1024


def masked(values, flag):
    return values * jnp.full((1, BLK), flag.astype(jnp.float32)).astype(jnp.bfloat16)


def joined_tiles(grid):
    bands = [jnp.concatenate(t, axis=1) if len(t) > 1 else t[0] for t in grid]
    return jnp.concatenate(bands, axis=0) if len(bands) > 1 else bands[0]


def whole(shape):
    return pl.BlockSpec(shape, lambda i, *_: (0,) * len(shape))


def cost(flops, bytes_accessed):
    return pl.CostEstimate(flops=flops, bytes_accessed=bytes_accessed, transcendentals=0)


def params(limit=VMEM):
    return pltpu.CompilerParams(vmem_limit_bytes=limit)


class Table:
    def __init__(self, ref, pieces, a_tiles, b_all, c_all):
        self.ref, self.pieces = ref, pieces
        self.b_all, self.c_all = b_all, c_all
        self.r_at = pieces * (pieces + 2)
        self.s_at = self.r_at + a_tiles * b_all

    def block(self, e):
        return self.ref[e]

    def spot(self, target, e):
        return self.ref[(target + 1) * self.pieces + e]

    def column(self, target):
        return self.ref[(self.pieces + 1) * self.pieces + target]

    def r_flag(self, a, b):
        return self.ref[self.r_at + a * self.b_all + b]

    def s_flag(self, b, c):
        return self.ref[self.s_at + b * self.c_all + c]


def select_copy(choice, sources, target, sem):
    for d, source in enumerate(sources):

        @pl.when(choice == d)
        def _(source=source):
            pltpu.make_async_copy(source, target, sem).start()

    return pltpu.make_async_copy(sources[0], target, sem)


def products(table, target, first, r_refs, s_refs, r_buf, s_buf, r_sem, s_sem, use):
    pieces, blocks, block, width = r_buf.shape
    cols = s_buf.shape[1]
    b_tiles, c_tiles = width // BLK, cols // BLK

    def r_copy(e, n):
        rows = pl.ds(pl.multiple_of(first + n * block, block), block)
        return pltpu.make_async_copy(r_refs[e].at[rows], r_buf.at[e, n], r_sem.at[e, n])

    waits = [
        select_copy(table.spot(target, e), s_refs, s_buf.at[pl.ds(e * width, width)], s_sem.at[e])
        for e in range(pieces)
    ]
    for n in range(blocks):
        for e in range(pieces):
            r_copy(e, n).start()
    for e in range(pieces):
        waits[e].wait()
        for t in range(b_tiles):
            for u in range(c_tiles):
                flag = table.s_flag(table.block(e) * b_tiles + t, table.column(target) * c_tiles + u)
                down = slice(e * width + t * BLK, e * width + (t + 1) * BLK)
                over = slice(u * BLK, (u + 1) * BLK)
                s_buf[down, over] = masked(s_buf[down, over], flag)

    def one(n, carry):
        for e in range(pieces):
            r_copy(e, n).wait()
        grid = []
        for t in range(block // BLK):
            a = first // BLK + n * (block // BLK) + t
            grid.append(
                [
                    masked(
                        r_buf[e, n, t * BLK : (t + 1) * BLK, u * BLK : (u + 1) * BLK],
                        table.r_flag(a, table.block(e) * b_tiles + u),
                    )
                    for e in range(pieces)
                    for u in range(b_tiles)
                ]
            )
        use(n, jnp.dot(joined_tiles(grid), s_buf[...], preferred_element_type=jnp.float32))
        return carry

    lax.fori_loop(0, blocks, one, 0)


def encode(total, out):
    rows, cols = total.shape
    group = rows // STRIP
    strip_row = lax.broadcasted_iota(jnp.int32, (STRIP, cols), 0)
    strip = jnp.zeros((STRIP, cols), jnp.float32)
    for g in range(STRIP):
        part = total[g * group : (g + 1) * group]
        top = jnp.max(jnp.max(jnp.abs(part), axis=0, keepdims=True), axis=1, keepdims=True)
        level = jnp.ceil(jnp.log2(jnp.maximum(top, 1e-30)) * FINE) + 1.0
        gain = jnp.exp2(level * (-1.0 / FINE)) * LEVELS
        code = jnp.clip(jnp.round(part * gain), -LEVELS, LEVELS)
        out[g * group : (g + 1) * group] = code.astype(jnp.int16)
        strip = jnp.where(strip_row == g, level, strip)
    out[rows:] = strip.astype(jnp.int16)


def coded_kernel(sizes, target, first, numbers, *refs):
    *ins, out, r_buf, s_buf, r_sem, s_sem = refs
    pieces = r_buf.shape[0]

    def use(n, total):
        encode(total, out.at[n])

    products(
        Table(numbers, *sizes), target, first, ins[:pieces], ins[pieces:],
        r_buf, s_buf, r_sem, s_sem, use,
    )


def own_kernel(sizes, count, numbers, order, *refs):
    *ins, out, mirror, r_buf, s_buf, r_sem, s_sem, t_sem = refs
    pieces = r_buf.shape[0]
    t_refs = ins[pieces + count :]
    blocks, block, _ = mirror.shape
    a_part = t_refs[0].shape[0]
    split = block // a_part
    waits = []
    for o in range(blocks * split):
        rows = pl.ds(o % split * a_part, a_part)
        waits.append(select_copy(order[o], t_refs, mirror.at[o // split, rows], t_sem.at[o]))

    def use(n, total):
        out[n] = total

    products(
        Table(numbers, *sizes), 0, 0, ins[:pieces], ins[pieces : pieces + count],
        r_buf, s_buf, r_sem, s_sem, use,
    )
    for wait in waits:
        wait.wait()


SCALARS = pl.BlockSpec(memory_space=pltpu.SMEM)
ANYWHERE = pl.BlockSpec(memory_space=pl.ANY)
INSIDE = pl.BlockSpec(memory_space=pltpu.VMEM)


def product_scratch(pieces, blocks, block, width, cols):
    return [
        pltpu.VMEM((pieces, blocks, block, width), jnp.bfloat16),
        pltpu.VMEM((pieces * width, cols), jnp.bfloat16),
        pltpu.SemaphoreType.DMA((pieces, blocks)),
        pltpu.SemaphoreType.DMA((pieces,)),
    ]


def coded_product(sizes, table, r_pieces, s_pieces, target, block, first, blocks):
    pieces = len(r_pieces)
    width, cols = s_pieces[0].shape
    return pl.pallas_call(
        functools.partial(coded_kernel, sizes, target, first),
        out_shape=pltpu.VMEM((blocks, block + STRIP, cols), jnp.int16),
        in_specs=[SCALARS] + [ANYWHERE] * (pieces + len(s_pieces)),
        out_specs=INSIDE,
        scratch_shapes=product_scratch(pieces, blocks, block, width, cols),
        compiler_params=params(),
        cost_estimate=cost(2 * blocks * block * pieces * width * cols // 16, 0),
    )(table, *r_pieces, *s_pieces)


def own_product(sizes, table, order, r_pieces, s_pieces, t_pieces, block):
    pieces = len(r_pieces)
    width, cols = s_pieces[0].shape
    blocks = r_pieces[0].shape[0] // block
    return pl.pallas_call(
        functools.partial(own_kernel, sizes, len(s_pieces)),
        out_shape=[
            pltpu.VMEM((blocks, block, cols), jnp.float32),
            pltpu.VMEM((blocks, block, cols), jnp.bfloat16),
        ],
        in_specs=[SCALARS] * 2 + [ANYWHERE] * (pieces + len(s_pieces) + len(t_pieces)),
        out_specs=[INSIDE] * 2,
        scratch_shapes=product_scratch(pieces, blocks, block, width, cols)
        + [pltpu.SemaphoreType.DMA((len(t_pieces),))],
        compiler_params=params(),
        cost_estimate=cost(2 * blocks * block * pieces * width * cols // 16, 0),
    )(table, order, *r_pieces, *s_pieces, *t_pieces)


def join_kernel(parts, first, own, mirror, *refs):
    codes = refs[:parts]
    out, o_buf, gains, o_sem = refs[-4:]
    blocks, block, cols = o_buf.shape
    group = block // STRIP
    outs = []
    for n in range(blocks):
        for k in range(parts):
            level = codes[k][n, block:].astype(jnp.float32)
            gains[k] = jnp.exp2(level * (1.0 / FINE)) * (1.0 / LEVELS)
        for half in range(2):
            for g in range(half * STRIP // 2, (half + 1) * STRIP // 2):
                at = slice(g * group, (g + 1) * group)
                total = own[first + n, at]
                for k in range(parts):
                    total += codes[k][n, at].astype(jnp.float32) * gains[k, g : g + 1]
                factor = mirror[first + n, at].astype(jnp.float32)
                o_buf[n, at] = (total * factor).astype(jnp.bfloat16)
            here = pl.ds(half * block // 2, block // 2)
            rows = pl.ds((first + n) * block + half * block // 2, block // 2)
            outs.append(
                pltpu.make_async_copy(o_buf.at[n, here], out.at[rows], o_sem.at[n, half])
            )
            outs[-1].start()
    for copy in outs:
        copy.wait()


def in_vmem(values):
    return pltpu.with_memory_space_constraint(values, pltpu.VMEM)


def join(own, mirror, coded, first, before):
    steps, block, cols = own.shape
    blocks = coded[0].shape[0]
    aliases, carried = {}, ()
    if before is not None:
        aliases, carried = {2 + len(coded): 0}, (before,)
    return pl.pallas_call(
        functools.partial(join_kernel, len(coded), first),
        out_shape=jax.ShapeDtypeStruct((steps * block, cols), jnp.bfloat16),
        in_specs=[INSIDE] * (2 + len(coded)) + [ANYWHERE] * len(carried),
        out_specs=ANYWHERE,
        scratch_shapes=[
            pltpu.VMEM((blocks, block, cols), jnp.bfloat16),
            pltpu.VMEM((len(coded), STRIP, cols), jnp.float32),
            pltpu.SemaphoreType.DMA((blocks, 2)),
        ],
        input_output_aliases=aliases,
        compiler_params=params(),
        cost_estimate=cost(0, 0),
    )(own, mirror, *[in_vmem(codes) for codes in coded], *carried)


def turn_kernel(pieces, width, places, flags, t_ref, *outs):
    a_width = t_ref.shape[1]
    for e in range(pieces):

        def one(t, carry, e=e):
            start = pl.multiple_of(places[e] * width + t * BLK, BLK)
            over = pl.ds(pl.multiple_of(t * BLK, BLK), BLK)
            for u in range(a_width // BLK):
                tile = masked(
                    t_ref[pl.ds(start, BLK), u * BLK : (u + 1) * BLK],
                    flags[places[e] * (width // BLK) + t, u],
                )
                outs[e][u * BLK : (u + 1) * BLK, over] = tile.T
            return carry

        lax.fori_loop(0, width // BLK, one, 0)


def turn(places, flags, t_vals, c_width):
    pieces = t_vals.shape[0] // c_width
    shape = (t_vals.shape[1], c_width)
    return pl.pallas_call(
        functools.partial(turn_kernel, pieces, c_width),
        out_shape=[jax.ShapeDtypeStruct(shape, jnp.bfloat16)] * pieces,
        grid_spec=pltpu.PrefetchScalarGridSpec(
            num_scalar_prefetch=2,
            grid=(1,),
            in_specs=[whole(t_vals.shape)],
            out_specs=[whole(shape)] * pieces,
        ),
        compiler_params=params(),
        cost_estimate=cost(0, 4 * t_vals.size),
    )(places, flags, t_vals)


def body(n_row, n_col, r_vals, s_vals, t_vals, r_pattern, s_pattern, t_pattern):
    side = math.isqrt(n_col)
    row = lax.axis_index("row")
    col = lax.axis_index("col")
    line, kind = row // 2, row % 2
    y, x = col // side, col % side
    a_rows, b_width = r_vals.shape
    c_width = s_vals.shape[1]
    a_part = t_vals.shape[1]
    a_tiles, ap_tiles = a_rows // BLK, a_part // BLK
    along = kind == 1
    gather_at = jnp.where(along, x, y)
    target_at = jnp.where(along, y, x)
    axes = ("row", "col")

    def place(k, h, yy, xx):
        return (k * 2 + h) * n_col + yy * side + xx

    def shifted(e, gather):
        pairs = []
        for k in range(n_row // 2):
            for h in range(2):
                for yy in range(side):
                    for xx in range(side):
                        if (h == 1) == gather:
                            to = (yy, (xx + e) % side)
                        else:
                            to = ((yy + e) % side, xx)
                        pairs.append((place(k, h, yy, xx), place(k, h, *to)))
        return pairs

    r_pieces = [r_vals] + [lax.ppermute(r_vals, axes, shifted(e, True)) for e in range(1, side)]

    flat = n_col & (n_col - 1) == 0
    partner = [(col ^ e) if flat else (col + e) % n_col for e in range(n_col)]
    t_flags = lax.dynamic_slice_in_dim(t_pattern, (row * n_col + col) * ap_tiles, ap_tiles, 1)
    turned = turn(jnp.stack(partner).astype(jnp.int32), t_flags, t_vals, c_width)
    same, other, switched, moved, crossed = [], [], [], [], []
    for a in range(side):
        for b in range(side):
            for c in range(side):
                for d in range(side):
                    k = a * side + b
                    to_odd = (c * side + b, 1, a, d)
                    to_even = (a * side + d, 0, c, b)
                    same.append((place(k, 0, c, d), place(*to_even)))
                    same.append((place(k, 1, c, d), place(*to_odd)))
                    other.append((place(k, 1, c, d), place(*to_even)))
                    other.append((place(k, 0, c, d), place(*to_odd)))
                    if a == c:
                        switched.append(other[-1])
                    else:
                        half_way = place(c * side + b, 0, c, d)
                        moved.append((place(k, 0, c, d), half_way))
                        crossed.append((half_way, place(*to_odd)))
                    if b == d:
                        switched.append(other[-2])
                    else:
                        half_way = place(a * side + d, 1, c, d)
                        moved.append((place(k, 1, c, d), half_way))
                        crossed.append((half_way, place(*to_even)))
    s_same = lax.ppermute(s_vals, axes, same)
    if side == 2:
        s_moved = lax.ppermute(lax.ppermute(s_vals, axes, moved), axes, crossed)
        stays = jnp.where(along, line // side == y, line % side == x)
        s_other = jnp.where(stays, lax.ppermute(s_vals, axes, switched), s_moved)
    else:
        s_other = lax.ppermute(s_vals, axes, other)
    s_held = jnp.concatenate(
        [jnp.where(along, s_other, s_same), jnp.where(along, s_same, s_other)], axis=0
    )

    def along_line(values, hop):
        pairs = [(k * 2 + h, hop(k) * 2 + h) for k in range(n_col) for h in range(2)]
        return lax.ppermute(values, "row", pairs)

    if flat:
        got = {0: s_held}
        bit = n_col // 2
        while bit:
            got |= {m | bit: along_line(v, lambda k, bit=bit: k ^ bit) for m, v in got.items()}
            if len(got) == 2:
                got[bit], *turned = lax.optimization_barrier((got[bit], *turned))
            bit //= 2
        s_pieces = [got[m] for m in range(n_col)]
    else:
        s_pieces = [s_held] + [
            along_line(s_held, lambda k, d=d: (k + d) % n_col) for d in range(1, n_col)
        ]

    t_pieces = [turned[0]]
    for e in range(1, n_col):
        pairs = [(j, (j ^ e) if flat else (j + e) % n_col) for j in range(n_col)]
        t_pieces.append(lax.ppermute(turned[e], "col", pairs))

    r_flags = lax.dynamic_slice_in_dim(r_pattern, row * a_tiles, a_tiles, 0)
    flags = [r_flags.reshape(-1), s_pattern.reshape(-1)]
    sizes = (side, a_tiles, r_pattern.shape[1], s_pattern.shape[1])

    blocks, spots, targets = [], [], []
    for e in range(side):
        g = (gather_at - e) % side
        blocks.append(jnp.where(along, y * side + g, g * side + x))
    for t in range(side):
        target = (target_at + t) % side
        for e in range(side):
            g = (gather_at - e) % side
            k = jnp.where(along, target * side + g, g * side + target)
            spots.append((line ^ k) if flat else (line - k) % n_col)
        targets.append(jnp.where(along, target * side + x, y * side + target))
    table = jnp.concatenate([jnp.stack(blocks + spots + targets).astype(jnp.int32), *flags])

    block = max(a_part, math.gcd(a_rows, 4 * BLK))
    steps = a_rows // block
    chunks = 2 if steps % 2 == 0 else 1
    steps //= chunks
    coded = []
    for chunk in range(chunks):
        parts = []
        for e in range(1, side):
            codes = coded_product(
                sizes, table, r_pieces, s_pieces, e, block, chunk * steps * block, steps
            )
            if chunk:
                codes, *t_pieces[1:] = lax.optimization_barrier((codes, *t_pieces[1:]))
            parts.append(lax.ppermute(codes, axes, shifted(e, False)))
        coded.append(parts)
    order = [(col ^ o) if flat else (col - o) % n_col for o in range(n_col)]
    own, mirror = own_product(
        sizes, table, jnp.stack(order).astype(jnp.int32), r_pieces, s_pieces, t_pieces, block
    )
    own, mirror = in_vmem(own), in_vmem(mirror)
    out = None
    for chunk in range(chunks):
        out = join(own, mirror, coded[chunk], chunk * steps, out)
    return out


def plain_body(r_vals, s_vals, t_vals, r_pattern, s_pattern, t_pattern):
    row, col = lax.axis_index("row"), lax.axis_index("col")
    s_all = lax.all_gather(s_vals, "row", axis=0, tiled=True)
    r_all = lax.all_gather(r_vals, "col", axis=1, tiled=True)
    t_all = lax.all_to_all(t_vals, "col", split_axis=0, concat_axis=1, tiled=True)
    a_tiles, c_tiles = r_vals.shape[0] // BLK, s_vals.shape[1] // BLK

    def spread(flags):
        return jnp.repeat(jnp.repeat(flags.astype(jnp.bfloat16), BLK, axis=0), BLK, axis=1)

    r_flags = lax.dynamic_slice_in_dim(r_pattern, row * a_tiles, a_tiles, 0)
    s_flags = lax.dynamic_slice_in_dim(s_pattern, col * c_tiles, c_tiles, 1)
    t_flags = lax.dynamic_slice(t_pattern, (col * c_tiles, row * a_tiles), (c_tiles, a_tiles))
    paths = jnp.dot(
        r_all * spread(r_flags), s_all * spread(s_flags), preferred_element_type=jnp.float32
    )
    mirror = (t_all * spread(t_flags)).T
    return (paths * mirror.astype(jnp.float32)).astype(jnp.bfloat16)


def solution(mesh):
    placed = (P("row", "col"), P("row", "col"), P(None, ("row", "col")), P(), P(), P())
    n_row, n_col = mesh.shape["row"], mesh.shape["col"]
    fits = n_row == 2 * n_col and math.isqrt(n_col) ** 2 == n_col > 1
    return jax.shard_map(
        functools.partial(body, n_row, n_col) if fits else plain_body,
        mesh=mesh,
        in_specs=placed,
        out_specs=P("row", "col"),
        check_vma=False,
    )
```

```python
import functools
import math

import jax
import jax.numpy as jnp
from jax import lax
from jax.experimental import pallas as pl
from jax.experimental.pallas import tpu as pltpu
from jax.sharding import PartitionSpec as P

BLK = 128
STRIP = 16
LEVELS = 32767.0
FINE = 64.0
VMEM = 24 * 1024 * 1024


def masked(values, flag):
    return values * jnp.full((1, BLK), flag.astype(jnp.float32)).astype(jnp.bfloat16)


def joined_tiles(grid):
    bands = [jnp.concatenate(t, axis=1) if len(t) > 1 else t[0] for t in grid]
    return jnp.concatenate(bands, axis=0) if len(bands) > 1 else bands[0]


def whole(shape):
    return pl.BlockSpec(shape, lambda i, *_: (0,) * len(shape))


def cost(flops, bytes_accessed):
    return pl.CostEstimate(flops=flops, bytes_accessed=bytes_accessed, transcendentals=0)


def params(limit=VMEM):
    return pltpu.CompilerParams(vmem_limit_bytes=limit)


class Table:
    def __init__(self, ref, pieces, a_tiles, b_all, c_all):
        self.ref, self.pieces = ref, pieces
        self.b_all, self.c_all = b_all, c_all
        self.r_at = pieces * (pieces + 2)
        self.s_at = self.r_at + a_tiles * b_all

    def block(self, e):
        return self.ref[e]

    def spot(self, target, e):
        return self.ref[(target + 1) * self.pieces + e]

    def column(self, target):
        return self.ref[(self.pieces + 1) * self.pieces + target]

    def r_flag(self, a, b):
        return self.ref[self.r_at + a * self.b_all + b]

    def s_flag(self, b, c):
        return self.ref[self.s_at + b * self.c_all + c]


def select_copy(choice, sources, target, sem):
    for d, source in enumerate(sources):

        @pl.when(choice == d)
        def _(source=source):
            pltpu.make_async_copy(source, target, sem).start()

    return pltpu.make_async_copy(sources[0], target, sem)


def products(table, target, first, r_refs, s_refs, r_buf, s_buf, r_sem, s_sem, use):
    pieces, blocks, block, width = r_buf.shape
    cols = s_buf.shape[1]
    b_tiles, c_tiles = width // BLK, cols // BLK

    def r_copy(e, n):
        rows = pl.ds(pl.multiple_of(first + n * block, block), block)
        return pltpu.make_async_copy(r_refs[e].at[rows], r_buf.at[e, n], r_sem.at[e, n])

    waits = [
        select_copy(table.spot(target, e), s_refs, s_buf.at[pl.ds(e * width, width)], s_sem.at[e])
        for e in range(pieces)
    ]
    for n in range(blocks):
        for e in range(pieces):
            r_copy(e, n).start()
    for e in range(pieces):
        waits[e].wait()
        for t in range(b_tiles):
            for u in range(c_tiles):
                flag = table.s_flag(table.block(e) * b_tiles + t, table.column(target) * c_tiles + u)
                down = slice(e * width + t * BLK, e * width + (t + 1) * BLK)
                over = slice(u * BLK, (u + 1) * BLK)
                s_buf[down, over] = masked(s_buf[down, over], flag)

    def one(n, carry):
        for e in range(pieces):
            r_copy(e, n).wait()
        grid = []
        for t in range(block // BLK):
            a = first // BLK + n * (block // BLK) + t
            grid.append(
                [
                    masked(
                        r_buf[e, n, t * BLK : (t + 1) * BLK, u * BLK : (u + 1) * BLK],
                        table.r_flag(a, table.block(e) * b_tiles + u),
                    )
                    for e in range(pieces)
                    for u in range(b_tiles)
                ]
            )
        use(n, jnp.dot(joined_tiles(grid), s_buf[...], preferred_element_type=jnp.float32))
        return carry

    lax.fori_loop(0, blocks, one, 0)


def encode(total, out):
    rows, cols = total.shape
    group = rows // STRIP
    strip_row = lax.broadcasted_iota(jnp.int32, (STRIP, cols), 0)
    strip = jnp.zeros((STRIP, cols), jnp.float32)
    for g in range(STRIP):
        part = total[g * group : (g + 1) * group]
        top = jnp.max(jnp.max(jnp.abs(part), axis=0, keepdims=True), axis=1, keepdims=True)
        level = jnp.ceil(jnp.log2(jnp.maximum(top, 1e-37)) * FINE) + 1.0
        root = jnp.exp2(level * (-0.5 / FINE))
        code = jnp.clip(jnp.round(part * root * (root * LEVELS)), -LEVELS, LEVELS)
        out[g * group : (g + 1) * group] = code.astype(jnp.int16)
        strip = jnp.where(strip_row == g, level, strip)
    out[rows:] = strip.astype(jnp.int16)


def coded_kernel(sizes, target, first, numbers, *refs):
    *ins, out, r_buf, s_buf, r_sem, s_sem = refs
    pieces = r_buf.shape[0]

    def use(n, total):
        encode(total, out.at[n])

    products(
        Table(numbers, *sizes), target, first, ins[:pieces], ins[pieces:],
        r_buf, s_buf, r_sem, s_sem, use,
    )


def own_kernel(sizes, count, numbers, order, *refs):
    *ins, out, mirror, r_buf, s_buf, r_sem, s_sem, t_sem = refs
    pieces = r_buf.shape[0]
    t_refs = ins[pieces + count :]
    blocks, block, _ = mirror.shape
    a_part = t_refs[0].shape[0]
    split = block // a_part
    waits = []
    for o in range(blocks * split):
        rows = pl.ds(o % split * a_part, a_part)
        waits.append(select_copy(order[o], t_refs, mirror.at[o // split, rows], t_sem.at[o]))

    def use(n, total):
        out[n] = total

    products(
        Table(numbers, *sizes), 0, 0, ins[:pieces], ins[pieces : pieces + count],
        r_buf, s_buf, r_sem, s_sem, use,
    )
    for wait in waits:
        wait.wait()


SCALARS = pl.BlockSpec(memory_space=pltpu.SMEM)
ANYWHERE = pl.BlockSpec(memory_space=pl.ANY)
INSIDE = pl.BlockSpec(memory_space=pltpu.VMEM)


def product_scratch(pieces, blocks, block, width, cols):
    return [
        pltpu.VMEM((pieces, blocks, block, width), jnp.bfloat16),
        pltpu.VMEM((pieces * width, cols), jnp.bfloat16),
        pltpu.SemaphoreType.DMA((pieces, blocks)),
        pltpu.SemaphoreType.DMA((pieces,)),
    ]


def coded_product(sizes, table, r_pieces, s_pieces, target, block, first, blocks):
    pieces = len(r_pieces)
    width, cols = s_pieces[0].shape
    return pl.pallas_call(
        functools.partial(coded_kernel, sizes, target, first),
        out_shape=pltpu.VMEM((blocks, block + STRIP, cols), jnp.int16),
        in_specs=[SCALARS] + [ANYWHERE] * (pieces + len(s_pieces)),
        out_specs=INSIDE,
        scratch_shapes=product_scratch(pieces, blocks, block, width, cols),
        compiler_params=params(),
        cost_estimate=cost(2 * blocks * block * pieces * width * cols // 16, 0),
    )(table, *r_pieces, *s_pieces)


def own_product(sizes, table, order, r_pieces, s_pieces, t_pieces, block):
    pieces = len(r_pieces)
    width, cols = s_pieces[0].shape
    blocks = r_pieces[0].shape[0] // block
    return pl.pallas_call(
        functools.partial(own_kernel, sizes, len(s_pieces)),
        out_shape=[
            pltpu.VMEM((blocks, block, cols), jnp.float32),
            pltpu.VMEM((blocks, block, cols), jnp.bfloat16),
        ],
        in_specs=[SCALARS] * 2 + [ANYWHERE] * (pieces + len(s_pieces) + len(t_pieces)),
        out_specs=[INSIDE] * 2,
        scratch_shapes=product_scratch(pieces, blocks, block, width, cols)
        + [pltpu.SemaphoreType.DMA((len(t_pieces),))],
        compiler_params=params(),
        cost_estimate=cost(2 * blocks * block * pieces * width * cols // 16, 0),
    )(table, order, *r_pieces, *s_pieces, *t_pieces)


def join_kernel(parts, first, own, mirror, *refs):
    codes = refs[:parts]
    out, o_buf, roots, o_sem = refs[-4:]
    blocks, block, cols = o_buf.shape
    group = block // STRIP
    outs = []
    for n in range(blocks):
        for k in range(parts):
            level = codes[k][n, block:].astype(jnp.float32)
            roots[k] = jnp.exp2(level * (0.5 / FINE))
        for half in range(2):
            for g in range(half * STRIP // 2, (half + 1) * STRIP // 2):
                at = slice(g * group, (g + 1) * group)
                total = own[first + n, at]
                for k in range(parts):
                    root = roots[k, g : g + 1]
                    total += codes[k][n, at].astype(jnp.float32) * (root * (1.0 / LEVELS)) * root
                factor = mirror[first + n, at].astype(jnp.float32)
                o_buf[n, at] = (total * factor).astype(jnp.bfloat16)
            here = pl.ds(half * block // 2, block // 2)
            rows = pl.ds((first + n) * block + half * block // 2, block // 2)
            outs.append(
                pltpu.make_async_copy(o_buf.at[n, here], out.at[rows], o_sem.at[n, half])
            )
            outs[-1].start()
    for copy in outs:
        copy.wait()


def in_vmem(values):
    return pltpu.with_memory_space_constraint(values, pltpu.VMEM)


def join(own, mirror, coded, first, before):
    steps, block, cols = own.shape
    blocks = coded[0].shape[0]
    aliases, carried = {}, ()
    if before is not None:
        aliases, carried = {2 + len(coded): 0}, (before,)
    return pl.pallas_call(
        functools.partial(join_kernel, len(coded), first),
        out_shape=jax.ShapeDtypeStruct((steps * block, cols), jnp.bfloat16),
        in_specs=[INSIDE] * (2 + len(coded)) + [ANYWHERE] * len(carried),
        out_specs=ANYWHERE,
        scratch_shapes=[
            pltpu.VMEM((blocks, block, cols), jnp.bfloat16),
            pltpu.VMEM((len(coded), STRIP, cols), jnp.float32),
            pltpu.SemaphoreType.DMA((blocks, 2)),
        ],
        input_output_aliases=aliases,
        compiler_params=params(),
        cost_estimate=cost(0, 0),
    )(own, mirror, *[in_vmem(codes) for codes in coded], *carried)


def turn_kernel(pieces, width, places, flags, t_ref, *outs):
    a_width = t_ref.shape[1]
    for e in range(pieces):

        def one(t, carry, e=e):
            start = pl.multiple_of(places[e] * width + t * BLK, BLK)
            over = pl.ds(pl.multiple_of(t * BLK, BLK), BLK)
            for u in range(a_width // BLK):
                tile = masked(
                    t_ref[pl.ds(start, BLK), u * BLK : (u + 1) * BLK],
                    flags[places[e] * (width // BLK) + t, u],
                )
                outs[e][u * BLK : (u + 1) * BLK, over] = tile.T
            return carry

        lax.fori_loop(0, width // BLK, one, 0)


def turn(places, flags, t_vals, c_width):
    pieces = t_vals.shape[0] // c_width
    shape = (t_vals.shape[1], c_width)
    return pl.pallas_call(
        functools.partial(turn_kernel, pieces, c_width),
        out_shape=[jax.ShapeDtypeStruct(shape, jnp.bfloat16)] * pieces,
        grid_spec=pltpu.PrefetchScalarGridSpec(
            num_scalar_prefetch=2,
            grid=(1,),
            in_specs=[whole(t_vals.shape)],
            out_specs=[whole(shape)] * pieces,
        ),
        compiler_params=params(),
        cost_estimate=cost(0, 4 * t_vals.size),
    )(places, flags, t_vals)


def body(n_row, n_col, r_vals, s_vals, t_vals, r_pattern, s_pattern, t_pattern):
    side = math.isqrt(n_col)
    row = lax.axis_index("row")
    col = lax.axis_index("col")
    line, kind = row // 2, row % 2
    y, x = col // side, col % side
    a_rows, b_width = r_vals.shape
    c_width = s_vals.shape[1]
    a_part = t_vals.shape[1]
    a_tiles, ap_tiles = a_rows // BLK, a_part // BLK
    along = kind == 1
    gather_at = jnp.where(along, x, y)
    target_at = jnp.where(along, y, x)
    axes = ("row", "col")

    def place(k, h, yy, xx):
        return (k * 2 + h) * n_col + yy * side + xx

    def shifted(e, gather):
        pairs = []
        for k in range(n_row // 2):
            for h in range(2):
                for yy in range(side):
                    for xx in range(side):
                        if (h == 1) == gather:
                            to = (yy, (xx + e) % side)
                        else:
                            to = ((yy + e) % side, xx)
                        pairs.append((place(k, h, yy, xx), place(k, h, *to)))
        return pairs

    r_pieces = [r_vals] + [lax.ppermute(r_vals, axes, shifted(e, True)) for e in range(1, side)]

    flat = n_col & (n_col - 1) == 0
    partner = [(col ^ e) if flat else (col + e) % n_col for e in range(n_col)]
    t_flags = lax.dynamic_slice_in_dim(t_pattern, (row * n_col + col) * ap_tiles, ap_tiles, 1)
    turned = turn(jnp.stack(partner).astype(jnp.int32), t_flags, t_vals, c_width)
    same, other = [], []
    for a in range(side):
        for b in range(side):
            for c in range(side):
                for d in range(side):
                    k = a * side + b
                    to_odd = (c * side + b, 1, a, d)
                    to_even = (a * side + d, 0, c, b)
                    same.append((place(k, 0, c, d), place(*to_even)))
                    same.append((place(k, 1, c, d), place(*to_odd)))
                    other.append((place(k, 1, c, d), place(*to_even)))
                    other.append((place(k, 0, c, d), place(*to_odd)))
    s_same = lax.ppermute(s_vals, axes, same)
    s_other = lax.ppermute(s_vals, axes, other)
    s_held = jnp.concatenate(
        [jnp.where(along, s_other, s_same), jnp.where(along, s_same, s_other)], axis=0
    )

    def along_line(values, hop):
        pairs = [(k * 2 + h, hop(k) * 2 + h) for k in range(n_col) for h in range(2)]
        return lax.ppermute(values, "row", pairs)

    if flat:
        got = {0: s_held}
        bit = n_col // 2
        while bit:
            got |= {m | bit: along_line(v, lambda k, bit=bit: k ^ bit) for m, v in got.items()}
            if len(got) == 2:
                got[bit], *turned = lax.optimization_barrier((got[bit], *turned))
            bit //= 2
        s_pieces = [got[m] for m in range(n_col)]
    else:
        s_pieces = [s_held] + [
            along_line(s_held, lambda k, d=d: (k + d) % n_col) for d in range(1, n_col)
        ]

    t_pieces = [turned[0]]
    for e in range(1, n_col):
        pairs = [(j, (j ^ e) if flat else (j + e) % n_col) for j in range(n_col)]
        t_pieces.append(lax.ppermute(turned[e], "col", pairs))

    r_flags = lax.dynamic_slice_in_dim(r_pattern, row * a_tiles, a_tiles, 0)
    flags = [r_flags.reshape(-1), s_pattern.reshape(-1)]
    sizes = (side, a_tiles, r_pattern.shape[1], s_pattern.shape[1])

    blocks, spots, targets = [], [], []
    for e in range(side):
        g = (gather_at - e) % side
        blocks.append(jnp.where(along, y * side + g, g * side + x))
    for t in range(side):
        target = (target_at + t) % side
        for e in range(side):
            g = (gather_at - e) % side
            k = jnp.where(along, target * side + g, g * side + target)
            spots.append((line ^ k) if flat else (line - k) % n_col)
        targets.append(jnp.where(along, target * side + x, y * side + target))
    table = jnp.concatenate([jnp.stack(blocks + spots + targets).astype(jnp.int32), *flags])

    block = max(a_part, math.gcd(a_rows, 4 * BLK))
    steps = a_rows // block
    chunks = 2 if steps % 2 == 0 else 1
    steps //= chunks
    coded = []
    for chunk in range(chunks):
        parts = []
        for e in range(1, side):
            codes = coded_product(
                sizes, table, r_pieces, s_pieces, e, block, chunk * steps * block, steps
            )
            if chunk:
                codes, *t_pieces[1:] = lax.optimization_barrier((codes, *t_pieces[1:]))
            parts.append(lax.ppermute(codes, axes, shifted(e, False)))
        coded.append(parts)
    order = [(col ^ o) if flat else (col - o) % n_col for o in range(n_col)]
    own, mirror = own_product(
        sizes, table, jnp.stack(order).astype(jnp.int32), r_pieces, s_pieces, t_pieces, block
    )
    own, mirror = in_vmem(own), in_vmem(mirror)
    out = None
    for chunk in range(chunks):
        out = join(own, mirror, coded[chunk], chunk * steps, out)
    return out


def plain_body(r_vals, s_vals, t_vals, r_pattern, s_pattern, t_pattern):
    row, col = lax.axis_index("row"), lax.axis_index("col")
    s_all = lax.all_gather(s_vals, "row", axis=0, tiled=True)
    r_all = lax.all_gather(r_vals, "col", axis=1, tiled=True)
    t_all = lax.all_to_all(t_vals, "col", split_axis=0, concat_axis=1, tiled=True)
    a_tiles, c_tiles = r_vals.shape[0] // BLK, s_vals.shape[1] // BLK

    def spread(flags):
        return jnp.repeat(jnp.repeat(flags.astype(jnp.bfloat16), BLK, axis=0), BLK, axis=1)

    r_flags = lax.dynamic_slice_in_dim(r_pattern, row * a_tiles, a_tiles, 0)
    s_flags = lax.dynamic_slice_in_dim(s_pattern, col * c_tiles, c_tiles, 1)
    t_flags = lax.dynamic_slice(t_pattern, (col * c_tiles, row * a_tiles), (c_tiles, a_tiles))
    paths = jnp.dot(
        r_all * spread(r_flags), s_all * spread(s_flags), preferred_element_type=jnp.float32
    )
    mirror = (t_all * spread(t_flags)).T
    return (paths * mirror.astype(jnp.float32)).astype(jnp.bfloat16)


def solution(mesh):
    placed = (P("row", "col"), P("row", "col"), P(None, ("row", "col")), P(), P(), P())
    n_row, n_col = mesh.shape["row"], mesh.shape["col"]
    fits = n_row == 2 * n_col and math.isqrt(n_col) ** 2 == n_col > 1
    return jax.shard_map(
        functools.partial(body, n_row, n_col) if fits else plain_body,
        mesh=mesh,
        in_specs=placed,
        out_specs=P("row", "col"),
        check_vma=False,
    )
```

```python
import functools
import math

import jax
import jax.numpy as jnp
from jax import lax
from jax.experimental import pallas as pl
from jax.experimental.pallas import tpu as pltpu
from jax.sharding import PartitionSpec as P

BLK = 128
STRIP = 16
LEVELS = 32767.0
FINE = 64.0
VMEM = 24 * 1024 * 1024


def masked(values, flag):
    return values * jnp.full((1, BLK), flag.astype(jnp.float32)).astype(jnp.bfloat16)


def joined_tiles(grid):
    bands = [jnp.concatenate(t, axis=1) if len(t) > 1 else t[0] for t in grid]
    return jnp.concatenate(bands, axis=0) if len(bands) > 1 else bands[0]


def whole(shape):
    return pl.BlockSpec(shape, lambda i, *_: (0,) * len(shape))


def cost(flops, bytes_accessed):
    return pl.CostEstimate(flops=flops, bytes_accessed=bytes_accessed, transcendentals=0)


def params(limit=VMEM):
    return pltpu.CompilerParams(vmem_limit_bytes=limit)


class Table:
    def __init__(self, ref, pieces, a_tiles, b_all, c_all):
        self.ref, self.pieces = ref, pieces
        self.b_all, self.c_all = b_all, c_all
        self.r_at = pieces * (pieces + 2)
        self.s_at = self.r_at + a_tiles * b_all

    def block(self, e):
        return self.ref[e]

    def spot(self, target, e):
        return self.ref[(target + 1) * self.pieces + e]

    def column(self, target):
        return self.ref[(self.pieces + 1) * self.pieces + target]

    def r_flag(self, a, b):
        return self.ref[self.r_at + a * self.b_all + b]

    def s_flag(self, b, c):
        return self.ref[self.s_at + b * self.c_all + c]


def select_copy(choice, sources, target, sem):
    for d, source in enumerate(sources):

        @pl.when(choice == d)
        def _(source=source):
            pltpu.make_async_copy(source, target, sem).start()

    return pltpu.make_async_copy(sources[0], target, sem)


def products(table, target, first, r_refs, s_refs, r_buf, s_buf, r_sem, s_sem, use):
    pieces, blocks, block, width = r_buf.shape
    cols = s_buf.shape[1]
    b_tiles, c_tiles = width // BLK, cols // BLK

    def r_copy(e, n):
        rows = pl.ds(pl.multiple_of(first + n * block, block), block)
        return pltpu.make_async_copy(r_refs[e].at[rows], r_buf.at[e, n], r_sem.at[e, n])

    waits = [
        select_copy(table.spot(target, e), s_refs, s_buf.at[pl.ds(e * width, width)], s_sem.at[e])
        for e in range(pieces)
    ]
    for n in range(blocks):
        for e in range(pieces):
            r_copy(e, n).start()
    for e in range(pieces):
        waits[e].wait()
        for t in range(b_tiles):
            for u in range(c_tiles):
                flag = table.s_flag(table.block(e) * b_tiles + t, table.column(target) * c_tiles + u)
                down = slice(e * width + t * BLK, e * width + (t + 1) * BLK)
                over = slice(u * BLK, (u + 1) * BLK)
                s_buf[down, over] = masked(s_buf[down, over], flag)

    def one(n, carry):
        for e in range(pieces):
            r_copy(e, n).wait()
        grid = []
        for t in range(block // BLK):
            a = first // BLK + n * (block // BLK) + t
            grid.append(
                [
                    masked(
                        r_buf[e, n, t * BLK : (t + 1) * BLK, u * BLK : (u + 1) * BLK],
                        table.r_flag(a, table.block(e) * b_tiles + u),
                    )
                    for e in range(pieces)
                    for u in range(b_tiles)
                ]
            )
        use(n, jnp.dot(joined_tiles(grid), s_buf[...], preferred_element_type=jnp.float32))
        return carry

    lax.fori_loop(0, blocks, one, 0)


def encode(total, out):
    rows, cols = total.shape
    group = rows // STRIP
    strip_row = lax.broadcasted_iota(jnp.int32, (STRIP, cols), 0)
    strip = jnp.zeros((STRIP, cols), jnp.float32)
    for g in range(STRIP):
        part = total[g * group : (g + 1) * group]
        top = jnp.max(jnp.max(jnp.abs(part), axis=0, keepdims=True), axis=1, keepdims=True)
        level = jnp.ceil(jnp.log2(jnp.maximum(top, 1e-37)) * FINE) + 1.0
        root = jnp.exp2(level * (-0.5 / FINE))
        code = jnp.clip(jnp.round(part * root * (root * LEVELS)), -LEVELS, LEVELS)
        out[g * group : (g + 1) * group] = code.astype(jnp.int16)
        strip = jnp.where(strip_row == g, level, strip)
    out[rows:] = strip.astype(jnp.int16)


def coded_kernel(sizes, target, first, numbers, *refs):
    *ins, out, r_buf, s_buf, r_sem, s_sem = refs
    pieces = r_buf.shape[0]

    def use(n, total):
        encode(total, out.at[n])

    products(
        Table(numbers, *sizes), target, first, ins[:pieces], ins[pieces:],
        r_buf, s_buf, r_sem, s_sem, use,
    )


def own_kernel(sizes, count, numbers, order, *refs):
    *ins, out, mirror, r_buf, s_buf, r_sem, s_sem, t_sem = refs
    pieces = r_buf.shape[0]
    t_refs = ins[pieces + count :]
    blocks, block, _ = mirror.shape
    a_part = t_refs[0].shape[0]
    split = block // a_part
    waits = []
    for o in range(blocks * split):
        rows = pl.ds(o % split * a_part, a_part)
        waits.append(select_copy(order[o], t_refs, mirror.at[o // split, rows], t_sem.at[o]))

    def use(n, total):
        out[n] = total

    products(
        Table(numbers, *sizes), 0, 0, ins[:pieces], ins[pieces : pieces + count],
        r_buf, s_buf, r_sem, s_sem, use,
    )
    for wait in waits:
        wait.wait()


SCALARS = pl.BlockSpec(memory_space=pltpu.SMEM)
ANYWHERE = pl.BlockSpec(memory_space=pl.ANY)
INSIDE = pl.BlockSpec(memory_space=pltpu.VMEM)


def product_scratch(pieces, blocks, block, width, cols):
    return [
        pltpu.VMEM((pieces, blocks, block, width), jnp.bfloat16),
        pltpu.VMEM((pieces * width, cols), jnp.bfloat16),
        pltpu.SemaphoreType.DMA((pieces, blocks)),
        pltpu.SemaphoreType.DMA((pieces,)),
    ]


def coded_product(sizes, table, r_pieces, s_pieces, target, block, first, blocks):
    pieces = len(r_pieces)
    width, cols = s_pieces[0].shape
    return pl.pallas_call(
        functools.partial(coded_kernel, sizes, target, first),
        out_shape=pltpu.VMEM((blocks, block + STRIP, cols), jnp.int16),
        in_specs=[SCALARS] + [ANYWHERE] * (pieces + len(s_pieces)),
        out_specs=INSIDE,
        scratch_shapes=product_scratch(pieces, blocks, block, width, cols),
        compiler_params=params(),
        cost_estimate=cost(2 * blocks * block * pieces * width * cols // 16, 0),
    )(table, *r_pieces, *s_pieces)


def own_product(sizes, table, order, r_pieces, s_pieces, t_pieces, block):
    pieces = len(r_pieces)
    width, cols = s_pieces[0].shape
    blocks = r_pieces[0].shape[0] // block
    return pl.pallas_call(
        functools.partial(own_kernel, sizes, len(s_pieces)),
        out_shape=[
            pltpu.VMEM((blocks, block, cols), jnp.float32),
            pltpu.VMEM((blocks, block, cols), jnp.bfloat16),
        ],
        in_specs=[SCALARS] * 2 + [ANYWHERE] * (pieces + len(s_pieces) + len(t_pieces)),
        out_specs=[INSIDE] * 2,
        scratch_shapes=product_scratch(pieces, blocks, block, width, cols)
        + [pltpu.SemaphoreType.DMA((len(t_pieces),))],
        compiler_params=params(),
        cost_estimate=cost(2 * blocks * block * pieces * width * cols // 16, 0),
    )(table, order, *r_pieces, *s_pieces, *t_pieces)


def join_kernel(parts, first, own, mirror, *refs):
    codes = refs[:parts]
    out, o_buf, roots, o_sem = refs[-4:]
    blocks, block, cols = o_buf.shape
    group = block // STRIP
    outs = []
    for n in range(blocks):
        for k in range(parts):
            level = codes[k][n, block:].astype(jnp.float32)
            roots[k] = jnp.exp2(level * (0.5 / FINE))
        for half in range(2):
            for g in range(half * STRIP // 2, (half + 1) * STRIP // 2):
                at = slice(g * group, (g + 1) * group)
                total = own[first + n, at]
                for k in range(parts):
                    root = roots[k, g : g + 1]
                    total += codes[k][n, at].astype(jnp.float32) * (root * (1.0 / LEVELS)) * root
                factor = mirror[first + n, at].astype(jnp.float32)
                o_buf[n, at] = (total * factor).astype(jnp.bfloat16)
            here = pl.ds(half * block // 2, block // 2)
            rows = pl.ds((first + n) * block + half * block // 2, block // 2)
            outs.append(
                pltpu.make_async_copy(o_buf.at[n, here], out.at[rows], o_sem.at[n, half])
            )
            outs[-1].start()
    for copy in outs:
        copy.wait()


def in_vmem(values):
    return pltpu.with_memory_space_constraint(values, pltpu.VMEM)


def join(own, mirror, coded, first, before):
    steps, block, cols = own.shape
    blocks = coded[0].shape[0]
    aliases, carried = {}, ()
    if before is not None:
        aliases, carried = {2 + len(coded): 0}, (before,)
    return pl.pallas_call(
        functools.partial(join_kernel, len(coded), first),
        out_shape=jax.ShapeDtypeStruct((steps * block, cols), jnp.bfloat16),
        in_specs=[INSIDE] * (2 + len(coded)) + [ANYWHERE] * len(carried),
        out_specs=ANYWHERE,
        scratch_shapes=[
            pltpu.VMEM((blocks, block, cols), jnp.bfloat16),
            pltpu.VMEM((len(coded), STRIP, cols), jnp.float32),
            pltpu.SemaphoreType.DMA((blocks, 2)),
        ],
        input_output_aliases=aliases,
        compiler_params=params(),
        cost_estimate=cost(0, 0),
    )(own, mirror, *[in_vmem(codes) for codes in coded], *carried)


def turn_kernel(pieces, width, places, flags, t_ref, *outs):
    a_width = t_ref.shape[1]
    for e in range(pieces):

        def one(t, carry, e=e):
            start = pl.multiple_of(places[e] * width + t * BLK, BLK)
            over = pl.ds(pl.multiple_of(t * BLK, BLK), BLK)
            for u in range(a_width // BLK):
                tile = masked(
                    t_ref[pl.ds(start, BLK), u * BLK : (u + 1) * BLK],
                    flags[places[e] * (width // BLK) + t, u],
                )
                outs[e][u * BLK : (u + 1) * BLK, over] = tile.T
            return carry

        lax.fori_loop(0, width // BLK, one, 0)


def turn(places, flags, t_vals, c_width):
    pieces = t_vals.shape[0] // c_width
    shape = (t_vals.shape[1], c_width)
    return pl.pallas_call(
        functools.partial(turn_kernel, pieces, c_width),
        out_shape=[jax.ShapeDtypeStruct(shape, jnp.bfloat16)] * pieces,
        grid_spec=pltpu.PrefetchScalarGridSpec(
            num_scalar_prefetch=2,
            grid=(1,),
            in_specs=[whole(t_vals.shape)],
            out_specs=[whole(shape)] * pieces,
        ),
        compiler_params=params(),
        cost_estimate=cost(0, 4 * t_vals.size),
    )(places, flags, t_vals)


def body(n_row, n_col, r_vals, s_vals, t_vals, r_pattern, s_pattern, t_pattern):
    side = math.isqrt(n_col)
    row = lax.axis_index("row")
    col = lax.axis_index("col")
    line, kind = row // 2, row % 2
    y, x = col // side, col % side
    a_rows, b_width = r_vals.shape
    c_width = s_vals.shape[1]
    a_part = t_vals.shape[1]
    a_tiles, ap_tiles = a_rows // BLK, a_part // BLK
    along = kind == 1
    gather_at = jnp.where(along, x, y)
    target_at = jnp.where(along, y, x)
    axes = ("row", "col")

    def place(k, h, yy, xx):
        return (k * 2 + h) * n_col + yy * side + xx

    def shifted(e, gather):
        pairs = []
        for k in range(n_row // 2):
            for h in range(2):
                for yy in range(side):
                    for xx in range(side):
                        if (h == 1) == gather:
                            to = (yy, (xx + e) % side)
                        else:
                            to = ((yy + e) % side, xx)
                        pairs.append((place(k, h, yy, xx), place(k, h, *to)))
        return pairs

    r_pieces = [r_vals] + [lax.ppermute(r_vals, axes, shifted(e, True)) for e in range(1, side)]

    flat = n_col & (n_col - 1) == 0
    partner = [(col ^ e) if flat else (col + e) % n_col for e in range(n_col)]
    t_flags = lax.dynamic_slice_in_dim(t_pattern, (row * n_col + col) * ap_tiles, ap_tiles, 1)
    turned = turn(jnp.stack(partner).astype(jnp.int32), t_flags, t_vals, c_width)
    same, other = [], []
    for a in range(side):
        for b in range(side):
            for c in range(side):
                for d in range(side):
                    k = a * side + b
                    to_odd = (c * side + b, 1, a, d)
                    to_even = (a * side + d, 0, c, b)
                    same.append((place(k, 0, c, d), place(*to_even)))
                    same.append((place(k, 1, c, d), place(*to_odd)))
                    other.append((place(k, 1, c, d), place(*to_even)))
                    other.append((place(k, 0, c, d), place(*to_odd)))
    s_same = lax.ppermute(s_vals, axes, same)
    s_other = lax.ppermute(s_vals, axes, other)
    s_held = jnp.concatenate(
        [jnp.where(along, s_other, s_same), jnp.where(along, s_same, s_other)], axis=0
    )

    def to_partner(e):
        pairs = [(j, (j ^ e) if flat else (j + e) % n_col) for j in range(n_col)]
        return lax.ppermute(turned[e], "col", pairs)

    t_last = to_partner(n_col - 1)

    def along_line(values, hop):
        pairs = [(k * 2 + h, hop(k) * 2 + h) for k in range(n_col) for h in range(2)]
        return lax.ppermute(values, "row", pairs)

    if flat:
        got = {0: s_held}
        bit = n_col // 2
        while bit:
            got |= {m | bit: along_line(v, lambda k, bit=bit: k ^ bit) for m, v in got.items()}
            if len(got) == 2:
                got[bit], t_last, *turned = lax.optimization_barrier((got[bit], t_last, *turned))
            bit //= 2
        s_pieces = [got[m] for m in range(n_col)]
    else:
        s_pieces = [s_held] + [
            along_line(s_held, lambda k, d=d: (k + d) % n_col) for d in range(1, n_col)
        ]

    t_pieces = [turned[0]] + [to_partner(e) for e in range(1, n_col - 1)] + [t_last]

    r_flags = lax.dynamic_slice_in_dim(r_pattern, row * a_tiles, a_tiles, 0)
    flags = [r_flags.reshape(-1), s_pattern.reshape(-1)]
    sizes = (side, a_tiles, r_pattern.shape[1], s_pattern.shape[1])

    blocks, spots, targets = [], [], []
    for e in range(side):
        g = (gather_at - e) % side
        blocks.append(jnp.where(along, y * side + g, g * side + x))
    for t in range(side):
        target = (target_at + t) % side
        for e in range(side):
            g = (gather_at - e) % side
            k = jnp.where(along, target * side + g, g * side + target)
            spots.append((line ^ k) if flat else (line - k) % n_col)
        targets.append(jnp.where(along, target * side + x, y * side + target))
    table = jnp.concatenate([jnp.stack(blocks + spots + targets).astype(jnp.int32), *flags])

    block = max(a_part, math.gcd(a_rows, 4 * BLK))
    steps = a_rows // block
    chunks = 2 if steps % 2 == 0 else 1
    steps //= chunks
    coded = []
    for chunk in range(chunks):
        parts = []
        for e in range(1, side):
            codes = coded_product(
                sizes, table, r_pieces, s_pieces, e, block, chunk * steps * block, steps
            )
            if chunk:
                codes, *t_pieces[1:] = lax.optimization_barrier((codes, *t_pieces[1:]))
            parts.append(lax.ppermute(codes, axes, shifted(e, False)))
        coded.append(parts)
    order = [(col ^ o) if flat else (col - o) % n_col for o in range(n_col)]
    own, mirror = own_product(
        sizes, table, jnp.stack(order).astype(jnp.int32), r_pieces, s_pieces, t_pieces, block
    )
    own, mirror = in_vmem(own), in_vmem(mirror)
    out = None
    for chunk in range(chunks):
        out = join(own, mirror, coded[chunk], chunk * steps, out)
    return out


def plain_body(r_vals, s_vals, t_vals, r_pattern, s_pattern, t_pattern):
    row, col = lax.axis_index("row"), lax.axis_index("col")
    s_all = lax.all_gather(s_vals, "row", axis=0, tiled=True)
    r_all = lax.all_gather(r_vals, "col", axis=1, tiled=True)
    t_all = lax.all_to_all(t_vals, "col", split_axis=0, concat_axis=1, tiled=True)
    a_tiles, c_tiles = r_vals.shape[0] // BLK, s_vals.shape[1] // BLK

    def spread(flags):
        return jnp.repeat(jnp.repeat(flags.astype(jnp.bfloat16), BLK, axis=0), BLK, axis=1)

    r_flags = lax.dynamic_slice_in_dim(r_pattern, row * a_tiles, a_tiles, 0)
    s_flags = lax.dynamic_slice_in_dim(s_pattern, col * c_tiles, c_tiles, 1)
    t_flags = lax.dynamic_slice(t_pattern, (col * c_tiles, row * a_tiles), (c_tiles, a_tiles))
    paths = jnp.dot(
        r_all * spread(r_flags), s_all * spread(s_flags), preferred_element_type=jnp.float32
    )
    mirror = (t_all * spread(t_flags)).T
    return (paths * mirror.astype(jnp.float32)).astype(jnp.bfloat16)


def solution(mesh):
    placed = (P("row", "col"), P("row", "col"), P(None, ("row", "col")), P(), P(), P())
    n_row, n_col = mesh.shape["row"], mesh.shape["col"]
    fits = n_row == 2 * n_col and math.isqrt(n_col) ** 2 == n_col > 1
    return jax.shard_map(
        functools.partial(body, n_row, n_col) if fits else plain_body,
        mesh=mesh,
        in_specs=placed,
        out_specs=P("row", "col"),
        check_vma=False,
    )
```

```python
import functools
import math

import jax
import jax.numpy as jnp
from jax import lax
from jax.experimental import pallas as pl
from jax.experimental.pallas import tpu as pltpu
from jax.sharding import PartitionSpec as P

BLK = 128
STRIP = 16
LEVELS = 32767.0
FINE = 64.0
VMEM = 24 * 1024 * 1024


def masked(values, flag):
    return values * jnp.full((1, BLK), flag.astype(jnp.float32)).astype(jnp.bfloat16)


def joined_tiles(grid):
    bands = [jnp.concatenate(t, axis=1) if len(t) > 1 else t[0] for t in grid]
    return jnp.concatenate(bands, axis=0) if len(bands) > 1 else bands[0]


def whole(shape):
    return pl.BlockSpec(shape, lambda i, *_: (0,) * len(shape))


def cost(flops, bytes_accessed):
    return pl.CostEstimate(flops=flops, bytes_accessed=bytes_accessed, transcendentals=0)


def params(limit=VMEM):
    return pltpu.CompilerParams(vmem_limit_bytes=limit)


class Table:
    def __init__(self, ref, pieces, a_tiles, b_all, c_all):
        self.ref, self.pieces = ref, pieces
        self.b_all, self.c_all = b_all, c_all
        self.r_at = pieces * (pieces + 2)
        self.s_at = self.r_at + a_tiles * b_all

    def block(self, e):
        return self.ref[e]

    def spot(self, target, e):
        return self.ref[(target + 1) * self.pieces + e]

    def column(self, target):
        return self.ref[(self.pieces + 1) * self.pieces + target]

    def r_flag(self, a, b):
        return self.ref[self.r_at + a * self.b_all + b]

    def s_flag(self, b, c):
        return self.ref[self.s_at + b * self.c_all + c]


def select_copy(choice, sources, target, sem):
    for d, source in enumerate(sources):

        @pl.when(choice == d)
        def _(source=source):
            pltpu.make_async_copy(source, target, sem).start()

    return pltpu.make_async_copy(sources[0], target, sem)


def products(table, target, first, r_refs, s_refs, r_buf, s_buf, r_sem, s_sem, use):
    pieces, blocks, block, width = r_buf.shape
    cols = s_buf.shape[1]
    b_tiles, c_tiles = width // BLK, cols // BLK

    def r_copy(e, n):
        rows = pl.ds(pl.multiple_of(first + n * block, block), block)
        return pltpu.make_async_copy(r_refs[e].at[rows], r_buf.at[e, n], r_sem.at[e, n])

    waits = [
        select_copy(table.spot(target, e), s_refs, s_buf.at[pl.ds(e * width, width)], s_sem.at[e])
        for e in range(pieces)
    ]
    for n in range(blocks):
        for e in range(pieces):
            r_copy(e, n).start()
    for e in range(pieces):
        waits[e].wait()
        for t in range(b_tiles):
            for u in range(c_tiles):
                flag = table.s_flag(table.block(e) * b_tiles + t, table.column(target) * c_tiles + u)
                down = slice(e * width + t * BLK, e * width + (t + 1) * BLK)
                over = slice(u * BLK, (u + 1) * BLK)
                s_buf[down, over] = masked(s_buf[down, over], flag)

    def one(n, carry):
        for e in range(pieces):
            r_copy(e, n).wait()
        grid = []
        for t in range(block // BLK):
            a = first // BLK + n * (block // BLK) + t
            grid.append(
                [
                    masked(
                        r_buf[e, n, t * BLK : (t + 1) * BLK, u * BLK : (u + 1) * BLK],
                        table.r_flag(a, table.block(e) * b_tiles + u),
                    )
                    for e in range(pieces)
                    for u in range(b_tiles)
                ]
            )
        use(n, jnp.dot(joined_tiles(grid), s_buf[...], preferred_element_type=jnp.float32))
        return carry

    lax.fori_loop(0, blocks, one, 0)


def encode(total, out):
    rows, cols = total.shape
    group = rows // STRIP
    strip_row = lax.broadcasted_iota(jnp.int32, (STRIP, cols), 0)
    strip = jnp.zeros((STRIP, cols), jnp.float32)
    for g in range(STRIP):
        part = total[g * group : (g + 1) * group]
        top = jnp.max(jnp.max(jnp.abs(part), axis=0, keepdims=True), axis=1, keepdims=True)
        level = jnp.ceil(jnp.log2(jnp.maximum(top, 1e-37)) * FINE) + 1.0
        root = jnp.exp2(level * (-0.5 / FINE))
        code = jnp.clip(jnp.round(part * root * (root * LEVELS)), -LEVELS, LEVELS)
        out[g * group : (g + 1) * group] = code.astype(jnp.int16)
        strip = jnp.where(strip_row == g, level, strip)
    out[rows:] = strip.astype(jnp.int16)


def coded_kernel(sizes, target, first, numbers, *refs):
    *ins, out, r_buf, s_buf, r_sem, s_sem = refs
    pieces = r_buf.shape[0]

    def use(n, total):
        encode(total, out.at[n])

    products(
        Table(numbers, *sizes), target, first, ins[:pieces], ins[pieces:],
        r_buf, s_buf, r_sem, s_sem, use,
    )


def own_kernel(sizes, count, numbers, order, *refs):
    *ins, out, mirror, r_buf, s_buf, r_sem, s_sem, t_sem = refs
    pieces = r_buf.shape[0]
    t_refs = ins[pieces + count :]
    blocks, block, _ = mirror.shape
    a_part = t_refs[0].shape[0]
    split = block // a_part
    waits = []
    for o in range(blocks * split):
        rows = pl.ds(o % split * a_part, a_part)
        waits.append(select_copy(order[o], t_refs, mirror.at[o // split, rows], t_sem.at[o]))

    def use(n, total):
        out[n] = total

    products(
        Table(numbers, *sizes), 0, 0, ins[:pieces], ins[pieces : pieces + count],
        r_buf, s_buf, r_sem, s_sem, use,
    )
    for wait in waits:
        wait.wait()


SCALARS = pl.BlockSpec(memory_space=pltpu.SMEM)
ANYWHERE = pl.BlockSpec(memory_space=pl.ANY)
INSIDE = pl.BlockSpec(memory_space=pltpu.VMEM)


def product_scratch(pieces, blocks, block, width, cols):
    return [
        pltpu.VMEM((pieces, blocks, block, width), jnp.bfloat16),
        pltpu.VMEM((pieces * width, cols), jnp.bfloat16),
        pltpu.SemaphoreType.DMA((pieces, blocks)),
        pltpu.SemaphoreType.DMA((pieces,)),
    ]


def coded_product(sizes, table, r_pieces, s_pieces, target, block, first, blocks):
    pieces = len(r_pieces)
    width, cols = s_pieces[0].shape
    return pl.pallas_call(
        functools.partial(coded_kernel, sizes, target, first),
        out_shape=pltpu.VMEM((blocks, block + STRIP, cols), jnp.int16),
        in_specs=[SCALARS] + [ANYWHERE] * (pieces + len(s_pieces)),
        out_specs=INSIDE,
        scratch_shapes=product_scratch(pieces, blocks, block, width, cols),
        compiler_params=params(),
        cost_estimate=cost(2 * blocks * block * pieces * width * cols // 16, 0),
    )(table, *r_pieces, *s_pieces)


def own_product(sizes, table, order, r_pieces, s_pieces, t_pieces, block):
    pieces = len(r_pieces)
    width, cols = s_pieces[0].shape
    blocks = r_pieces[0].shape[0] // block
    return pl.pallas_call(
        functools.partial(own_kernel, sizes, len(s_pieces)),
        out_shape=[
            pltpu.VMEM((blocks, block, cols), jnp.float32),
            pltpu.VMEM((blocks, block, cols), jnp.bfloat16),
        ],
        in_specs=[SCALARS] * 2 + [ANYWHERE] * (pieces + len(s_pieces) + len(t_pieces)),
        out_specs=[INSIDE] * 2,
        scratch_shapes=product_scratch(pieces, blocks, block, width, cols)
        + [pltpu.SemaphoreType.DMA((len(t_pieces),))],
        compiler_params=params(),
        cost_estimate=cost(2 * blocks * block * pieces * width * cols // 16, 0),
    )(table, order, *r_pieces, *s_pieces, *t_pieces)


def join_kernel(parts, first, own, mirror, *refs):
    codes = refs[:parts]
    out, o_buf, roots, o_sem = refs[-4:]
    blocks, block, cols = o_buf.shape
    group = block // STRIP
    outs = []
    for n in range(blocks):
        for k in range(parts):
            level = codes[k][n, block:].astype(jnp.float32)
            roots[k] = jnp.exp2(level * (0.5 / FINE))
        for half in range(2):
            for g in range(half * STRIP // 2, (half + 1) * STRIP // 2):
                at = slice(g * group, (g + 1) * group)
                total = own[first + n, at]
                for k in range(parts):
                    root = roots[k, g : g + 1]
                    total += codes[k][n, at].astype(jnp.float32) * (root * (1.0 / LEVELS)) * root
                factor = mirror[first + n, at].astype(jnp.float32)
                o_buf[n, at] = (total * factor).astype(jnp.bfloat16)
            here = pl.ds(half * block // 2, block // 2)
            rows = pl.ds((first + n) * block + half * block // 2, block // 2)
            outs.append(
                pltpu.make_async_copy(o_buf.at[n, here], out.at[rows], o_sem.at[n, half])
            )
            outs[-1].start()
    for copy in outs:
        copy.wait()


def in_vmem(values):
    return pltpu.with_memory_space_constraint(values, pltpu.VMEM)


def join(own, mirror, coded, first, before):
    steps, block, cols = own.shape
    blocks = coded[0].shape[0]
    aliases, carried = {}, ()
    if before is not None:
        aliases, carried = {2 + len(coded): 0}, (before,)
    return pl.pallas_call(
        functools.partial(join_kernel, len(coded), first),
        out_shape=jax.ShapeDtypeStruct((steps * block, cols), jnp.bfloat16),
        in_specs=[INSIDE] * (2 + len(coded)) + [ANYWHERE] * len(carried),
        out_specs=ANYWHERE,
        scratch_shapes=[
            pltpu.VMEM((blocks, block, cols), jnp.bfloat16),
            pltpu.VMEM((len(coded), STRIP, cols), jnp.float32),
            pltpu.SemaphoreType.DMA((blocks, 2)),
        ],
        input_output_aliases=aliases,
        compiler_params=params(),
        cost_estimate=cost(0, 0),
    )(own, mirror, *[in_vmem(codes) for codes in coded], *carried)


def turn_kernel(pieces, width, places, flags, t_ref, *outs):
    a_width = t_ref.shape[1]
    for e in range(pieces):

        def one(t, carry, e=e):
            start = pl.multiple_of(places[e] * width + t * BLK, BLK)
            over = pl.ds(pl.multiple_of(t * BLK, BLK), BLK)
            for u in range(a_width // BLK):
                tile = masked(
                    t_ref[pl.ds(start, BLK), u * BLK : (u + 1) * BLK],
                    flags[places[e] * (width // BLK) + t, u],
                )
                outs[e][u * BLK : (u + 1) * BLK, over] = tile.T
            return carry

        lax.fori_loop(0, width // BLK, one, 0)


def turn(places, flags, t_vals, c_width):
    pieces = t_vals.shape[0] // c_width
    shape = (t_vals.shape[1], c_width)
    return pl.pallas_call(
        functools.partial(turn_kernel, pieces, c_width),
        out_shape=[jax.ShapeDtypeStruct(shape, jnp.bfloat16)] * pieces,
        grid_spec=pltpu.PrefetchScalarGridSpec(
            num_scalar_prefetch=2,
            grid=(1,),
            in_specs=[whole(t_vals.shape)],
            out_specs=[whole(shape)] * pieces,
        ),
        compiler_params=params(),
        cost_estimate=cost(0, 4 * t_vals.size),
    )(places, flags, t_vals)


def body(n_row, n_col, r_vals, s_vals, t_vals, r_pattern, s_pattern, t_pattern):
    side = math.isqrt(n_col)
    row = lax.axis_index("row")
    col = lax.axis_index("col")
    line, kind = row // 2, row % 2
    y, x = col // side, col % side
    a_rows, b_width = r_vals.shape
    c_width = s_vals.shape[1]
    a_part = t_vals.shape[1]
    a_tiles, ap_tiles = a_rows // BLK, a_part // BLK
    along = kind == 1
    gather_at = jnp.where(along, x, y)
    target_at = jnp.where(along, y, x)
    axes = ("row", "col")

    def place(k, h, yy, xx):
        return (k * 2 + h) * n_col + yy * side + xx

    def shifted(e, gather):
        pairs = []
        for k in range(n_row // 2):
            for h in range(2):
                for yy in range(side):
                    for xx in range(side):
                        if (h == 1) == gather:
                            to = (yy, (xx + e) % side)
                        else:
                            to = ((yy + e) % side, xx)
                        pairs.append((place(k, h, yy, xx), place(k, h, *to)))
        return pairs

    r_pieces = [r_vals] + [lax.ppermute(r_vals, axes, shifted(e, True)) for e in range(1, side)]

    flat = n_col & (n_col - 1) == 0
    if side == 2:
        first = jnp.where(along, 2, 1)
        partner = [col, col ^ first, col ^ (3 - first), col ^ 3]
    else:
        partner = [(col ^ e) if flat else (col + e) % n_col for e in range(n_col)]
    t_flags = lax.dynamic_slice_in_dim(t_pattern, (row * n_col + col) * ap_tiles, ap_tiles, 1)
    turned = turn(jnp.stack(partner).astype(jnp.int32), t_flags, t_vals, c_width)
    same, other = [], []
    for a in range(side):
        for b in range(side):
            for c in range(side):
                for d in range(side):
                    k = a * side + b
                    to_odd = (c * side + b, 1, a, d)
                    to_even = (a * side + d, 0, c, b)
                    same.append((place(k, 0, c, d), place(*to_even)))
                    same.append((place(k, 1, c, d), place(*to_odd)))
                    other.append((place(k, 1, c, d), place(*to_even)))
                    other.append((place(k, 0, c, d), place(*to_odd)))
    s_same = lax.ppermute(s_vals, axes, same)
    s_other = lax.ppermute(s_vals, axes, other)
    s_held = jnp.concatenate(
        [jnp.where(along, s_other, s_same), jnp.where(along, s_same, s_other)], axis=0
    )

    def to_partner(e, values):
        pairs = []
        for i in range(n_row):
            for j in range(n_col):
                if side == 2:
                    to = j ^ (3 if e == 3 else (1, 2)[(e + i + 1) % 2])
                else:
                    to = (j ^ e) if flat else (j + e) % n_col
                pairs.append((i * n_col + j, i * n_col + to))
        return lax.ppermute(values, axes, pairs)

    t_pieces = [turned[0], to_partner(1, turned[1])]

    def along_line(values, hop):
        pairs = [(k * 2 + h, hop(k) * 2 + h) for k in range(n_col) for h in range(2)]
        return lax.ppermute(values, "row", pairs)

    if flat:
        got = {0: s_held}
        bit = n_col // 2
        while bit:
            got |= {m | bit: along_line(v, lambda k, bit=bit: k ^ bit) for m, v in got.items()}
            if len(got) == 2:
                got[bit], *turned = lax.optimization_barrier((got[bit], *turned))
            bit //= 2
        s_pieces = [got[m] for m in range(n_col)]
    else:
        s_pieces = [s_held] + [
            along_line(s_held, lambda k, d=d: (k + d) % n_col) for d in range(1, n_col)
        ]

    t_pieces += [to_partner(e, turned[e]) for e in range(2, n_col)]

    r_flags = lax.dynamic_slice_in_dim(r_pattern, row * a_tiles, a_tiles, 0)
    flags = [r_flags.reshape(-1), s_pattern.reshape(-1)]
    sizes = (side, a_tiles, r_pattern.shape[1], s_pattern.shape[1])

    blocks, spots, targets = [], [], []
    for e in range(side):
        g = (gather_at - e) % side
        blocks.append(jnp.where(along, y * side + g, g * side + x))
    for t in range(side):
        target = (target_at + t) % side
        for e in range(side):
            g = (gather_at - e) % side
            k = jnp.where(along, target * side + g, g * side + target)
            spots.append((line ^ k) if flat else (line - k) % n_col)
        targets.append(jnp.where(along, target * side + x, y * side + target))
    table = jnp.concatenate([jnp.stack(blocks + spots + targets).astype(jnp.int32), *flags])

    block = max(a_part, math.gcd(a_rows, 4 * BLK))
    steps = a_rows // block
    chunks = 2 if steps % 2 == 0 else 1
    steps //= chunks
    coded = []
    for chunk in range(chunks):
        parts = []
        for e in range(1, side):
            codes = coded_product(
                sizes, table, r_pieces, s_pieces, e, block, chunk * steps * block, steps
            )
            if chunk:
                codes, *t_pieces[1:] = lax.optimization_barrier((codes, *t_pieces[1:]))
            parts.append(lax.ppermute(codes, axes, shifted(e, False)))
        coded.append(parts)
    order = [(col ^ o) if flat else (col - o) % n_col for o in range(n_col)]
    if side == 2:
        order = [jnp.where(along & (m % 3 > 0), 3 - m, m) for m in order]
    own, mirror = own_product(
        sizes, table, jnp.stack(order).astype(jnp.int32), r_pieces, s_pieces, t_pieces, block
    )
    own, mirror = in_vmem(own), in_vmem(mirror)
    out = None
    for chunk in range(chunks):
        out = join(own, mirror, coded[chunk], chunk * steps, out)
    return out


def plain_body(r_vals, s_vals, t_vals, r_pattern, s_pattern, t_pattern):
    row, col = lax.axis_index("row"), lax.axis_index("col")
    s_all = lax.all_gather(s_vals, "row", axis=0, tiled=True)
    r_all = lax.all_gather(r_vals, "col", axis=1, tiled=True)
    t_all = lax.all_to_all(t_vals, "col", split_axis=0, concat_axis=1, tiled=True)
    a_tiles, c_tiles = r_vals.shape[0] // BLK, s_vals.shape[1] // BLK

    def spread(flags):
        return jnp.repeat(jnp.repeat(flags.astype(jnp.bfloat16), BLK, axis=0), BLK, axis=1)

    r_flags = lax.dynamic_slice_in_dim(r_pattern, row * a_tiles, a_tiles, 0)
    s_flags = lax.dynamic_slice_in_dim(s_pattern, col * c_tiles, c_tiles, 1)
    t_flags = lax.dynamic_slice(t_pattern, (col * c_tiles, row * a_tiles), (c_tiles, a_tiles))
    paths = jnp.dot(
        r_all * spread(r_flags), s_all * spread(s_flags), preferred_element_type=jnp.float32
    )
    mirror = (t_all * spread(t_flags)).T
    return (paths * mirror.astype(jnp.float32)).astype(jnp.bfloat16)


def solution(mesh):
    placed = (P("row", "col"), P("row", "col"), P(None, ("row", "col")), P(), P(), P())
    n_row, n_col = mesh.shape["row"], mesh.shape["col"]
    fits = n_row == 2 * n_col and math.isqrt(n_col) ** 2 == n_col > 1
    return jax.shard_map(
        functools.partial(body, n_row, n_col) if fits else plain_body,
        mesh=mesh,
        in_specs=placed,
        out_specs=P("row", "col"),
        check_vma=False,
    )
```

```python
import functools
import math

import jax
import jax.numpy as jnp
from jax import lax
from jax.experimental import pallas as pl
from jax.experimental.pallas import tpu as pltpu
from jax.sharding import PartitionSpec as P

BLK = 128
STRIP = 16
LEVELS = 32767.0
FINE = 64.0
VMEM = 24 * 1024 * 1024


def masked(values, flag):
    return values * jnp.full((1, BLK), flag.astype(jnp.float32)).astype(jnp.bfloat16)


def joined_tiles(grid):
    bands = [jnp.concatenate(t, axis=1) if len(t) > 1 else t[0] for t in grid]
    return jnp.concatenate(bands, axis=0) if len(bands) > 1 else bands[0]


def whole(shape):
    return pl.BlockSpec(shape, lambda i, *_: (0,) * len(shape))


def cost(flops, bytes_accessed):
    return pl.CostEstimate(flops=flops, bytes_accessed=bytes_accessed, transcendentals=0)


def params(limit=VMEM):
    return pltpu.CompilerParams(vmem_limit_bytes=limit)


class Table:
    def __init__(self, ref, pieces, a_tiles, b_all, c_all):
        self.ref, self.pieces = ref, pieces
        self.b_all, self.c_all = b_all, c_all
        self.r_at = pieces * (pieces + 2)
        self.s_at = self.r_at + a_tiles * b_all

    def block(self, e):
        return self.ref[e]

    def spot(self, target, e):
        return self.ref[(target + 1) * self.pieces + e]

    def column(self, target):
        return self.ref[(self.pieces + 1) * self.pieces + target]

    def r_flag(self, a, b):
        return self.ref[self.r_at + a * self.b_all + b]

    def s_flag(self, b, c):
        return self.ref[self.s_at + b * self.c_all + c]

    def order(self, o, b_all):
        return self.ref[self.s_at + b_all * self.c_all + o]


def select_copy(choice, sources, target, sem):
    for d, source in enumerate(sources):

        @pl.when(choice == d)
        def _(source=source):
            pltpu.make_async_copy(source, target, sem).start()

    return pltpu.make_async_copy(sources[0], target, sem)


def products(table, target, first, r_refs, s_refs, r_buf, s_buf, r_sem, s_sem, use):
    pieces, blocks, block, width = r_buf.shape
    cols = s_buf.shape[1]
    b_tiles, c_tiles = width // BLK, cols // BLK

    def r_copy(e, n):
        rows = pl.ds(pl.multiple_of(first + n * block, block), block)
        return pltpu.make_async_copy(r_refs[e].at[rows], r_buf.at[e, n], r_sem.at[e, n])

    waits = [
        select_copy(table.spot(target, e), s_refs, s_buf.at[pl.ds(e * width, width)], s_sem.at[e])
        for e in range(pieces)
    ]
    for n in range(blocks):
        for e in range(pieces):
            r_copy(e, n).start()
    for e in range(pieces):
        waits[e].wait()
        for t in range(b_tiles):
            for u in range(c_tiles):
                flag = table.s_flag(table.block(e) * b_tiles + t, table.column(target) * c_tiles + u)
                down = slice(e * width + t * BLK, e * width + (t + 1) * BLK)
                over = slice(u * BLK, (u + 1) * BLK)
                s_buf[down, over] = masked(s_buf[down, over], flag)

    def one(n, carry):
        for e in range(pieces):
            r_copy(e, n).wait()
        grid = []
        for t in range(block // BLK):
            a = first // BLK + n * (block // BLK) + t
            grid.append(
                [
                    masked(
                        r_buf[e, n, t * BLK : (t + 1) * BLK, u * BLK : (u + 1) * BLK],
                        table.r_flag(a, table.block(e) * b_tiles + u),
                    )
                    for e in range(pieces)
                    for u in range(b_tiles)
                ]
            )
        use(n, jnp.dot(joined_tiles(grid), s_buf[...], preferred_element_type=jnp.float32))
        return carry

    lax.fori_loop(0, blocks, one, 0)


def encode(total, out):
    rows, cols = total.shape
    group = rows // STRIP
    strip_row = lax.broadcasted_iota(jnp.int32, (STRIP, cols), 0)
    strip = jnp.zeros((STRIP, cols), jnp.float32)
    for g in range(STRIP):
        part = total[g * group : (g + 1) * group]
        top = jnp.max(jnp.max(jnp.abs(part), axis=0, keepdims=True), axis=1, keepdims=True)
        level = jnp.ceil(jnp.log2(jnp.maximum(top, 1e-37)) * FINE) + 1.0
        root = jnp.exp2(level * (-0.5 / FINE))
        code = jnp.clip(jnp.round(part * root * (root * LEVELS)), -LEVELS, LEVELS)
        out[g * group : (g + 1) * group] = code.astype(jnp.int16)
        strip = jnp.where(strip_row == g, level, strip)
    out[rows:] = strip.astype(jnp.int16)


def coded_kernel(sizes, target, first, numbers, *refs):
    *ins, out, r_buf, s_buf, r_sem, s_sem = refs
    pieces = r_buf.shape[0]

    def use(n, total):
        encode(total, out.at[n])

    products(
        Table(numbers, *sizes), target, first, ins[:pieces], ins[pieces:],
        r_buf, s_buf, r_sem, s_sem, use,
    )


def own_kernel(sizes, count, numbers, *refs):
    *ins, out, mirror, r_buf, s_buf, r_sem, s_sem, t_sem = refs
    pieces = r_buf.shape[0]
    t_refs = ins[pieces + count :]
    blocks, block, _ = mirror.shape
    a_part = t_refs[0].shape[0]
    split = block // a_part
    table = Table(numbers, *sizes)
    waits = []
    for o in range(blocks * split):
        rows = pl.ds(o % split * a_part, a_part)
        waits.append(select_copy(table.order(o, sizes[2]), t_refs, mirror.at[o // split, rows], t_sem.at[o]))

    def use(n, total):
        out[n] = total

    products(
        table, 0, 0, ins[:pieces], ins[pieces : pieces + count],
        r_buf, s_buf, r_sem, s_sem, use,
    )
    for wait in waits:
        wait.wait()


SCALARS = pl.BlockSpec(memory_space=pltpu.SMEM)
ANYWHERE = pl.BlockSpec(memory_space=pl.ANY)
INSIDE = pl.BlockSpec(memory_space=pltpu.VMEM)


def product_scratch(pieces, blocks, block, width, cols):
    return [
        pltpu.VMEM((pieces, blocks, block, width), jnp.bfloat16),
        pltpu.VMEM((pieces * width, cols), jnp.bfloat16),
        pltpu.SemaphoreType.DMA((pieces, blocks)),
        pltpu.SemaphoreType.DMA((pieces,)),
    ]


def coded_product(sizes, table, r_pieces, s_pieces, target, block, first, blocks):
    pieces = len(r_pieces)
    width, cols = s_pieces[0].shape
    return pl.pallas_call(
        functools.partial(coded_kernel, sizes, target, first),
        out_shape=pltpu.VMEM((blocks, block + STRIP, cols), jnp.int16),
        in_specs=[SCALARS] + [ANYWHERE] * (pieces + len(s_pieces)),
        out_specs=INSIDE,
        scratch_shapes=product_scratch(pieces, blocks, block, width, cols),
        compiler_params=params(),
        cost_estimate=cost(2 * blocks * block * pieces * width * cols // 16, 0),
    )(table, *r_pieces, *s_pieces)


def own_product(sizes, table, r_pieces, s_pieces, t_pieces, block):
    pieces = len(r_pieces)
    width, cols = s_pieces[0].shape
    blocks = r_pieces[0].shape[0] // block
    return pl.pallas_call(
        functools.partial(own_kernel, sizes, len(s_pieces)),
        out_shape=[
            pltpu.VMEM((blocks, block, cols), jnp.float32),
            pltpu.VMEM((blocks, block, cols), jnp.bfloat16),
        ],
        in_specs=[SCALARS] + [ANYWHERE] * (pieces + len(s_pieces) + len(t_pieces)),
        out_specs=[INSIDE] * 2,
        scratch_shapes=product_scratch(pieces, blocks, block, width, cols)
        + [pltpu.SemaphoreType.DMA((len(t_pieces),))],
        compiler_params=params(),
        cost_estimate=cost(2 * blocks * block * pieces * width * cols // 16, 0),
    )(table, *r_pieces, *s_pieces, *t_pieces)


def join_kernel(parts, first, own, mirror, *refs):
    codes = refs[:parts]
    out, o_buf, roots, o_sem = refs[-4:]
    blocks, block, cols = o_buf.shape
    group = block // STRIP
    outs = []
    for n in range(blocks):
        for k in range(parts):
            level = codes[k][n, block:].astype(jnp.float32)
            roots[k] = jnp.exp2(level * (0.5 / FINE))
        for half in range(2):
            for g in range(half * STRIP // 2, (half + 1) * STRIP // 2):
                at = slice(g * group, (g + 1) * group)
                total = own[first + n, at]
                for k in range(parts):
                    root = roots[k, g : g + 1]
                    total += codes[k][n, at].astype(jnp.float32) * (root * (1.0 / LEVELS)) * root
                factor = mirror[first + n, at].astype(jnp.float32)
                o_buf[n, at] = (total * factor).astype(jnp.bfloat16)
            here = pl.ds(half * block // 2, block // 2)
            rows = pl.ds((first + n) * block + half * block // 2, block // 2)
            outs.append(
                pltpu.make_async_copy(o_buf.at[n, here], out.at[rows], o_sem.at[n, half])
            )
            outs[-1].start()
    for copy in outs:
        copy.wait()


def in_vmem(values):
    return pltpu.with_memory_space_constraint(values, pltpu.VMEM)


def join(own, mirror, coded, first, before):
    steps, block, cols = own.shape
    blocks = coded[0].shape[0]
    aliases, carried = {}, ()
    if before is not None:
        aliases, carried = {2 + len(coded): 0}, (before,)
    return pl.pallas_call(
        functools.partial(join_kernel, len(coded), first),
        out_shape=jax.ShapeDtypeStruct((steps * block, cols), jnp.bfloat16),
        in_specs=[INSIDE] * (2 + len(coded)) + [ANYWHERE] * len(carried),
        out_specs=ANYWHERE,
        scratch_shapes=[
            pltpu.VMEM((blocks, block, cols), jnp.bfloat16),
            pltpu.VMEM((len(coded), STRIP, cols), jnp.float32),
            pltpu.SemaphoreType.DMA((blocks, 2)),
        ],
        input_output_aliases=aliases,
        compiler_params=params(),
        cost_estimate=cost(0, 0),
    )(own, mirror, *[in_vmem(codes) for codes in coded], *carried)


def turn_kernel(pieces, width, places, flags, t_ref, *outs):
    a_width = t_ref.shape[1]
    for e in range(pieces):

        def one(t, carry, e=e):
            start = pl.multiple_of(places[e] * width + t * BLK, BLK)
            over = pl.ds(pl.multiple_of(t * BLK, BLK), BLK)
            for u in range(a_width // BLK):
                tile = masked(
                    t_ref[pl.ds(start, BLK), u * BLK : (u + 1) * BLK],
                    flags[places[e] * (width // BLK) + t, u],
                )
                outs[e][u * BLK : (u + 1) * BLK, over] = tile.T
            return carry

        lax.fori_loop(0, width // BLK, one, 0)


def turn(places, flags, t_vals, c_width):
    pieces = t_vals.shape[0] // c_width
    shape = (t_vals.shape[1], c_width)
    return pl.pallas_call(
        functools.partial(turn_kernel, pieces, c_width),
        out_shape=[jax.ShapeDtypeStruct(shape, jnp.bfloat16)] * pieces,
        grid_spec=pltpu.PrefetchScalarGridSpec(
            num_scalar_prefetch=2,
            grid=(1,),
            in_specs=[whole(t_vals.shape)],
            out_specs=[whole(shape)] * pieces,
        ),
        compiler_params=params(),
        cost_estimate=cost(0, 4 * t_vals.size),
    )(places, flags, t_vals)


def body(n_row, n_col, r_vals, s_vals, t_vals, r_pattern, s_pattern, t_pattern):
    side = math.isqrt(n_col)
    row = lax.axis_index("row")
    col = lax.axis_index("col")
    line, kind = row // 2, row % 2
    y, x = col // side, col % side
    a_rows, b_width = r_vals.shape
    c_width = s_vals.shape[1]
    a_part = t_vals.shape[1]
    a_tiles, ap_tiles = a_rows // BLK, a_part // BLK
    along = kind == 1
    gather_at = jnp.where(along, x, y)
    target_at = jnp.where(along, y, x)
    axes = ("row", "col")

    def place(k, h, yy, xx):
        return (k * 2 + h) * n_col + yy * side + xx

    def shifted(e, gather):
        pairs = []
        for k in range(n_row // 2):
            for h in range(2):
                for yy in range(side):
                    for xx in range(side):
                        if (h == 1) == gather:
                            to = (yy, (xx + e) % side)
                        else:
                            to = ((yy + e) % side, xx)
                        pairs.append((place(k, h, yy, xx), place(k, h, *to)))
        return pairs

    r_pieces = [r_vals] + [lax.ppermute(r_vals, axes, shifted(e, True)) for e in range(1, side)]

    flat = n_col & (n_col - 1) == 0
    if side == 2:
        first = jnp.where(along, 2, 1)
        partner = [col, col ^ first, col ^ (3 - first), col ^ 3]
    else:
        partner = [(col ^ e) if flat else (col + e) % n_col for e in range(n_col)]
    t_flags = lax.dynamic_slice_in_dim(t_pattern, (row * n_col + col) * ap_tiles, ap_tiles, 1)
    turned = turn(jnp.stack(partner).astype(jnp.int32), t_flags, t_vals, c_width)
    same, other = [], []
    for a in range(side):
        for b in range(side):
            for c in range(side):
                for d in range(side):
                    k = a * side + b
                    to_odd = (c * side + b, 1, a, d)
                    to_even = (a * side + d, 0, c, b)
                    same.append((place(k, 0, c, d), place(*to_even)))
                    same.append((place(k, 1, c, d), place(*to_odd)))
                    other.append((place(k, 1, c, d), place(*to_even)))
                    other.append((place(k, 0, c, d), place(*to_odd)))
    s_same = lax.ppermute(s_vals, axes, same)
    s_other = lax.ppermute(s_vals, axes, other)
    s_held = jnp.concatenate(
        [jnp.where(along, s_other, s_same), jnp.where(along, s_same, s_other)], axis=0
    )

    def to_partner(e, values):
        pairs = []
        for i in range(n_row):
            for j in range(n_col):
                if side == 2:
                    to = j ^ (3 if e == 3 else (1, 2)[(e + i + 1) % 2])
                else:
                    to = (j ^ e) if flat else (j + e) % n_col
                pairs.append((i * n_col + j, i * n_col + to))
        return lax.ppermute(values, axes, pairs)

    t_pieces = [turned[0], to_partner(1, turned[1])]

    def along_line(values, hop):
        pairs = [(k * 2 + h, hop(k) * 2 + h) for k in range(n_col) for h in range(2)]
        return lax.ppermute(values, "row", pairs)

    if flat:
        got = {0: s_held}
        bit = n_col // 2
        while bit:
            got |= {m | bit: along_line(v, lambda k, bit=bit: k ^ bit) for m, v in got.items()}
            if len(got) == 2:
                got[bit], *turned = lax.optimization_barrier((got[bit], *turned))
            bit //= 2
        s_pieces = [got[m] for m in range(n_col)]
    else:
        s_pieces = [s_held] + [
            along_line(s_held, lambda k, d=d: (k + d) % n_col) for d in range(1, n_col)
        ]

    t_pieces += [to_partner(e, turned[e]) for e in range(2, n_col)]

    r_flags = lax.dynamic_slice_in_dim(r_pattern, row * a_tiles, a_tiles, 0)
    flags = [r_flags.reshape(-1), s_pattern.reshape(-1)]
    sizes = (side, a_tiles, r_pattern.shape[1], s_pattern.shape[1])

    blocks, spots, targets = [], [], []
    for e in range(side):
        g = (gather_at - e) % side
        blocks.append(jnp.where(along, y * side + g, g * side + x))
    for t in range(side):
        target = (target_at + t) % side
        for e in range(side):
            g = (gather_at - e) % side
            k = jnp.where(along, target * side + g, g * side + target)
            spots.append((line ^ k) if flat else (line - k) % n_col)
        targets.append(jnp.where(along, target * side + x, y * side + target))
    order = [(col ^ o) if flat else (col - o) % n_col for o in range(n_col)]
    if side == 2:
        order = [jnp.where(along & (m % 3 > 0), 3 - m, m) for m in order]
    table = jnp.concatenate(
        [jnp.stack(blocks + spots + targets).astype(jnp.int32), *flags, jnp.stack(order).astype(jnp.int32)]
    )

    block = max(a_part, math.gcd(a_rows, 4 * BLK))
    steps = a_rows // block
    chunks = 2 if steps % 2 == 0 else 1
    steps //= chunks
    coded = []
    for chunk in range(chunks):
        parts = []
        for e in range(1, side):
            codes = coded_product(
                sizes, table, r_pieces, s_pieces, e, block, chunk * steps * block, steps
            )
            if chunk:
                codes, *t_pieces[1:] = lax.optimization_barrier((codes, *t_pieces[1:]))
            parts.append(lax.ppermute(codes, axes, shifted(e, False)))
        coded.append(parts)
    own, mirror = own_product(
        sizes, table, r_pieces, s_pieces, t_pieces, block
    )
    own, mirror = in_vmem(own), in_vmem(mirror)
    out = None
    for chunk in range(chunks):
        out = join(own, mirror, coded[chunk], chunk * steps, out)
    return out


def plain_body(r_vals, s_vals, t_vals, r_pattern, s_pattern, t_pattern):
    row, col = lax.axis_index("row"), lax.axis_index("col")
    s_all = lax.all_gather(s_vals, "row", axis=0, tiled=True)
    r_all = lax.all_gather(r_vals, "col", axis=1, tiled=True)
    t_all = lax.all_to_all(t_vals, "col", split_axis=0, concat_axis=1, tiled=True)
    a_tiles, c_tiles = r_vals.shape[0] // BLK, s_vals.shape[1] // BLK

    def spread(flags):
        return jnp.repeat(jnp.repeat(flags.astype(jnp.bfloat16), BLK, axis=0), BLK, axis=1)

    r_flags = lax.dynamic_slice_in_dim(r_pattern, row * a_tiles, a_tiles, 0)
    s_flags = lax.dynamic_slice_in_dim(s_pattern, col * c_tiles, c_tiles, 1)
    t_flags = lax.dynamic_slice(t_pattern, (col * c_tiles, row * a_tiles), (c_tiles, a_tiles))
    paths = jnp.dot(
        r_all * spread(r_flags), s_all * spread(s_flags), preferred_element_type=jnp.float32
    )
    mirror = (t_all * spread(t_flags)).T
    return (paths * mirror.astype(jnp.float32)).astype(jnp.bfloat16)


def solution(mesh):
    placed = (P("row", "col"), P("row", "col"), P(None, ("row", "col")), P(), P(), P())
    n_row, n_col = mesh.shape["row"], mesh.shape["col"]
    fits = n_row == 2 * n_col and math.isqrt(n_col) ** 2 == n_col > 1
    return jax.shard_map(
        functools.partial(body, n_row, n_col) if fits else plain_body,
        mesh=mesh,
        in_specs=placed,
        out_specs=P("row", "col"),
        check_vma=False,
    )
```

```python
import functools
import math

import jax
import jax.numpy as jnp
from jax import lax
from jax.experimental import pallas as pl
from jax.experimental.pallas import tpu as pltpu
from jax.sharding import PartitionSpec as P

BLK = 128
STRIP = 16
LEVELS = 32767.0
FINE = 64.0
VMEM = 24 * 1024 * 1024


def masked(values, flag):
    return values * jnp.full((1, BLK), flag.astype(jnp.float32)).astype(jnp.bfloat16)


def joined_tiles(grid):
    bands = [jnp.concatenate(t, axis=1) if len(t) > 1 else t[0] for t in grid]
    return jnp.concatenate(bands, axis=0) if len(bands) > 1 else bands[0]


def whole(shape):
    return pl.BlockSpec(shape, lambda i, *_: (0,) * len(shape))


def cost(flops, bytes_accessed):
    return pl.CostEstimate(flops=flops, bytes_accessed=bytes_accessed, transcendentals=0)


def params(limit=VMEM):
    return pltpu.CompilerParams(vmem_limit_bytes=limit)


class Table:
    def __init__(self, ref, pieces, a_tiles, b_all, c_all):
        self.ref, self.pieces = ref, pieces
        self.b_all, self.c_all = b_all, c_all
        self.r_at = pieces * (pieces + 2)
        self.s_at = self.r_at + a_tiles * b_all

    def block(self, e):
        return self.ref[e]

    def spot(self, target, e):
        return self.ref[(target + 1) * self.pieces + e]

    def column(self, target):
        return self.ref[(self.pieces + 1) * self.pieces + target]

    def r_flag(self, a, b):
        return self.ref[self.r_at + a * self.b_all + b]

    def s_flag(self, b, c):
        return self.ref[self.s_at + b * self.c_all + c]

    def order(self, o, b_all):
        return self.ref[self.s_at + b_all * self.c_all + o]


def select_copy(choice, sources, target, sem):
    for d, source in enumerate(sources):

        @pl.when(choice == d)
        def _(source=source):
            pltpu.make_async_copy(source, target, sem).start()

    return pltpu.make_async_copy(sources[0], target, sem)


def products(table, target, first, r_refs, s_refs, r_buf, s_buf, r_sem, s_sem, use):
    pieces, blocks, block, width = r_buf.shape
    cols = s_buf.shape[1]
    b_tiles, c_tiles = width // BLK, cols // BLK

    def r_copy(e, n):
        rows = pl.ds(pl.multiple_of(first + n * block, block), block)
        return pltpu.make_async_copy(r_refs[e].at[rows], r_buf.at[e, n], r_sem.at[e, n])

    waits = [
        select_copy(table.spot(target, e), s_refs, s_buf.at[pl.ds(e * width, width)], s_sem.at[e])
        for e in range(pieces)
    ]
    for n in range(blocks):
        for e in range(pieces):
            r_copy(e, n).start()
    for e in range(pieces):
        waits[e].wait()
        for t in range(b_tiles):
            for u in range(c_tiles):
                flag = table.s_flag(table.block(e) * b_tiles + t, table.column(target) * c_tiles + u)
                down = slice(e * width + t * BLK, e * width + (t + 1) * BLK)
                over = slice(u * BLK, (u + 1) * BLK)
                s_buf[down, over] = masked(s_buf[down, over], flag)

    def one(n, carry):
        for e in range(pieces):
            r_copy(e, n).wait()
        grid = []
        for t in range(block // BLK):
            a = first // BLK + n * (block // BLK) + t
            grid.append(
                [
                    masked(
                        r_buf[e, n, t * BLK : (t + 1) * BLK, u * BLK : (u + 1) * BLK],
                        table.r_flag(a, table.block(e) * b_tiles + u),
                    )
                    for e in range(pieces)
                    for u in range(b_tiles)
                ]
            )
        use(n, jnp.dot(joined_tiles(grid), s_buf[...], preferred_element_type=jnp.float32))
        return carry

    lax.fori_loop(0, blocks, one, 0)


def encode(total, out):
    rows, cols = total.shape
    group = rows // STRIP
    strip_row = lax.broadcasted_iota(jnp.int32, (STRIP, cols), 0)
    strip = jnp.zeros((STRIP, cols), jnp.float32)
    for g in range(STRIP):
        part = total[g * group : (g + 1) * group]
        top = jnp.max(jnp.max(jnp.abs(part), axis=0, keepdims=True), axis=1, keepdims=True)
        level = jnp.ceil(jnp.log2(jnp.maximum(top, 1e-37)) * FINE) + 1.0
        root = jnp.exp2(level * (-0.5 / FINE))
        code = jnp.clip(jnp.round(part * root * (root * LEVELS)), -LEVELS, LEVELS)
        out[g * group : (g + 1) * group] = code.astype(jnp.int16)
        strip = jnp.where(strip_row == g, level, strip)
    out[rows:] = strip.astype(jnp.int16)


def coded_kernel(sizes, target, first, numbers, *refs):
    *ins, out, r_buf, s_buf, r_sem, s_sem = refs
    pieces = r_buf.shape[0]

    def use(n, total):
        encode(total, out.at[n])

    products(
        Table(numbers, *sizes), target, first, ins[:pieces], ins[pieces:],
        r_buf, s_buf, r_sem, s_sem, use,
    )


def own_kernel(sizes, count, numbers, *refs):
    *ins, out, mirror, r_buf, s_buf, r_sem, s_sem, t_sem = refs
    pieces = r_buf.shape[0]
    t_refs = ins[pieces + count :]
    blocks, block, _ = mirror.shape
    a_part = t_refs[0].shape[0]
    split = block // a_part
    table = Table(numbers, *sizes)
    waits = []
    for o in range(blocks * split):
        rows = pl.ds(o % split * a_part, a_part)
        waits.append(select_copy(table.order(o, sizes[2]), t_refs, mirror.at[o // split, rows], t_sem.at[o]))

    def use(n, total):
        out[n] = total

    products(
        table, 0, 0, ins[:pieces], ins[pieces : pieces + count],
        r_buf, s_buf, r_sem, s_sem, use,
    )
    for wait in waits:
        wait.wait()


SCALARS = pl.BlockSpec(memory_space=pltpu.SMEM)
ANYWHERE = pl.BlockSpec(memory_space=pl.ANY)
INSIDE = pl.BlockSpec(memory_space=pltpu.VMEM)


def product_scratch(pieces, blocks, block, width, cols):
    return [
        pltpu.VMEM((pieces, blocks, block, width), jnp.bfloat16),
        pltpu.VMEM((pieces * width, cols), jnp.bfloat16),
        pltpu.SemaphoreType.DMA((pieces, blocks)),
        pltpu.SemaphoreType.DMA((pieces,)),
    ]


def coded_product(sizes, table, r_pieces, s_pieces, target, block, first, blocks):
    pieces = len(r_pieces)
    width, cols = s_pieces[0].shape
    return pl.pallas_call(
        functools.partial(coded_kernel, sizes, target, first),
        out_shape=pltpu.VMEM((blocks, block + STRIP, cols), jnp.int16),
        in_specs=[SCALARS] + [ANYWHERE] * (pieces + len(s_pieces)),
        out_specs=INSIDE,
        scratch_shapes=product_scratch(pieces, blocks, block, width, cols),
        compiler_params=params(),
        cost_estimate=cost(2 * blocks * block * pieces * width * cols // 16, 0),
    )(table, *r_pieces, *s_pieces)


def own_product(sizes, table, r_pieces, s_pieces, t_pieces, block):
    pieces = len(r_pieces)
    width, cols = s_pieces[0].shape
    blocks = r_pieces[0].shape[0] // block
    return pl.pallas_call(
        functools.partial(own_kernel, sizes, len(s_pieces)),
        out_shape=[
            pltpu.VMEM((blocks, block, cols), jnp.float32),
            pltpu.VMEM((blocks, block, cols), jnp.bfloat16),
        ],
        in_specs=[SCALARS] + [ANYWHERE] * (pieces + len(s_pieces) + len(t_pieces)),
        out_specs=[INSIDE] * 2,
        scratch_shapes=product_scratch(pieces, blocks, block, width, cols)
        + [pltpu.SemaphoreType.DMA((len(t_pieces),))],
        compiler_params=params(),
        cost_estimate=cost(2 * blocks * block * pieces * width * cols // 16, 0),
    )(table, *r_pieces, *s_pieces, *t_pieces)


def join_kernel(parts, first, own, mirror, *refs):
    codes = refs[:parts]
    out, o_buf, roots, o_sem = refs[-4:]
    blocks, block, cols = o_buf.shape
    group = block // STRIP
    outs = []
    for n in range(blocks):
        for k in range(parts):
            level = codes[k][n, block:].astype(jnp.float32)
            roots[k] = jnp.exp2(level * (0.5 / FINE))
        for half in range(2):
            for g in range(half * STRIP // 2, (half + 1) * STRIP // 2):
                at = slice(g * group, (g + 1) * group)
                total = own[first + n, at]
                for k in range(parts):
                    root = roots[k, g : g + 1]
                    total += codes[k][n, at].astype(jnp.float32) * (root * (1.0 / LEVELS)) * root
                factor = mirror[first + n, at].astype(jnp.float32)
                o_buf[n, at] = (total * factor).astype(jnp.bfloat16)
            here = pl.ds(half * block // 2, block // 2)
            rows = pl.ds((first + n) * block + half * block // 2, block // 2)
            outs.append(
                pltpu.make_async_copy(o_buf.at[n, here], out.at[rows], o_sem.at[n, half])
            )
            outs[-1].start()
    for copy in outs:
        copy.wait()


def in_vmem(values):
    return pltpu.with_memory_space_constraint(values, pltpu.VMEM)


def join(own, mirror, coded, first, before):
    steps, block, cols = own.shape
    blocks = coded[0].shape[0]
    aliases, carried = {}, ()
    if before is not None:
        aliases, carried = {2 + len(coded): 0}, (before,)
    return pl.pallas_call(
        functools.partial(join_kernel, len(coded), first),
        out_shape=jax.ShapeDtypeStruct((steps * block, cols), jnp.bfloat16),
        in_specs=[INSIDE] * (2 + len(coded)) + [ANYWHERE] * len(carried),
        out_specs=ANYWHERE,
        scratch_shapes=[
            pltpu.VMEM((blocks, block, cols), jnp.bfloat16),
            pltpu.VMEM((len(coded), STRIP, cols), jnp.float32),
            pltpu.SemaphoreType.DMA((blocks, 2)),
        ],
        input_output_aliases=aliases,
        compiler_params=params(),
        cost_estimate=cost(0, 0),
    )(own, mirror, *[in_vmem(codes) for codes in coded], *carried)


def turn_kernel(pieces, width, places, flags, t_ref, *outs):
    a_width = t_ref.shape[1]
    for e in range(pieces):

        def one(t, carry, e=e):
            start = pl.multiple_of(places[e] * width + t * BLK, BLK)
            over = pl.ds(pl.multiple_of(t * BLK, BLK), BLK)
            for u in range(a_width // BLK):
                tile = masked(
                    t_ref[pl.ds(start, BLK), u * BLK : (u + 1) * BLK],
                    flags[places[e] * (width // BLK) + t, u],
                )
                outs[e][u * BLK : (u + 1) * BLK, over] = tile.T
            return carry

        lax.fori_loop(0, width // BLK, one, 0)


def turn(places, flags, t_vals, c_width):
    pieces = t_vals.shape[0] // c_width
    shape = (t_vals.shape[1], c_width)
    return pl.pallas_call(
        functools.partial(turn_kernel, pieces, c_width),
        out_shape=[jax.ShapeDtypeStruct(shape, jnp.bfloat16)] * pieces,
        grid_spec=pltpu.PrefetchScalarGridSpec(
            num_scalar_prefetch=2,
            grid=(1,),
            in_specs=[whole(t_vals.shape)],
            out_specs=[whole(shape)] * pieces,
        ),
        compiler_params=params(),
        cost_estimate=cost(0, 4 * t_vals.size),
    )(places, flags, t_vals)


def body(n_row, n_col, r_vals, s_vals, t_vals, r_pattern, s_pattern, t_pattern):
    side = math.isqrt(n_col)
    row = lax.axis_index("row")
    col = lax.axis_index("col")
    line, kind = row // 2, row % 2
    y, x = col // side, col % side
    a_rows, b_width = r_vals.shape
    c_width = s_vals.shape[1]
    a_part = t_vals.shape[1]
    a_tiles, ap_tiles = a_rows // BLK, a_part // BLK
    along = kind == 1
    gather_at = jnp.where(along, x, y)
    target_at = jnp.where(along, y, x)
    axes = ("row", "col")

    def place(k, h, yy, xx):
        return (k * 2 + h) * n_col + yy * side + xx

    def shifted(e, gather):
        pairs = []
        for k in range(n_row // 2):
            for h in range(2):
                for yy in range(side):
                    for xx in range(side):
                        if (h == 1) == gather:
                            to = (yy, (xx + e) % side)
                        else:
                            to = ((yy + e) % side, xx)
                        pairs.append((place(k, h, yy, xx), place(k, h, *to)))
        return pairs

    r_pieces = [r_vals] + [lax.ppermute(r_vals, axes, shifted(e, True)) for e in range(1, side)]

    flat = n_col & (n_col - 1) == 0
    if side == 2:
        first = jnp.where(along, 1, 2)
        partner = [col, col ^ first, col ^ (3 - first), col ^ 3]
    else:
        partner = [(col ^ e) if flat else (col + e) % n_col for e in range(n_col)]
    t_flags = lax.dynamic_slice_in_dim(t_pattern, (row * n_col + col) * ap_tiles, ap_tiles, 1)
    turned = turn(jnp.stack(partner).astype(jnp.int32), t_flags, t_vals, c_width)
    same, other = [], []
    for a in range(side):
        for b in range(side):
            for c in range(side):
                for d in range(side):
                    k = a * side + b
                    to_odd = (c * side + b, 1, a, d)
                    to_even = (a * side + d, 0, c, b)
                    same.append((place(k, 0, c, d), place(*to_even)))
                    same.append((place(k, 1, c, d), place(*to_odd)))
                    other.append((place(k, 1, c, d), place(*to_even)))
                    other.append((place(k, 0, c, d), place(*to_odd)))
    s_same = lax.ppermute(s_vals, axes, same)
    s_other = lax.ppermute(s_vals, axes, other)
    s_held = jnp.concatenate(
        [jnp.where(along, s_other, s_same), jnp.where(along, s_same, s_other)], axis=0
    )

    def to_partner(e, values):
        pairs = []
        for i in range(n_row):
            for j in range(n_col):
                if side == 2:
                    to = j ^ (3 if e == 3 else (1, 2)[(e + i) % 2])
                else:
                    to = (j ^ e) if flat else (j + e) % n_col
                pairs.append((i * n_col + j, i * n_col + to))
        return lax.ppermute(values, axes, pairs)

    t_pieces = [turned[0], to_partner(1, turned[1])]

    def along_line(values, hop):
        pairs = [(k * 2 + h, hop(k) * 2 + h) for k in range(n_col) for h in range(2)]
        return lax.ppermute(values, "row", pairs)

    if flat:
        got = {0: s_held}
        bit = n_col // 2
        while bit:
            got |= {m | bit: along_line(v, lambda k, bit=bit: k ^ bit) for m, v in got.items()}
            if len(got) == 2:
                got[bit], *turned = lax.optimization_barrier((got[bit], *turned))
            bit //= 2
        s_pieces = [got[m] for m in range(n_col)]
    else:
        s_pieces = [s_held] + [
            along_line(s_held, lambda k, d=d: (k + d) % n_col) for d in range(1, n_col)
        ]

    t_pieces += [to_partner(e, turned[e]) for e in range(2, n_col)]

    r_flags = lax.dynamic_slice_in_dim(r_pattern, row * a_tiles, a_tiles, 0)
    flags = [r_flags.reshape(-1), s_pattern.reshape(-1)]
    sizes = (side, a_tiles, r_pattern.shape[1], s_pattern.shape[1])

    blocks, spots, targets = [], [], []
    for e in range(side):
        g = (gather_at - e) % side
        blocks.append(jnp.where(along, y * side + g, g * side + x))
    for t in range(side):
        target = (target_at + t) % side
        for e in range(side):
            g = (gather_at - e) % side
            k = jnp.where(along, target * side + g, g * side + target)
            spots.append((line ^ k) if flat else (line - k) % n_col)
        targets.append(jnp.where(along, target * side + x, y * side + target))
    order = [(col ^ o) if flat else (col - o) % n_col for o in range(n_col)]
    if side == 2:
        order = [jnp.where(~along & (m % 3 > 0), 3 - m, m) for m in order]
    table = jnp.concatenate(
        [jnp.stack(blocks + spots + targets).astype(jnp.int32), *flags, jnp.stack(order).astype(jnp.int32)]
    )

    block = max(a_part, math.gcd(a_rows, 4 * BLK))
    steps = a_rows // block
    chunks = 2 if steps % 2 == 0 else 1
    steps //= chunks
    coded = []
    for chunk in range(chunks):
        parts = []
        for e in range(1, side):
            codes = coded_product(
                sizes, table, r_pieces, s_pieces, e, block, chunk * steps * block, steps
            )
            if chunk:
                codes, *t_pieces[1:] = lax.optimization_barrier((codes, *t_pieces[1:]))
            parts.append(lax.ppermute(codes, axes, shifted(e, False)))
        coded.append(parts)
    own, mirror = own_product(
        sizes, table, r_pieces, s_pieces, t_pieces, block
    )
    own, mirror = in_vmem(own), in_vmem(mirror)
    out = None
    for chunk in range(chunks):
        out = join(own, mirror, coded[chunk], chunk * steps, out)
    return out


def plain_body(r_vals, s_vals, t_vals, r_pattern, s_pattern, t_pattern):
    row, col = lax.axis_index("row"), lax.axis_index("col")
    s_all = lax.all_gather(s_vals, "row", axis=0, tiled=True)
    r_all = lax.all_gather(r_vals, "col", axis=1, tiled=True)
    t_all = lax.all_to_all(t_vals, "col", split_axis=0, concat_axis=1, tiled=True)
    a_tiles, c_tiles = r_vals.shape[0] // BLK, s_vals.shape[1] // BLK

    def spread(flags):
        return jnp.repeat(jnp.repeat(flags.astype(jnp.bfloat16), BLK, axis=0), BLK, axis=1)

    r_flags = lax.dynamic_slice_in_dim(r_pattern, row * a_tiles, a_tiles, 0)
    s_flags = lax.dynamic_slice_in_dim(s_pattern, col * c_tiles, c_tiles, 1)
    t_flags = lax.dynamic_slice(t_pattern, (col * c_tiles, row * a_tiles), (c_tiles, a_tiles))
    paths = jnp.dot(
        r_all * spread(r_flags), s_all * spread(s_flags), preferred_element_type=jnp.float32
    )
    mirror = (t_all * spread(t_flags)).T
    return (paths * mirror.astype(jnp.float32)).astype(jnp.bfloat16)


def solution(mesh):
    placed = (P("row", "col"), P("row", "col"), P(None, ("row", "col")), P(), P(), P())
    n_row, n_col = mesh.shape["row"], mesh.shape["col"]
    fits = n_row == 2 * n_col and math.isqrt(n_col) ** 2 == n_col > 1
    return jax.shard_map(
        functools.partial(body, n_row, n_col) if fits else plain_body,
        mesh=mesh,
        in_specs=placed,
        out_specs=P("row", "col"),
        check_vma=False,
    )
```

```python
import functools
import math

import jax
import jax.numpy as jnp
from jax import lax
from jax.experimental import pallas as pl
from jax.experimental.pallas import tpu as pltpu
from jax.sharding import PartitionSpec as P

BLK = 128
STRIP = 16
LEVELS = 32767.0
FINE = 64.0
VMEM = 24 * 1024 * 1024


def masked(values, flag):
    return values * jnp.full((1, BLK), flag.astype(jnp.float32)).astype(jnp.bfloat16)


def joined_tiles(grid):
    bands = [jnp.concatenate(t, axis=1) if len(t) > 1 else t[0] for t in grid]
    return jnp.concatenate(bands, axis=0) if len(bands) > 1 else bands[0]


def whole(shape):
    return pl.BlockSpec(shape, lambda i, *_: (0,) * len(shape))


def cost(flops, bytes_accessed):
    return pl.CostEstimate(flops=flops, bytes_accessed=bytes_accessed, transcendentals=0)


def params(limit=VMEM):
    return pltpu.CompilerParams(vmem_limit_bytes=limit)


class Table:
    def __init__(self, ref, pieces, a_tiles, b_all, c_all):
        self.ref, self.pieces = ref, pieces
        self.b_all, self.c_all = b_all, c_all
        self.r_at = pieces * (pieces + 2)
        self.s_at = self.r_at + a_tiles * b_all

    def block(self, e):
        return self.ref[e]

    def spot(self, target, e):
        return self.ref[(target + 1) * self.pieces + e]

    def column(self, target):
        return self.ref[(self.pieces + 1) * self.pieces + target]

    def r_flag(self, a, b):
        return self.ref[self.r_at + a * self.b_all + b]

    def s_flag(self, b, c):
        return self.ref[self.s_at + b * self.c_all + c]


def select_copy(choice, sources, target, sem):
    for d, source in enumerate(sources):

        @pl.when(choice == d)
        def _(source=source):
            pltpu.make_async_copy(source, target, sem).start()

    return pltpu.make_async_copy(sources[0], target, sem)


def products(table, target, first, r_refs, s_refs, r_buf, s_buf, r_sem, s_sem, use):
    pieces, blocks, block, width = r_buf.shape
    cols = s_buf.shape[1]
    b_tiles, c_tiles = width // BLK, cols // BLK

    def r_copy(e, n):
        rows = pl.ds(pl.multiple_of(first + n * block, block), block)
        return pltpu.make_async_copy(r_refs[e].at[rows], r_buf.at[e, n], r_sem.at[e, n])

    waits = [
        select_copy(table.spot(target, e), s_refs, s_buf.at[pl.ds(e * width, width)], s_sem.at[e])
        for e in range(pieces)
    ]
    for n in range(blocks):
        for e in range(pieces):
            r_copy(e, n).start()
    for e in range(pieces):
        waits[e].wait()
        for t in range(b_tiles):
            for u in range(c_tiles):
                flag = table.s_flag(table.block(e) * b_tiles + t, table.column(target) * c_tiles + u)
                down = slice(e * width + t * BLK, e * width + (t + 1) * BLK)
                over = slice(u * BLK, (u + 1) * BLK)
                s_buf[down, over] = masked(s_buf[down, over], flag)

    def one(n, carry):
        for e in range(pieces):
            r_copy(e, n).wait()
        grid = []
        for t in range(block // BLK):
            a = first // BLK + n * (block // BLK) + t
            grid.append(
                [
                    masked(
                        r_buf[e, n, t * BLK : (t + 1) * BLK, u * BLK : (u + 1) * BLK],
                        table.r_flag(a, table.block(e) * b_tiles + u),
                    )
                    for e in range(pieces)
                    for u in range(b_tiles)
                ]
            )
        use(n, jnp.dot(joined_tiles(grid), s_buf[...], preferred_element_type=jnp.float32))
        return carry

    lax.fori_loop(0, blocks, one, 0)


def encode(total, out):
    rows, cols = total.shape
    group = rows // STRIP
    strip_row = lax.broadcasted_iota(jnp.int32, (STRIP, cols), 0)
    strip = jnp.zeros((STRIP, cols), jnp.float32)
    for g in range(STRIP):
        part = total[g * group : (g + 1) * group]
        top = jnp.max(jnp.max(jnp.abs(part), axis=0, keepdims=True), axis=1, keepdims=True)
        level = jnp.ceil(jnp.log2(jnp.maximum(top, 1e-37)) * FINE) + 1.0
        root = jnp.exp2(level * (-0.5 / FINE))
        code = jnp.clip(jnp.round(part * root * (root * LEVELS)), -LEVELS, LEVELS)
        out[g * group : (g + 1) * group] = code.astype(jnp.int16)
        strip = jnp.where(strip_row == g, level, strip)
    out[rows:] = strip.astype(jnp.int16)


def coded_kernel(sizes, target, first, numbers, *refs):
    *ins, out, r_buf, s_buf, r_sem, s_sem = refs
    pieces = r_buf.shape[0]

    def use(n, total):
        encode(total, out.at[n])

    products(
        Table(numbers, *sizes), target, first, ins[:pieces], ins[pieces:],
        r_buf, s_buf, r_sem, s_sem, use,
    )


def own_kernel(sizes, count, numbers, order, *refs):
    *ins, out, mirror, r_buf, s_buf, r_sem, s_sem, t_sem = refs
    pieces = r_buf.shape[0]
    t_refs = ins[pieces + count :]
    blocks, block, _ = mirror.shape
    a_part = t_refs[0].shape[0]
    split = block // a_part
    waits = []
    for o in range(blocks * split):
        rows = pl.ds(o % split * a_part, a_part)
        waits.append(select_copy(order[o], t_refs, mirror.at[o // split, rows], t_sem.at[o]))

    def use(n, total):
        out[n] = total

    products(
        Table(numbers, *sizes), 0, 0, ins[:pieces], ins[pieces : pieces + count],
        r_buf, s_buf, r_sem, s_sem, use,
    )
    for wait in waits:
        wait.wait()


SCALARS = pl.BlockSpec(memory_space=pltpu.SMEM)
ANYWHERE = pl.BlockSpec(memory_space=pl.ANY)
INSIDE = pl.BlockSpec(memory_space=pltpu.VMEM)


def product_scratch(pieces, blocks, block, width, cols):
    return [
        pltpu.VMEM((pieces, blocks, block, width), jnp.bfloat16),
        pltpu.VMEM((pieces * width, cols), jnp.bfloat16),
        pltpu.SemaphoreType.DMA((pieces, blocks)),
        pltpu.SemaphoreType.DMA((pieces,)),
    ]


def coded_product(sizes, table, r_pieces, s_pieces, target, block, first, blocks):
    pieces = len(r_pieces)
    width, cols = s_pieces[0].shape
    return pl.pallas_call(
        functools.partial(coded_kernel, sizes, target, first),
        out_shape=pltpu.VMEM((blocks, block + STRIP, cols), jnp.int16),
        in_specs=[SCALARS] + [ANYWHERE] * (pieces + len(s_pieces)),
        out_specs=INSIDE,
        scratch_shapes=product_scratch(pieces, blocks, block, width, cols),
        compiler_params=params(),
        cost_estimate=cost(2 * blocks * block * pieces * width * cols // 16, 0),
    )(table, *r_pieces, *s_pieces)


def own_product(sizes, table, order, r_pieces, s_pieces, t_pieces, block):
    pieces = len(r_pieces)
    width, cols = s_pieces[0].shape
    blocks = r_pieces[0].shape[0] // block
    return pl.pallas_call(
        functools.partial(own_kernel, sizes, len(s_pieces)),
        out_shape=[
            pltpu.VMEM((blocks, block, cols), jnp.float32),
            pltpu.VMEM((blocks, block, cols), jnp.bfloat16),
        ],
        in_specs=[SCALARS] * 2 + [ANYWHERE] * (pieces + len(s_pieces) + len(t_pieces)),
        out_specs=[INSIDE] * 2,
        scratch_shapes=product_scratch(pieces, blocks, block, width, cols)
        + [pltpu.SemaphoreType.DMA((len(t_pieces),))],
        compiler_params=params(),
        cost_estimate=cost(2 * blocks * block * pieces * width * cols // 16, 0),
    )(table, order, *r_pieces, *s_pieces, *t_pieces)


def join_kernel(parts, first, own, mirror, *refs):
    codes = refs[:parts]
    out, o_buf, roots, o_sem = refs[-4:]
    blocks, block, cols = o_buf.shape
    group = block // STRIP
    outs = []
    for n in range(blocks):
        for k in range(parts):
            level = codes[k][n, block:].astype(jnp.float32)
            roots[k] = jnp.exp2(level * (0.5 / FINE))
        for half in range(2):
            for g in range(half * STRIP // 2, (half + 1) * STRIP // 2):
                at = slice(g * group, (g + 1) * group)
                total = own[first + n, at]
                for k in range(parts):
                    root = roots[k, g : g + 1]
                    total += codes[k][n, at].astype(jnp.float32) * (root * (1.0 / LEVELS)) * root
                factor = mirror[first + n, at].astype(jnp.float32)
                o_buf[n, at] = (total * factor).astype(jnp.bfloat16)
            here = pl.ds(half * block // 2, block // 2)
            rows = pl.ds((first + n) * block + half * block // 2, block // 2)
            outs.append(
                pltpu.make_async_copy(o_buf.at[n, here], out.at[rows], o_sem.at[n, half])
            )
            outs[-1].start()
    for copy in outs:
        copy.wait()


def in_vmem(values):
    return pltpu.with_memory_space_constraint(values, pltpu.VMEM)


def join(own, mirror, coded, first, before):
    steps, block, cols = own.shape
    blocks = coded[0].shape[0]
    aliases, carried = {}, ()
    if before is not None:
        aliases, carried = {2 + len(coded): 0}, (before,)
    return pl.pallas_call(
        functools.partial(join_kernel, len(coded), first),
        out_shape=jax.ShapeDtypeStruct((steps * block, cols), jnp.bfloat16),
        in_specs=[INSIDE] * (2 + len(coded)) + [ANYWHERE] * len(carried),
        out_specs=ANYWHERE,
        scratch_shapes=[
            pltpu.VMEM((blocks, block, cols), jnp.bfloat16),
            pltpu.VMEM((len(coded), STRIP, cols), jnp.float32),
            pltpu.SemaphoreType.DMA((blocks, 2)),
        ],
        input_output_aliases=aliases,
        compiler_params=params(),
        cost_estimate=cost(0, 0),
    )(own, mirror, *[in_vmem(codes) for codes in coded], *carried)


def turn_kernel(pieces, width, places, flags, t_ref, *outs):
    a_width = t_ref.shape[1]
    for e in range(pieces):

        def one(t, carry, e=e):
            start = pl.multiple_of(places[e] * width + t * BLK, BLK)
            over = pl.ds(pl.multiple_of(t * BLK, BLK), BLK)
            for u in range(a_width // BLK):
                tile = masked(
                    t_ref[pl.ds(start, BLK), u * BLK : (u + 1) * BLK],
                    flags[places[e] * (width // BLK) + t, u],
                )
                outs[e][u * BLK : (u + 1) * BLK, over] = tile.T
            return carry

        lax.fori_loop(0, width // BLK, one, 0)


def turn(places, flags, t_vals, c_width):
    pieces = t_vals.shape[0] // c_width
    shape = (t_vals.shape[1], c_width)
    return pl.pallas_call(
        functools.partial(turn_kernel, pieces, c_width),
        out_shape=[jax.ShapeDtypeStruct(shape, jnp.bfloat16)] * pieces,
        grid_spec=pltpu.PrefetchScalarGridSpec(
            num_scalar_prefetch=2,
            grid=(1,),
            in_specs=[whole(t_vals.shape)],
            out_specs=[whole(shape)] * pieces,
        ),
        compiler_params=params(),
        cost_estimate=cost(0, 4 * t_vals.size),
    )(places, flags, t_vals)


def body(n_row, n_col, r_vals, s_vals, t_vals, r_pattern, s_pattern, t_pattern):
    side = math.isqrt(n_col)
    row = lax.axis_index("row")
    col = lax.axis_index("col")
    line, kind = row // 2, row % 2
    y, x = col // side, col % side
    a_rows, b_width = r_vals.shape
    c_width = s_vals.shape[1]
    a_part = t_vals.shape[1]
    a_tiles, ap_tiles = a_rows // BLK, a_part // BLK
    along = kind == 1
    gather_at = jnp.where(along, x, y)
    target_at = jnp.where(along, y, x)
    axes = ("row", "col")

    def place(k, h, yy, xx):
        return (k * 2 + h) * n_col + yy * side + xx

    def shifted(e, gather):
        pairs = []
        for k in range(n_row // 2):
            for h in range(2):
                for yy in range(side):
                    for xx in range(side):
                        if (h == 1) == gather:
                            to = (yy, (xx + e) % side)
                        else:
                            to = ((yy + e) % side, xx)
                        pairs.append((place(k, h, yy, xx), place(k, h, *to)))
        return pairs

    r_pieces = [r_vals] + [lax.ppermute(r_vals, axes, shifted(e, True)) for e in range(1, side)]

    flat = n_col & (n_col - 1) == 0
    partner = [(col ^ e) if flat else (col + e) % n_col for e in range(n_col)]
    t_flags = lax.dynamic_slice_in_dim(t_pattern, (row * n_col + col) * ap_tiles, ap_tiles, 1)
    turned = turn(jnp.stack(partner).astype(jnp.int32), t_flags, t_vals, c_width)
    same, other = [], []
    for a in range(side):
        for b in range(side):
            for c in range(side):
                for d in range(side):
                    k = a * side + b
                    to_odd = (c * side + b, 1, a, d)
                    to_even = (a * side + d, 0, c, b)
                    same.append((place(k, 0, c, d), place(*to_even)))
                    same.append((place(k, 1, c, d), place(*to_odd)))
                    other.append((place(k, 1, c, d), place(*to_even)))
                    other.append((place(k, 0, c, d), place(*to_odd)))
    s_same = lax.ppermute(s_vals, axes, same)
    s_other = lax.ppermute(s_vals, axes, other)
    s_held = jnp.concatenate(
        [jnp.where(along, s_other, s_same), jnp.where(along, s_same, s_other)], axis=0
    )

    def along_line(values, hop):
        pairs = [(k * 2 + h, hop(k) * 2 + h) for k in range(n_col) for h in range(2)]
        return lax.ppermute(values, "row", pairs)

    if flat:
        got = {0: s_held}
        bit = n_col // 2
        while bit:
            got |= {m | bit: along_line(v, lambda k, bit=bit: k ^ bit) for m, v in got.items()}
            if len(got) == 2:
                got[bit], *turned = lax.optimization_barrier((got[bit], *turned))
            bit //= 2
        s_pieces = [got[m] for m in range(n_col)]
    else:
        s_pieces = [s_held] + [
            along_line(s_held, lambda k, d=d: (k + d) % n_col) for d in range(1, n_col)
        ]

    t_pieces = [turned[0]]
    for e in range(1, n_col):
        pairs = [(j, (j ^ e) if flat else (j + e) % n_col) for j in range(n_col)]
        t_pieces.append(lax.ppermute(turned[e], "col", pairs))

    r_flags = lax.dynamic_slice_in_dim(r_pattern, row * a_tiles, a_tiles, 0)
    flags = [r_flags.reshape(-1), s_pattern.reshape(-1)]
    sizes = (side, a_tiles, r_pattern.shape[1], s_pattern.shape[1])

    blocks, spots, targets = [], [], []
    for e in range(side):
        g = (gather_at - e) % side
        blocks.append(jnp.where(along, y * side + g, g * side + x))
    for t in range(side):
        target = (target_at + t) % side
        for e in range(side):
            g = (gather_at - e) % side
            k = jnp.where(along, target * side + g, g * side + target)
            spots.append((line ^ k) if flat else (line - k) % n_col)
        targets.append(jnp.where(along, target * side + x, y * side + target))
    table = jnp.concatenate([jnp.stack(blocks + spots + targets).astype(jnp.int32), *flags])

    block = max(a_part, math.gcd(a_rows, 4 * BLK))
    steps = a_rows // block
    chunks = [(0, steps - 1), (steps - 1, 1)] if steps > 1 else [(0, 1)]
    coded = []
    for first, count in chunks:
        parts = []
        for e in range(1, side):
            codes = coded_product(
                sizes, table, r_pieces, s_pieces, e, block, first * block, count
            )
            if first:
                codes, *t_pieces[1:] = lax.optimization_barrier((codes, *t_pieces[1:]))
            parts.append(lax.ppermute(codes, axes, shifted(e, False)))
        coded.append(parts)
    order = [(col ^ o) if flat else (col - o) % n_col for o in range(n_col)]
    own, mirror = own_product(
        sizes, table, jnp.stack(order).astype(jnp.int32), r_pieces, s_pieces, t_pieces, block
    )
    own, mirror = in_vmem(own), in_vmem(mirror)
    out = None
    for (first, _), parts in zip(chunks, coded):
        out = join(own, mirror, parts, first, out)
    return out


def plain_body(r_vals, s_vals, t_vals, r_pattern, s_pattern, t_pattern):
    row, col = lax.axis_index("row"), lax.axis_index("col")
    s_all = lax.all_gather(s_vals, "row", axis=0, tiled=True)
    r_all = lax.all_gather(r_vals, "col", axis=1, tiled=True)
    t_all = lax.all_to_all(t_vals, "col", split_axis=0, concat_axis=1, tiled=True)
    a_tiles, c_tiles = r_vals.shape[0] // BLK, s_vals.shape[1] // BLK

    def spread(flags):
        return jnp.repeat(jnp.repeat(flags.astype(jnp.bfloat16), BLK, axis=0), BLK, axis=1)

    r_flags = lax.dynamic_slice_in_dim(r_pattern, row * a_tiles, a_tiles, 0)
    s_flags = lax.dynamic_slice_in_dim(s_pattern, col * c_tiles, c_tiles, 1)
    t_flags = lax.dynamic_slice(t_pattern, (col * c_tiles, row * a_tiles), (c_tiles, a_tiles))
    paths = jnp.dot(
        r_all * spread(r_flags), s_all * spread(s_flags), preferred_element_type=jnp.float32
    )
    mirror = (t_all * spread(t_flags)).T
    return (paths * mirror.astype(jnp.float32)).astype(jnp.bfloat16)


def solution(mesh):
    placed = (P("row", "col"), P("row", "col"), P(None, ("row", "col")), P(), P(), P())
    n_row, n_col = mesh.shape["row"], mesh.shape["col"]
    fits = n_row == 2 * n_col and math.isqrt(n_col) ** 2 == n_col > 1
    return jax.shard_map(
        functools.partial(body, n_row, n_col) if fits else plain_body,
        mesh=mesh,
        in_specs=placed,
        out_specs=P("row", "col"),
        check_vma=False,
    )
```

```python
import functools
import math

import jax
import jax.numpy as jnp
from jax import lax
from jax.experimental import pallas as pl
from jax.experimental.pallas import tpu as pltpu
from jax.sharding import PartitionSpec as P

BLK = 128
STRIP = 16
LEVELS = 32767.0
FINE = 64.0
VMEM = 24 * 1024 * 1024


def masked(values, flag):
    return values * jnp.full((1, BLK), flag.astype(jnp.float32)).astype(jnp.bfloat16)


def joined_tiles(grid):
    bands = [jnp.concatenate(t, axis=1) if len(t) > 1 else t[0] for t in grid]
    return jnp.concatenate(bands, axis=0) if len(bands) > 1 else bands[0]


def whole(shape):
    return pl.BlockSpec(shape, lambda i, *_: (0,) * len(shape))


def cost(flops, bytes_accessed):
    return pl.CostEstimate(flops=flops, bytes_accessed=bytes_accessed, transcendentals=0)


def params(limit=VMEM):
    return pltpu.CompilerParams(vmem_limit_bytes=limit)


class Table:
    def __init__(self, ref, pieces, a_tiles, b_all, c_all):
        self.ref, self.pieces = ref, pieces
        self.b_all, self.c_all = b_all, c_all
        self.r_at = pieces * (pieces + 2)
        self.s_at = self.r_at + a_tiles * b_all

    def block(self, e):
        return self.ref[e]

    def spot(self, target, e):
        return self.ref[(target + 1) * self.pieces + e]

    def column(self, target):
        return self.ref[(self.pieces + 1) * self.pieces + target]

    def r_flag(self, a, b):
        return self.ref[self.r_at + a * self.b_all + b]

    def s_flag(self, b, c):
        return self.ref[self.s_at + b * self.c_all + c]

    def order(self, o, b_all):
        return self.ref[self.s_at + b_all * self.c_all + o]


def select_copy(choice, sources, target, sem):
    for d, source in enumerate(sources):

        @pl.when(choice == d)
        def _(source=source):
            pltpu.make_async_copy(source, target, sem).start()

    return pltpu.make_async_copy(sources[0], target, sem)


def products(table, target, first, r_refs, s_refs, r_buf, s_buf, r_sem, s_sem, use):
    pieces, blocks, block, width = r_buf.shape
    cols = s_buf.shape[1]
    b_tiles, c_tiles = width // BLK, cols // BLK

    def r_copy(e, n):
        rows = pl.ds(pl.multiple_of(first + n * block, block), block)
        return pltpu.make_async_copy(r_refs[e].at[rows], r_buf.at[e, n], r_sem.at[e, n])

    waits = [
        select_copy(table.spot(target, e), s_refs, s_buf.at[pl.ds(e * width, width)], s_sem.at[e])
        for e in range(pieces)
    ]
    for n in range(blocks):
        for e in range(pieces):
            r_copy(e, n).start()
    for e in range(pieces):
        waits[e].wait()
        for t in range(b_tiles):
            for u in range(c_tiles):
                flag = table.s_flag(table.block(e) * b_tiles + t, table.column(target) * c_tiles + u)
                down = slice(e * width + t * BLK, e * width + (t + 1) * BLK)
                over = slice(u * BLK, (u + 1) * BLK)
                s_buf[down, over] = masked(s_buf[down, over], flag)

    def one(n, carry):
        for e in range(pieces):
            r_copy(e, n).wait()
        grid = []
        for t in range(block // BLK):
            a = first // BLK + n * (block // BLK) + t
            grid.append(
                [
                    masked(
                        r_buf[e, n, t * BLK : (t + 1) * BLK, u * BLK : (u + 1) * BLK],
                        table.r_flag(a, table.block(e) * b_tiles + u),
                    )
                    for e in range(pieces)
                    for u in range(b_tiles)
                ]
            )
        use(n, jnp.dot(joined_tiles(grid), s_buf[...], preferred_element_type=jnp.float32))
        return carry

    lax.fori_loop(0, blocks, one, 0)


def encode(total, out):
    rows, cols = total.shape
    group = rows // STRIP
    strip_row = lax.broadcasted_iota(jnp.int32, (STRIP, cols), 0)
    strip = jnp.zeros((STRIP, cols), jnp.float32)
    for g in range(STRIP):
        part = total[g * group : (g + 1) * group]
        top = jnp.max(jnp.max(jnp.abs(part), axis=0, keepdims=True), axis=1, keepdims=True)
        level = jnp.ceil(jnp.log2(jnp.maximum(top, 1e-37)) * FINE) + 1.0
        root = jnp.exp2(level * (-0.5 / FINE))
        code = jnp.clip(jnp.round(part * root * (root * LEVELS)), -LEVELS, LEVELS)
        out[g * group : (g + 1) * group] = code.astype(jnp.int16)
        strip = jnp.where(strip_row == g, level, strip)
    out[rows:] = strip.astype(jnp.int16)


def coded_kernel(sizes, target, first, numbers, *refs):
    *ins, out, r_buf, s_buf, r_sem, s_sem = refs
    pieces = r_buf.shape[0]

    def use(n, total):
        encode(total, out.at[n])

    products(
        Table(numbers, *sizes), target, first, ins[:pieces], ins[pieces:],
        r_buf, s_buf, r_sem, s_sem, use,
    )


def own_kernel(sizes, count, numbers, *refs):
    *ins, out, mirror, r_buf, s_buf, r_sem, s_sem, t_sem = refs
    pieces = r_buf.shape[0]
    t_refs = ins[pieces + count :]
    blocks, block, _ = mirror.shape
    a_part = t_refs[0].shape[0]
    split = block // a_part
    table = Table(numbers, *sizes)
    waits = []
    for o in range(blocks * split):
        rows = pl.ds(o % split * a_part, a_part)
        waits.append(select_copy(table.order(o, sizes[2]), t_refs, mirror.at[o // split, rows], t_sem.at[o]))

    def use(n, total):
        out[n] = total

    products(
        table, 0, 0, ins[:pieces], ins[pieces : pieces + count],
        r_buf, s_buf, r_sem, s_sem, use,
    )
    for wait in waits:
        wait.wait()


SCALARS = pl.BlockSpec(memory_space=pltpu.SMEM)
ANYWHERE = pl.BlockSpec(memory_space=pl.ANY)
INSIDE = pl.BlockSpec(memory_space=pltpu.VMEM)


def product_scratch(pieces, blocks, block, width, cols):
    return [
        pltpu.VMEM((pieces, blocks, block, width), jnp.bfloat16),
        pltpu.VMEM((pieces * width, cols), jnp.bfloat16),
        pltpu.SemaphoreType.DMA((pieces, blocks)),
        pltpu.SemaphoreType.DMA((pieces,)),
    ]


def coded_product(sizes, table, r_pieces, s_pieces, target, block, first, blocks):
    pieces = len(r_pieces)
    width, cols = s_pieces[0].shape
    return pl.pallas_call(
        functools.partial(coded_kernel, sizes, target, first),
        out_shape=pltpu.VMEM((blocks, block + STRIP, cols), jnp.int16),
        in_specs=[SCALARS] + [ANYWHERE] * (pieces + len(s_pieces)),
        out_specs=INSIDE,
        scratch_shapes=product_scratch(pieces, blocks, block, width, cols),
        compiler_params=params(),
        cost_estimate=cost(2 * blocks * block * pieces * width * cols // 16, 0),
    )(table, *r_pieces, *s_pieces)


def own_product(sizes, table, r_pieces, s_pieces, t_pieces, block):
    pieces = len(r_pieces)
    width, cols = s_pieces[0].shape
    blocks = r_pieces[0].shape[0] // block
    return pl.pallas_call(
        functools.partial(own_kernel, sizes, len(s_pieces)),
        out_shape=[
            pltpu.VMEM((blocks, block, cols), jnp.float32),
            pltpu.VMEM((blocks, block, cols), jnp.bfloat16),
        ],
        in_specs=[SCALARS] + [ANYWHERE] * (pieces + len(s_pieces) + len(t_pieces)),
        out_specs=[INSIDE] * 2,
        scratch_shapes=product_scratch(pieces, blocks, block, width, cols)
        + [pltpu.SemaphoreType.DMA((len(t_pieces),))],
        compiler_params=params(),
        cost_estimate=cost(2 * blocks * block * pieces * width * cols // 16, 0),
    )(table, *r_pieces, *s_pieces, *t_pieces)


def join_kernel(parts, first, own, mirror, *refs):
    codes = refs[:parts]
    out, o_buf, roots, o_sem = refs[-4:]
    blocks, block, cols = o_buf.shape
    group = block // STRIP
    outs = []
    for n in range(blocks):
        for k in range(parts):
            level = codes[k][n, block:].astype(jnp.float32)
            roots[k] = jnp.exp2(level * (0.5 / FINE))
        for half in range(2):
            for g in range(half * STRIP // 2, (half + 1) * STRIP // 2):
                at = slice(g * group, (g + 1) * group)
                total = own[first + n, at]
                for k in range(parts):
                    root = roots[k, g : g + 1]
                    total += codes[k][n, at].astype(jnp.float32) * (root * (1.0 / LEVELS)) * root
                factor = mirror[first + n, at].astype(jnp.float32)
                o_buf[n, at] = (total * factor).astype(jnp.bfloat16)
            here = pl.ds(half * block // 2, block // 2)
            rows = pl.ds((first + n) * block + half * block // 2, block // 2)
            outs.append(
                pltpu.make_async_copy(o_buf.at[n, here], out.at[rows], o_sem.at[n, half])
            )
            outs[-1].start()
    for copy in outs:
        copy.wait()


def in_vmem(values):
    return pltpu.with_memory_space_constraint(values, pltpu.VMEM)


def join(own, mirror, coded, first, before):
    steps, block, cols = own.shape
    blocks = coded[0].shape[0]
    aliases, carried = {}, ()
    if before is not None:
        aliases, carried = {2 + len(coded): 0}, (before,)
    return pl.pallas_call(
        functools.partial(join_kernel, len(coded), first),
        out_shape=jax.ShapeDtypeStruct((steps * block, cols), jnp.bfloat16),
        in_specs=[INSIDE] * (2 + len(coded)) + [ANYWHERE] * len(carried),
        out_specs=ANYWHERE,
        scratch_shapes=[
            pltpu.VMEM((blocks, block, cols), jnp.bfloat16),
            pltpu.VMEM((len(coded), STRIP, cols), jnp.float32),
            pltpu.SemaphoreType.DMA((blocks, 2)),
        ],
        input_output_aliases=aliases,
        compiler_params=params(),
        cost_estimate=cost(0, 0),
    )(own, mirror, *[in_vmem(codes) for codes in coded], *carried)


def turn_kernel(pieces, width, places, flags, t_ref, *outs):
    a_width = t_ref.shape[1]
    for e in range(pieces):

        def one(t, carry, e=e):
            start = pl.multiple_of(places[e] * width + t * BLK, BLK)
            over = pl.ds(pl.multiple_of(t * BLK, BLK), BLK)
            for u in range(a_width // BLK):
                tile = masked(
                    t_ref[pl.ds(start, BLK), u * BLK : (u + 1) * BLK],
                    flags[places[e] * (width // BLK) + t, u],
                )
                outs[e][u * BLK : (u + 1) * BLK, over] = tile.T
            return carry

        lax.fori_loop(0, width // BLK, one, 0)


def turn(places, flags, t_vals, c_width):
    pieces = t_vals.shape[0] // c_width
    shape = (t_vals.shape[1], c_width)
    return pl.pallas_call(
        functools.partial(turn_kernel, pieces, c_width),
        out_shape=[jax.ShapeDtypeStruct(shape, jnp.bfloat16)] * pieces,
        grid_spec=pltpu.PrefetchScalarGridSpec(
            num_scalar_prefetch=2,
            grid=(1,),
            in_specs=[whole(t_vals.shape)],
            out_specs=[whole(shape)] * pieces,
        ),
        compiler_params=params(),
        cost_estimate=cost(0, 4 * t_vals.size),
    )(places, flags, t_vals)


def body(n_row, n_col, r_vals, s_vals, t_vals, r_pattern, s_pattern, t_pattern):
    side = math.isqrt(n_col)
    row = lax.axis_index("row")
    col = lax.axis_index("col")
    line, kind = row // 2, row % 2
    y, x = col // side, col % side
    a_rows, b_width = r_vals.shape
    c_width = s_vals.shape[1]
    a_part = t_vals.shape[1]
    a_tiles, ap_tiles = a_rows // BLK, a_part // BLK
    along = kind == 1
    gather_at = jnp.where(along, x, y)
    target_at = jnp.where(along, y, x)
    axes = ("row", "col")

    def place(k, h, yy, xx):
        return (k * 2 + h) * n_col + yy * side + xx

    def shifted(e, gather):
        pairs = []
        for k in range(n_row // 2):
            for h in range(2):
                for yy in range(side):
                    for xx in range(side):
                        if (h == 1) == gather:
                            to = (yy, (xx + e) % side)
                        else:
                            to = ((yy + e) % side, xx)
                        pairs.append((place(k, h, yy, xx), place(k, h, *to)))
        return pairs

    r_pieces = [r_vals] + [lax.ppermute(r_vals, axes, shifted(e, True)) for e in range(1, side)]

    flat = n_col & (n_col - 1) == 0
    partner = [(col ^ (-e % n_col)) if flat else (col + e) % n_col for e in range(n_col)]
    t_flags = lax.dynamic_slice_in_dim(t_pattern, (row * n_col + col) * ap_tiles, ap_tiles, 1)
    turned = turn(jnp.stack(partner).astype(jnp.int32), t_flags, t_vals, c_width)
    same, other = [], []
    for a in range(side):
        for b in range(side):
            for c in range(side):
                for d in range(side):
                    k = a * side + b
                    to_odd = (c * side + b, 1, a, d)
                    to_even = (a * side + d, 0, c, b)
                    same.append((place(k, 0, c, d), place(*to_even)))
                    same.append((place(k, 1, c, d), place(*to_odd)))
                    other.append((place(k, 1, c, d), place(*to_even)))
                    other.append((place(k, 0, c, d), place(*to_odd)))
    s_same = lax.ppermute(s_vals, axes, same)
    s_other = lax.ppermute(s_vals, axes, other)
    s_held = jnp.concatenate(
        [jnp.where(along, s_other, s_same), jnp.where(along, s_same, s_other)], axis=0
    )

    def to_partner(e, values):
        pairs = [(j, (j ^ (-e % n_col)) if flat else (j + e) % n_col) for j in range(n_col)]
        return lax.ppermute(values, "col", pairs)

    def along_line(values, hop):
        pairs = [(k * 2 + h, hop(k) * 2 + h) for k in range(n_col) for h in range(2)]
        return lax.ppermute(values, "row", pairs)

    if flat:
        got = {0: s_held}
        bit = n_col // 2
        while bit:
            got |= {m | bit: along_line(v, lambda k, bit=bit: k ^ bit) for m, v in got.items()}
            if len(got) == 2:
                got[bit], *turned = lax.optimization_barrier((got[bit], *turned))
            bit //= 2
        s_pieces = [got[m] for m in range(n_col)]
    else:
        s_pieces = [s_held] + [
            along_line(s_held, lambda k, d=d: (k + d) % n_col) for d in range(1, n_col)
        ]

    t_pieces = [turned[0]] + [to_partner(e, turned[e]) for e in range(1, n_col)]

    r_flags = lax.dynamic_slice_in_dim(r_pattern, row * a_tiles, a_tiles, 0)
    flags = [r_flags.reshape(-1), s_pattern.reshape(-1)]
    sizes = (side, a_tiles, r_pattern.shape[1], s_pattern.shape[1])

    blocks, spots, targets = [], [], []
    for e in range(side):
        g = (gather_at - e) % side
        blocks.append(jnp.where(along, y * side + g, g * side + x))
    for t in range(side):
        target = (target_at + t) % side
        for e in range(side):
            g = (gather_at - e) % side
            k = jnp.where(along, target * side + g, g * side + target)
            spots.append((line ^ k) if flat else (line - k) % n_col)
        targets.append(jnp.where(along, target * side + x, y * side + target))
    order = [-(col ^ o) % n_col if flat else (col - o) % n_col for o in range(n_col)]
    table = jnp.concatenate(
        [jnp.stack(blocks + spots + targets).astype(jnp.int32), *flags, jnp.stack(order).astype(jnp.int32)]
    )

    block = max(a_part, math.gcd(a_rows, 4 * BLK))
    steps = a_rows // block
    chunks = 2 if steps % 2 == 0 else 1
    steps //= chunks
    coded = []
    for chunk in range(chunks):
        parts = []
        for e in range(1, side):
            codes = coded_product(
                sizes, table, r_pieces, s_pieces, e, block, chunk * steps * block, steps
            )
            if chunk:
                codes, *t_pieces[1:] = lax.optimization_barrier((codes, *t_pieces[1:]))
            parts.append(lax.ppermute(codes, axes, shifted(e, False)))
        coded.append(parts)
    own, mirror = own_product(
        sizes, table, r_pieces, s_pieces, t_pieces, block
    )
    own, mirror = in_vmem(own), in_vmem(mirror)
    out = None
    for chunk in range(chunks):
        out = join(own, mirror, coded[chunk], chunk * steps, out)
    return out


def plain_body(r_vals, s_vals, t_vals, r_pattern, s_pattern, t_pattern):
    row, col = lax.axis_index("row"), lax.axis_index("col")
    s_all = lax.all_gather(s_vals, "row", axis=0, tiled=True)
    r_all = lax.all_gather(r_vals, "col", axis=1, tiled=True)
    t_all = lax.all_to_all(t_vals, "col", split_axis=0, concat_axis=1, tiled=True)
    a_tiles, c_tiles = r_vals.shape[0] // BLK, s_vals.shape[1] // BLK

    def spread(flags):
        return jnp.repeat(jnp.repeat(flags.astype(jnp.bfloat16), BLK, axis=0), BLK, axis=1)

    r_flags = lax.dynamic_slice_in_dim(r_pattern, row * a_tiles, a_tiles, 0)
    s_flags = lax.dynamic_slice_in_dim(s_pattern, col * c_tiles, c_tiles, 1)
    t_flags = lax.dynamic_slice(t_pattern, (col * c_tiles, row * a_tiles), (c_tiles, a_tiles))
    paths = jnp.dot(
        r_all * spread(r_flags), s_all * spread(s_flags), preferred_element_type=jnp.float32
    )
    mirror = (t_all * spread(t_flags)).T
    return (paths * mirror.astype(jnp.float32)).astype(jnp.bfloat16)


def solution(mesh):
    placed = (P("row", "col"), P("row", "col"), P(None, ("row", "col")), P(), P(), P())
    n_row, n_col = mesh.shape["row"], mesh.shape["col"]
    fits = n_row == 2 * n_col and math.isqrt(n_col) ** 2 == n_col > 1
    return jax.shard_map(
        functools.partial(body, n_row, n_col) if fits else plain_body,
        mesh=mesh,
        in_specs=placed,
        out_specs=P("row", "col"),
        check_vma=False,
    )
```

```python
import functools
import math

import jax
import jax.numpy as jnp
from jax import lax
from jax.experimental import pallas as pl
from jax.experimental.pallas import tpu as pltpu
from jax.sharding import PartitionSpec as P

BLK = 128
STRIP = 16
LEVELS = 32767.0
FINE = 64.0
VMEM = 24 * 1024 * 1024


def masked(values, flag):
    return values * jnp.full((1, BLK), flag.astype(jnp.float32)).astype(jnp.bfloat16)


def joined_tiles(grid):
    bands = [jnp.concatenate(t, axis=1) if len(t) > 1 else t[0] for t in grid]
    return jnp.concatenate(bands, axis=0) if len(bands) > 1 else bands[0]


def whole(shape):
    return pl.BlockSpec(shape, lambda i, *_: (0,) * len(shape))


def cost(flops, bytes_accessed):
    return pl.CostEstimate(flops=flops, bytes_accessed=bytes_accessed, transcendentals=0)


def params(limit=VMEM):
    return pltpu.CompilerParams(vmem_limit_bytes=limit)


class Table:
    def __init__(self, ref, pieces, a_tiles, b_all, c_all):
        self.ref, self.pieces = ref, pieces
        self.b_all, self.c_all = b_all, c_all
        self.r_at = pieces * (pieces + 2)
        self.s_at = self.r_at + a_tiles * b_all

    def block(self, e):
        return self.ref[e]

    def spot(self, target, e):
        return self.ref[(target + 1) * self.pieces + e]

    def column(self, target):
        return self.ref[(self.pieces + 1) * self.pieces + target]

    def r_flag(self, a, b):
        return self.ref[self.r_at + a * self.b_all + b]

    def s_flag(self, b, c):
        return self.ref[self.s_at + b * self.c_all + c]


def select_copy(choice, sources, target, sem):
    for d, source in enumerate(sources):

        @pl.when(choice == d)
        def _(source=source):
            pltpu.make_async_copy(source, target, sem).start()

    return pltpu.make_async_copy(sources[0], target, sem)


def products(table, target, first, r_refs, s_refs, r_buf, s_buf, r_sem, s_sem, use):
    pieces, blocks, block, width = r_buf.shape
    cols = s_buf.shape[1]
    b_tiles, c_tiles = width // BLK, cols // BLK

    def r_copy(e, n):
        rows = pl.ds(pl.multiple_of(first + n * block, block), block)
        return pltpu.make_async_copy(r_refs[e].at[rows], r_buf.at[e, n], r_sem.at[e, n])

    waits = [
        select_copy(table.spot(target, e), s_refs, s_buf.at[pl.ds(e * width, width)], s_sem.at[e])
        for e in range(pieces)
    ]
    for n in range(blocks):
        for e in range(pieces):
            r_copy(e, n).start()
    for e in range(pieces):
        waits[e].wait()
        for t in range(b_tiles):
            for u in range(c_tiles):
                flag = table.s_flag(table.block(e) * b_tiles + t, table.column(target) * c_tiles + u)
                down = slice(e * width + t * BLK, e * width + (t + 1) * BLK)
                over = slice(u * BLK, (u + 1) * BLK)
                s_buf[down, over] = masked(s_buf[down, over], flag)

    def one(n, carry):
        for e in range(pieces):
            r_copy(e, n).wait()
        grid = []
        for t in range(block // BLK):
            a = first // BLK + n * (block // BLK) + t
            grid.append(
                [
                    masked(
                        r_buf[e, n, t * BLK : (t + 1) * BLK, u * BLK : (u + 1) * BLK],
                        table.r_flag(a, table.block(e) * b_tiles + u),
                    )
                    for e in range(pieces)
                    for u in range(b_tiles)
                ]
            )
        use(n, jnp.dot(joined_tiles(grid), s_buf[...], preferred_element_type=jnp.float32))
        return carry

    lax.fori_loop(0, blocks, one, 0)


def encode(total, out):
    rows, cols = total.shape
    group = rows // STRIP
    strip_row = lax.broadcasted_iota(jnp.int32, (STRIP, cols), 0)
    strip = jnp.zeros((STRIP, cols), jnp.float32)
    for g in range(STRIP):
        part = total[g * group : (g + 1) * group]
        top = jnp.max(jnp.max(jnp.abs(part), axis=0, keepdims=True), axis=1, keepdims=True)
        level = jnp.ceil(jnp.log2(jnp.maximum(top, 1e-37)) * FINE) + 1.0
        root = jnp.exp2(level * (-0.5 / FINE))
        code = jnp.clip(jnp.round(part * root * (root * LEVELS)), -LEVELS, LEVELS)
        out[g * group : (g + 1) * group] = code.astype(jnp.int16)
        strip = jnp.where(strip_row == g, level, strip)
    out[rows:] = strip.astype(jnp.int16)


def coded_kernel(sizes, target, first, numbers, *refs):
    *ins, out, r_buf, s_buf, r_sem, s_sem = refs
    pieces = r_buf.shape[0]

    def use(n, total):
        encode(total, out.at[n])

    products(
        Table(numbers, *sizes), target, first, ins[:pieces], ins[pieces:],
        r_buf, s_buf, r_sem, s_sem, use,
    )


def own_kernel(sizes, count, numbers, order, *refs):
    *ins, out, mirror, r_buf, s_buf, r_sem, s_sem, t_sem = refs
    pieces = r_buf.shape[0]
    t_refs = ins[pieces + count :]
    blocks, block, _ = mirror.shape
    a_part = t_refs[0].shape[0]
    split = block // a_part
    waits = []
    for o in range(blocks * split):
        rows = pl.ds(o % split * a_part, a_part)
        waits.append(select_copy(order[o], t_refs, mirror.at[o // split, rows], t_sem.at[o]))

    def use(n, total):
        out[n] = total

    products(
        Table(numbers, *sizes), 0, 0, ins[:pieces], ins[pieces : pieces + count],
        r_buf, s_buf, r_sem, s_sem, use,
    )
    for wait in waits:
        wait.wait()


SCALARS = pl.BlockSpec(memory_space=pltpu.SMEM)
ANYWHERE = pl.BlockSpec(memory_space=pl.ANY)
INSIDE = pl.BlockSpec(memory_space=pltpu.VMEM)


def product_scratch(pieces, blocks, block, width, cols):
    return [
        pltpu.VMEM((pieces, blocks, block, width), jnp.bfloat16),
        pltpu.VMEM((pieces * width, cols), jnp.bfloat16),
        pltpu.SemaphoreType.DMA((pieces, blocks)),
        pltpu.SemaphoreType.DMA((pieces,)),
    ]


def coded_product(sizes, table, r_pieces, s_pieces, target, block, first, blocks):
    pieces = len(r_pieces)
    width, cols = s_pieces[0].shape
    return pl.pallas_call(
        functools.partial(coded_kernel, sizes, target, first),
        out_shape=pltpu.VMEM((blocks, block + STRIP, cols), jnp.int16),
        in_specs=[SCALARS] + [ANYWHERE] * (pieces + len(s_pieces)),
        out_specs=INSIDE,
        scratch_shapes=product_scratch(pieces, blocks, block, width, cols),
        compiler_params=params(),
        cost_estimate=cost(2 * blocks * block * pieces * width * cols // 16, 0),
    )(table, *r_pieces, *s_pieces)


def own_product(sizes, table, order, r_pieces, s_pieces, t_pieces, block):
    pieces = len(r_pieces)
    width, cols = s_pieces[0].shape
    blocks = r_pieces[0].shape[0] // block
    return pl.pallas_call(
        functools.partial(own_kernel, sizes, len(s_pieces)),
        out_shape=[
            pltpu.VMEM((blocks, block, cols), jnp.float32),
            pltpu.VMEM((blocks, block, cols), jnp.bfloat16),
        ],
        in_specs=[SCALARS] * 2 + [ANYWHERE] * (pieces + len(s_pieces) + len(t_pieces)),
        out_specs=[INSIDE] * 2,
        scratch_shapes=product_scratch(pieces, blocks, block, width, cols)
        + [pltpu.SemaphoreType.DMA((len(t_pieces),))],
        compiler_params=params(),
        cost_estimate=cost(2 * blocks * block * pieces * width * cols // 16, 0),
    )(table, order, *r_pieces, *s_pieces, *t_pieces)


def join_kernel(parts, first, own, mirror, *refs):
    codes = refs[:parts]
    out, o_buf, roots, o_sem = refs[-4:]
    blocks, block, cols = o_buf.shape
    group = block // STRIP
    outs = []
    for n in range(blocks):
        for k in range(parts):
            level = codes[k][n, block:].astype(jnp.float32)
            roots[k] = jnp.exp2(level * (0.5 / FINE))
        for half in range(2):
            for g in range(half * STRIP // 2, (half + 1) * STRIP // 2):
                at = slice(g * group, (g + 1) * group)
                total = own[first + n, at]
                for k in range(parts):
                    root = roots[k, g : g + 1]
                    total += codes[k][n, at].astype(jnp.float32) * (root * (1.0 / LEVELS)) * root
                factor = mirror[first + n, at].astype(jnp.float32)
                o_buf[n, at] = (total * factor).astype(jnp.bfloat16)
            here = pl.ds(half * block // 2, block // 2)
            rows = pl.ds((first + n) * block + half * block // 2, block // 2)
            outs.append(
                pltpu.make_async_copy(o_buf.at[n, here], out.at[rows], o_sem.at[n, half])
            )
            outs[-1].start()
    for copy in outs:
        copy.wait()


def in_vmem(values):
    return pltpu.with_memory_space_constraint(values, pltpu.VMEM)


def join(own, mirror, coded, first, before):
    steps, block, cols = own.shape
    blocks = coded[0].shape[0]
    aliases, carried = {}, ()
    if before is not None:
        aliases, carried = {2 + len(coded): 0}, (before,)
    return pl.pallas_call(
        functools.partial(join_kernel, len(coded), first),
        out_shape=jax.ShapeDtypeStruct((steps * block, cols), jnp.bfloat16),
        in_specs=[INSIDE] * (2 + len(coded)) + [ANYWHERE] * len(carried),
        out_specs=ANYWHERE,
        scratch_shapes=[
            pltpu.VMEM((blocks, block, cols), jnp.bfloat16),
            pltpu.VMEM((len(coded), STRIP, cols), jnp.float32),
            pltpu.SemaphoreType.DMA((blocks, 2)),
        ],
        input_output_aliases=aliases,
        compiler_params=params(),
        cost_estimate=cost(0, 0),
    )(own, mirror, *[in_vmem(codes) for codes in coded], *carried)


def turn_kernel(pieces, width, places, flags, t_ref, *outs):
    a_width = t_ref.shape[1]
    for e in range(pieces):

        def one(t, carry, e=e):
            start = pl.multiple_of(places[e] * width + t * BLK, BLK)
            over = pl.ds(pl.multiple_of(t * BLK, BLK), BLK)
            for u in range(a_width // BLK):
                tile = masked(
                    t_ref[pl.ds(start, BLK), u * BLK : (u + 1) * BLK],
                    flags[places[e] * (width // BLK) + t, u],
                )
                outs[e][u * BLK : (u + 1) * BLK, over] = tile.T
            return carry

        lax.fori_loop(0, width // BLK, one, 0)


def turn(places, flags, t_vals, c_width):
    pieces = t_vals.shape[0] // c_width
    shape = (t_vals.shape[1], c_width)
    return pl.pallas_call(
        functools.partial(turn_kernel, pieces, c_width),
        out_shape=[jax.ShapeDtypeStruct(shape, jnp.bfloat16)] * pieces,
        grid_spec=pltpu.PrefetchScalarGridSpec(
            num_scalar_prefetch=2,
            grid=(1,),
            in_specs=[whole(t_vals.shape)],
            out_specs=[whole(shape)] * pieces,
        ),
        compiler_params=params(),
        cost_estimate=cost(0, 4 * t_vals.size),
    )(places, flags, t_vals)


def body(n_row, n_col, r_vals, s_vals, t_vals, r_pattern, s_pattern, t_pattern):
    side = math.isqrt(n_col)
    row = lax.axis_index("row")
    col = lax.axis_index("col")
    line, kind = row // 2, row % 2
    y, x = col // side, col % side
    a_rows, b_width = r_vals.shape
    c_width = s_vals.shape[1]
    a_part = t_vals.shape[1]
    a_tiles, ap_tiles = a_rows // BLK, a_part // BLK
    along = kind == 1
    gather_at = jnp.where(along, x, y)
    target_at = jnp.where(along, y, x)
    axes = ("row", "col")

    def place(k, h, yy, xx):
        return (k * 2 + h) * n_col + yy * side + xx

    def shifted(e, gather):
        pairs = []
        for k in range(n_row // 2):
            for h in range(2):
                for yy in range(side):
                    for xx in range(side):
                        if (h == 1) == gather:
                            to = (yy, (xx + e) % side)
                        else:
                            to = ((yy + e) % side, xx)
                        pairs.append((place(k, h, yy, xx), place(k, h, *to)))
        return pairs

    r_pieces = [r_vals] + [lax.ppermute(r_vals, axes, shifted(e, True)) for e in range(1, side)]

    flat = n_col & (n_col - 1) == 0
    partner = [(col ^ e) if flat else (col + e) % n_col for e in range(n_col)]
    t_flags = lax.dynamic_slice_in_dim(t_pattern, (row * n_col + col) * ap_tiles, ap_tiles, 1)
    turned = turn(jnp.stack(partner).astype(jnp.int32), t_flags, t_vals, c_width)
    same, other = [], []
    for a in range(side):
        for b in range(side):
            for c in range(side):
                for d in range(side):
                    k = a * side + b
                    to_odd = (c * side + b, 1, a, d)
                    to_even = (a * side + d, 0, c, b)
                    same.append((place(k, 0, c, d), place(*to_even)))
                    same.append((place(k, 1, c, d), place(*to_odd)))
                    other.append((place(k, 1, c, d), place(*to_even)))
                    other.append((place(k, 0, c, d), place(*to_odd)))
    s_same = lax.ppermute(s_vals, axes, same)
    s_other = lax.ppermute(s_vals, axes, other)
    s_held = jnp.concatenate(
        [jnp.where(along, s_other, s_same), jnp.where(along, s_same, s_other)], axis=0
    )

    def along_line(values, hop):
        pairs = [(k * 2 + h, hop(k) * 2 + h) for k in range(n_col) for h in range(2)]
        return lax.ppermute(values, "row", pairs)

    if flat:
        got = {0: s_held}
        bit = n_col // 2
        while bit:
            got |= {m | bit: along_line(v, lambda k, bit=bit: k ^ bit) for m, v in got.items()}
            if len(got) == 2:
                got[bit], *turned = lax.optimization_barrier((got[bit], *turned))
            bit //= 2
        s_pieces = [got[m] for m in range(n_col)]
    else:
        s_pieces = [s_held] + [
            along_line(s_held, lambda k, d=d: (k + d) % n_col) for d in range(1, n_col)
        ]

    *r_pieces[1:], turned[-1] = lax.optimization_barrier((*r_pieces[1:], turned[-1]))
    t_pieces = [turned[0]]
    for e in range(1, n_col):
        pairs = [(j, (j ^ e) if flat else (j + e) % n_col) for j in range(n_col)]
        t_pieces.append(lax.ppermute(turned[e], "col", pairs))

    r_flags = lax.dynamic_slice_in_dim(r_pattern, row * a_tiles, a_tiles, 0)
    flags = [r_flags.reshape(-1), s_pattern.reshape(-1)]
    sizes = (side, a_tiles, r_pattern.shape[1], s_pattern.shape[1])

    blocks, spots, targets = [], [], []
    for e in range(side):
        g = (gather_at - e) % side
        blocks.append(jnp.where(along, y * side + g, g * side + x))
    for t in range(side):
        target = (target_at + t) % side
        for e in range(side):
            g = (gather_at - e) % side
            k = jnp.where(along, target * side + g, g * side + target)
            spots.append((line ^ k) if flat else (line - k) % n_col)
        targets.append(jnp.where(along, target * side + x, y * side + target))
    table = jnp.concatenate([jnp.stack(blocks + spots + targets).astype(jnp.int32), *flags])

    block = max(a_part, math.gcd(a_rows, 4 * BLK))
    steps = a_rows // block
    chunks = 2 if steps % 2 == 0 else 1
    steps //= chunks
    coded = []
    for chunk in range(chunks):
        parts = []
        for e in range(1, side):
            codes = coded_product(
                sizes, table, r_pieces, s_pieces, e, block, chunk * steps * block, steps
            )
            if chunk:
                codes, *t_pieces[1:] = lax.optimization_barrier((codes, *t_pieces[1:]))
            parts.append(lax.ppermute(codes, axes, shifted(e, False)))
        coded.append(parts)
    order = [(col ^ o) if flat else (col - o) % n_col for o in range(n_col)]
    own, mirror = own_product(
        sizes, table, jnp.stack(order).astype(jnp.int32), r_pieces, s_pieces, t_pieces, block
    )
    own, mirror = in_vmem(own), in_vmem(mirror)
    out = None
    for chunk in range(chunks):
        out = join(own, mirror, coded[chunk], chunk * steps, out)
    return out


def plain_body(r_vals, s_vals, t_vals, r_pattern, s_pattern, t_pattern):
    row, col = lax.axis_index("row"), lax.axis_index("col")
    s_all = lax.all_gather(s_vals, "row", axis=0, tiled=True)
    r_all = lax.all_gather(r_vals, "col", axis=1, tiled=True)
    t_all = lax.all_to_all(t_vals, "col", split_axis=0, concat_axis=1, tiled=True)
    a_tiles, c_tiles = r_vals.shape[0] // BLK, s_vals.shape[1] // BLK

    def spread(flags):
        return jnp.repeat(jnp.repeat(flags.astype(jnp.bfloat16), BLK, axis=0), BLK, axis=1)

    r_flags = lax.dynamic_slice_in_dim(r_pattern, row * a_tiles, a_tiles, 0)
    s_flags = lax.dynamic_slice_in_dim(s_pattern, col * c_tiles, c_tiles, 1)
    t_flags = lax.dynamic_slice(t_pattern, (col * c_tiles, row * a_tiles), (c_tiles, a_tiles))
    paths = jnp.dot(
        r_all * spread(r_flags), s_all * spread(s_flags), preferred_element_type=jnp.float32
    )
    mirror = (t_all * spread(t_flags)).T
    return (paths * mirror.astype(jnp.float32)).astype(jnp.bfloat16)


def solution(mesh):
    placed = (P("row", "col"), P("row", "col"), P(None, ("row", "col")), P(), P(), P())
    n_row, n_col = mesh.shape["row"], mesh.shape["col"]
    fits = n_row == 2 * n_col and math.isqrt(n_col) ** 2 == n_col > 1
    return jax.shard_map(
        functools.partial(body, n_row, n_col) if fits else plain_body,
        mesh=mesh,
        in_specs=placed,
        out_specs=P("row", "col"),
        check_vma=False,
    )
```

```python
import functools
import math

import jax
import jax.numpy as jnp
from jax import lax
from jax.experimental import pallas as pl
from jax.experimental.pallas import tpu as pltpu
from jax.sharding import PartitionSpec as P

BLK = 128
STRIP = 16
LEVELS = 32767.0
FINE = 64.0
VMEM = 24 * 1024 * 1024


def masked(values, flag):
    return values * jnp.full((1, BLK), flag.astype(jnp.float32)).astype(jnp.bfloat16)


def joined_tiles(grid):
    bands = [jnp.concatenate(t, axis=1) if len(t) > 1 else t[0] for t in grid]
    return jnp.concatenate(bands, axis=0) if len(bands) > 1 else bands[0]


def whole(shape):
    return pl.BlockSpec(shape, lambda i, *_: (0,) * len(shape))


def cost(flops, bytes_accessed):
    return pl.CostEstimate(flops=flops, bytes_accessed=bytes_accessed, transcendentals=0)


def params(limit=VMEM):
    return pltpu.CompilerParams(vmem_limit_bytes=limit)


class Table:
    def __init__(self, ref, pieces, a_tiles, b_all, c_all):
        self.ref, self.pieces = ref, pieces
        self.b_all, self.c_all = b_all, c_all
        self.r_at = pieces * (pieces + 2)
        self.s_at = self.r_at + a_tiles * b_all

    def block(self, e):
        return self.ref[e]

    def spot(self, target, e):
        return self.ref[(target + 1) * self.pieces + e]

    def column(self, target):
        return self.ref[(self.pieces + 1) * self.pieces + target]

    def r_flag(self, a, b):
        return self.ref[self.r_at + a * self.b_all + b]

    def s_flag(self, b, c):
        return self.ref[self.s_at + b * self.c_all + c]


def select_copy(choice, sources, target, sem):
    for d, source in enumerate(sources):

        @pl.when(choice == d)
        def _(source=source):
            pltpu.make_async_copy(source, target, sem).start()

    return pltpu.make_async_copy(sources[0], target, sem)


def products(table, target, first, r_refs, s_refs, r_buf, s_buf, r_sem, s_sem, use):
    pieces, blocks, block, width = r_buf.shape
    cols = s_buf.shape[1]
    b_tiles, c_tiles = width // BLK, cols // BLK

    def r_copy(e, n):
        rows = pl.ds(pl.multiple_of(first + n * block, block), block)
        return pltpu.make_async_copy(r_refs[e].at[rows], r_buf.at[e, n], r_sem.at[e, n])

    waits = [
        select_copy(table.spot(target, e), s_refs, s_buf.at[pl.ds(e * width, width)], s_sem.at[e])
        for e in range(pieces)
    ]
    for n in range(blocks):
        for e in range(pieces):
            r_copy(e, n).start()
    for e in range(pieces):
        waits[e].wait()
        for t in range(b_tiles):
            for u in range(c_tiles):
                flag = table.s_flag(table.block(e) * b_tiles + t, table.column(target) * c_tiles + u)
                down = slice(e * width + t * BLK, e * width + (t + 1) * BLK)
                over = slice(u * BLK, (u + 1) * BLK)
                s_buf[down, over] = masked(s_buf[down, over], flag)

    def one(n, carry):
        for e in range(pieces):
            r_copy(e, n).wait()
        grid = []
        for t in range(block // BLK):
            a = first // BLK + n * (block // BLK) + t
            grid.append(
                [
                    masked(
                        r_buf[e, n, t * BLK : (t + 1) * BLK, u * BLK : (u + 1) * BLK],
                        table.r_flag(a, table.block(e) * b_tiles + u),
                    )
                    for e in range(pieces)
                    for u in range(b_tiles)
                ]
            )
        use(n, jnp.dot(joined_tiles(grid), s_buf[...], preferred_element_type=jnp.float32))
        return carry

    lax.fori_loop(0, blocks, one, 0)


def encode(total, out):
    rows, cols = total.shape
    group = rows // STRIP
    strip_row = lax.broadcasted_iota(jnp.int32, (STRIP, cols), 0)
    strip = jnp.zeros((STRIP, cols), jnp.float32)
    for g in range(STRIP):
        part = total[g * group : (g + 1) * group]
        top = jnp.max(jnp.max(jnp.abs(part), axis=0, keepdims=True), axis=1, keepdims=True)
        level = jnp.ceil(jnp.log2(jnp.maximum(top, 1e-37)) * FINE) + 1.0
        root = jnp.exp2(level * (-0.5 / FINE))
        code = jnp.clip(jnp.round(part * root * (root * LEVELS)), -LEVELS, LEVELS)
        out[g * group : (g + 1) * group] = code.astype(jnp.int16)
        strip = jnp.where(strip_row == g, level, strip)
    out[rows:] = strip.astype(jnp.int16)


def coded_kernel(sizes, target, first, numbers, *refs):
    *ins, out, r_buf, s_buf, r_sem, s_sem = refs
    pieces = r_buf.shape[0]

    def use(n, total):
        encode(total, out.at[n])

    products(
        Table(numbers, *sizes), target, first, ins[:pieces], ins[pieces:],
        r_buf, s_buf, r_sem, s_sem, use,
    )


def own_kernel(sizes, count, numbers, order, *refs):
    *ins, out, mirror, r_buf, s_buf, r_sem, s_sem, t_sem = refs
    pieces = r_buf.shape[0]
    t_refs = ins[pieces + count :]
    blocks, block, _ = mirror.shape
    a_part = t_refs[0].shape[0]
    split = block // a_part
    waits = []
    for o in range(blocks * split):
        rows = pl.ds(o % split * a_part, a_part)
        waits.append(select_copy(order[o], t_refs, mirror.at[o // split, rows], t_sem.at[o]))

    def use(n, total):
        out[n] = total

    products(
        Table(numbers, *sizes), 0, 0, ins[:pieces], ins[pieces : pieces + count],
        r_buf, s_buf, r_sem, s_sem, use,
    )
    for wait in waits:
        wait.wait()


SCALARS = pl.BlockSpec(memory_space=pltpu.SMEM)
ANYWHERE = pl.BlockSpec(memory_space=pl.ANY)
INSIDE = pl.BlockSpec(memory_space=pltpu.VMEM)


def product_scratch(pieces, blocks, block, width, cols):
    return [
        pltpu.VMEM((pieces, blocks, block, width), jnp.bfloat16),
        pltpu.VMEM((pieces * width, cols), jnp.bfloat16),
        pltpu.SemaphoreType.DMA((pieces, blocks)),
        pltpu.SemaphoreType.DMA((pieces,)),
    ]


def coded_product(sizes, table, r_pieces, s_pieces, target, block, first, blocks):
    pieces = len(r_pieces)
    width, cols = s_pieces[0].shape
    return pl.pallas_call(
        functools.partial(coded_kernel, sizes, target, first),
        out_shape=pltpu.VMEM((blocks, block + STRIP, cols), jnp.int16),
        in_specs=[SCALARS] + [ANYWHERE] * (pieces + len(s_pieces)),
        out_specs=INSIDE,
        scratch_shapes=product_scratch(pieces, blocks, block, width, cols),
        compiler_params=params(),
        cost_estimate=cost(2 * blocks * block * pieces * width * cols // 16, 0),
    )(table, *r_pieces, *s_pieces)


def own_product(sizes, table, order, r_pieces, s_pieces, t_pieces, block):
    pieces = len(r_pieces)
    width, cols = s_pieces[0].shape
    blocks = r_pieces[0].shape[0] // block
    return pl.pallas_call(
        functools.partial(own_kernel, sizes, len(s_pieces)),
        out_shape=[
            pltpu.VMEM((blocks, block, cols), jnp.float32),
            pltpu.VMEM((blocks, block, cols), jnp.bfloat16),
        ],
        in_specs=[SCALARS] * 2 + [ANYWHERE] * (pieces + len(s_pieces) + len(t_pieces)),
        out_specs=[INSIDE] * 2,
        scratch_shapes=product_scratch(pieces, blocks, block, width, cols)
        + [pltpu.SemaphoreType.DMA((len(t_pieces),))],
        compiler_params=params(),
        cost_estimate=cost(2 * blocks * block * pieces * width * cols // 16, 0),
    )(table, order, *r_pieces, *s_pieces, *t_pieces)


def join_kernel(parts, first, own, mirror, *refs):
    codes = refs[:parts]
    out, o_buf, roots, o_sem = refs[-4:]
    blocks, block, cols = o_buf.shape
    group = block // STRIP
    outs = []
    for n in range(blocks):
        for k in range(parts):
            level = codes[k][n, block:].astype(jnp.float32)
            roots[k] = jnp.exp2(level * (0.5 / FINE))
        for half in range(2):
            for g in range(half * STRIP // 2, (half + 1) * STRIP // 2):
                at = slice(g * group, (g + 1) * group)
                total = own[first + n, at]
                for k in range(parts):
                    root = roots[k, g : g + 1]
                    total += codes[k][n, at].astype(jnp.float32) * (root * (1.0 / LEVELS)) * root
                factor = mirror[first + n, at].astype(jnp.float32)
                o_buf[n, at] = (total * factor).astype(jnp.bfloat16)
            here = pl.ds(half * block // 2, block // 2)
            rows = pl.ds((first + n) * block + half * block // 2, block // 2)
            outs.append(
                pltpu.make_async_copy(o_buf.at[n, here], out.at[rows], o_sem.at[n, half])
            )
            outs[-1].start()
    for copy in outs:
        copy.wait()


def in_vmem(values):
    return pltpu.with_memory_space_constraint(values, pltpu.VMEM)


def join(own, mirror, coded, first, before):
    steps, block, cols = own.shape
    blocks = coded[0].shape[0]
    aliases, carried = {}, ()
    if before is not None:
        aliases, carried = {2 + len(coded): 0}, (before,)
    return pl.pallas_call(
        functools.partial(join_kernel, len(coded), first),
        out_shape=jax.ShapeDtypeStruct((steps * block, cols), jnp.bfloat16),
        in_specs=[INSIDE] * (2 + len(coded)) + [ANYWHERE] * len(carried),
        out_specs=ANYWHERE,
        scratch_shapes=[
            pltpu.VMEM((blocks, block, cols), jnp.bfloat16),
            pltpu.VMEM((len(coded), STRIP, cols), jnp.float32),
            pltpu.SemaphoreType.DMA((blocks, 2)),
        ],
        input_output_aliases=aliases,
        compiler_params=params(),
        cost_estimate=cost(0, 0),
    )(own, mirror, *[in_vmem(codes) for codes in coded], *carried)


def turn_kernel(pieces, width, places, flags, t_ref, *outs):
    a_width = t_ref.shape[1]
    for e in range(pieces):

        def one(t, carry, e=e):
            start = pl.multiple_of(places[e] * width + t * BLK, BLK)
            over = pl.ds(pl.multiple_of(t * BLK, BLK), BLK)
            for u in range(a_width // BLK):
                tile = masked(
                    t_ref[pl.ds(start, BLK), u * BLK : (u + 1) * BLK],
                    flags[places[e] * (width // BLK) + t, u],
                )
                outs[e][u * BLK : (u + 1) * BLK, over] = tile.T
            return carry

        lax.fori_loop(0, width // BLK, one, 0)


def turn(places, flags, t_vals, c_width):
    pieces = t_vals.shape[0] // c_width
    shape = (t_vals.shape[1], c_width)
    return pl.pallas_call(
        functools.partial(turn_kernel, pieces, c_width),
        out_shape=[jax.ShapeDtypeStruct(shape, jnp.bfloat16)] * pieces,
        grid_spec=pltpu.PrefetchScalarGridSpec(
            num_scalar_prefetch=2,
            grid=(1,),
            in_specs=[whole(t_vals.shape)],
            out_specs=[whole(shape)] * pieces,
        ),
        compiler_params=params(),
        cost_estimate=cost(0, 4 * t_vals.size),
    )(places, flags, t_vals)


def body(n_row, n_col, r_vals, s_vals, t_vals, r_pattern, s_pattern, t_pattern):
    side = math.isqrt(n_col)
    row = lax.axis_index("row")
    col = lax.axis_index("col")
    line, kind = row // 2, row % 2
    y, x = col // side, col % side
    a_rows, b_width = r_vals.shape
    c_width = s_vals.shape[1]
    a_part = t_vals.shape[1]
    a_tiles, ap_tiles = a_rows // BLK, a_part // BLK
    along = kind == 1
    gather_at = jnp.where(along, x, y)
    target_at = jnp.where(along, y, x)
    axes = ("row", "col")

    def place(k, h, yy, xx):
        return (k * 2 + h) * n_col + yy * side + xx

    def shifted(e, gather):
        pairs = []
        for k in range(n_row // 2):
            for h in range(2):
                for yy in range(side):
                    for xx in range(side):
                        if (h == 1) == gather:
                            to = (yy, (xx + e) % side)
                        else:
                            to = ((yy + e) % side, xx)
                        pairs.append((place(k, h, yy, xx), place(k, h, *to)))
        return pairs

    r_pieces = [r_vals] + [lax.ppermute(r_vals, axes, shifted(e, True)) for e in range(1, side)]

    flat = n_col & (n_col - 1) == 0
    partner = [(col ^ e) if flat else (col + e) % n_col for e in range(n_col)]
    t_flags = lax.dynamic_slice_in_dim(t_pattern, (row * n_col + col) * ap_tiles, ap_tiles, 1)
    turned = turn(jnp.stack(partner).astype(jnp.int32), t_flags, t_vals, c_width)
    same, other = [], []
    for a in range(side):
        for b in range(side):
            for c in range(side):
                for d in range(side):
                    k = a * side + b
                    to_odd = (c * side + b, 1, a, d)
                    to_even = (a * side + d, 0, c, b)
                    same.append((place(k, 0, c, d), place(*to_even)))
                    same.append((place(k, 1, c, d), place(*to_odd)))
                    other.append((place(k, 1, c, d), place(*to_even)))
                    other.append((place(k, 0, c, d), place(*to_odd)))
    s_same = lax.ppermute(s_vals, axes, same)
    s_other = lax.ppermute(s_vals, axes, other)
    s_held = jnp.concatenate(
        [jnp.where(along, s_other, s_same), jnp.where(along, s_same, s_other)], axis=0
    )

    def along_line(values, hop):
        pairs = [(k * 2 + h, hop(k) * 2 + h) for k in range(n_col) for h in range(2)]
        return lax.ppermute(values, "row", pairs)

    if flat:
        got = {0: s_held}
        bit = n_col // 2
        while bit:
            got |= {m | bit: along_line(v, lambda k, bit=bit: k ^ bit) for m, v in got.items()}
            if len(got) == 2:
                got[bit], *turned = lax.optimization_barrier((got[bit], *turned))
            bit //= 2
        s_pieces = [got[m] for m in range(n_col)]
    else:
        s_pieces = [s_held] + [
            along_line(s_held, lambda k, d=d: (k + d) % n_col) for d in range(1, n_col)
        ]

    t_pieces = [turned[0]]
    for e in range(1, n_col):
        pairs = [(j, (j ^ e) if flat else (j + e) % n_col) for j in range(n_col)]
        t_pieces.append(lax.ppermute(turned[e], "col", pairs))

    r_flags = lax.dynamic_slice_in_dim(r_pattern, row * a_tiles, a_tiles, 0)
    flags = [r_flags.reshape(-1), s_pattern.reshape(-1)]
    sizes = (side, a_tiles, r_pattern.shape[1], s_pattern.shape[1])

    blocks, spots, targets = [], [], []
    for e in range(side):
        g = (gather_at - e) % side
        blocks.append(jnp.where(along, y * side + g, g * side + x))
    for t in range(side):
        target = (target_at + t) % side
        for e in range(side):
            g = (gather_at - e) % side
            k = jnp.where(along, target * side + g, g * side + target)
            spots.append((line ^ k) if flat else (line - k) % n_col)
        targets.append(jnp.where(along, target * side + x, y * side + target))
    table = jnp.concatenate([jnp.stack(blocks + spots + targets).astype(jnp.int32), *flags])

    block = max(a_part, math.gcd(a_rows, 8 * BLK))
    steps = a_rows // block
    chunks = 2 if steps % 2 == 0 else 1
    steps //= chunks
    coded = []
    for chunk in range(chunks):
        parts = []
        for e in range(1, side):
            codes = coded_product(
                sizes, table, r_pieces, s_pieces, e, block, chunk * steps * block, steps
            )
            if chunk:
                codes, *t_pieces[1:] = lax.optimization_barrier((codes, *t_pieces[1:]))
            parts.append(lax.ppermute(codes, axes, shifted(e, False)))
        coded.append(parts)
    order = [(col ^ o) if flat else (col - o) % n_col for o in range(n_col)]
    own, mirror = own_product(
        sizes, table, jnp.stack(order).astype(jnp.int32), r_pieces, s_pieces, t_pieces, block
    )
    own, mirror = in_vmem(own), in_vmem(mirror)
    out = None
    for chunk in range(chunks):
        out = join(own, mirror, coded[chunk], chunk * steps, out)
    return out


def plain_body(r_vals, s_vals, t_vals, r_pattern, s_pattern, t_pattern):
    row, col = lax.axis_index("row"), lax.axis_index("col")
    s_all = lax.all_gather(s_vals, "row", axis=0, tiled=True)
    r_all = lax.all_gather(r_vals, "col", axis=1, tiled=True)
    t_all = lax.all_to_all(t_vals, "col", split_axis=0, concat_axis=1, tiled=True)
    a_tiles, c_tiles = r_vals.shape[0] // BLK, s_vals.shape[1] // BLK

    def spread(flags):
        return jnp.repeat(jnp.repeat(flags.astype(jnp.bfloat16), BLK, axis=0), BLK, axis=1)

    r_flags = lax.dynamic_slice_in_dim(r_pattern, row * a_tiles, a_tiles, 0)
    s_flags = lax.dynamic_slice_in_dim(s_pattern, col * c_tiles, c_tiles, 1)
    t_flags = lax.dynamic_slice(t_pattern, (col * c_tiles, row * a_tiles), (c_tiles, a_tiles))
    paths = jnp.dot(
        r_all * spread(r_flags), s_all * spread(s_flags), preferred_element_type=jnp.float32
    )
    mirror = (t_all * spread(t_flags)).T
    return (paths * mirror.astype(jnp.float32)).astype(jnp.bfloat16)


def solution(mesh):
    placed = (P("row", "col"), P("row", "col"), P(None, ("row", "col")), P(), P(), P())
    n_row, n_col = mesh.shape["row"], mesh.shape["col"]
    fits = n_row == 2 * n_col and math.isqrt(n_col) ** 2 == n_col > 1
    return jax.shard_map(
        functools.partial(body, n_row, n_col) if fits else plain_body,
        mesh=mesh,
        in_specs=placed,
        out_specs=P("row", "col"),
        check_vma=False,
    )
```
